32 devices in a mesh: lat: 8 (over z, y), lev: 4 (over x, core).
Axes of the slice: x: 2, y: 2, z: 4, core: 2. Of those that a mesh axis runs over, the one named last changes fastest.
Arguments:
- grid: bfloat16 [3, 1536, 32, 2816], P(None, 'lat', 'lev'), may hold values from -6 to 6
- legendre: bfloat16 [384, 769, 1280], P(('lat', 'lev')), may hold values from -6 to 6
- gauss_weights: float32 [1280], replicated, may hold values from 0.00078125 to 0.003125
- band_counts: int32 [8], replicated, may hold values from 1 to 192, 1280 in all
- pair_m: int32 [384], replicated, may hold values from 0 to 383, each once
- vert_modes: float32 [32, 32], replicated, may hold values from -1 to 1
- mode_depth: float32 [32], replicated, may hold values from 0.5 to 50
- diffusion: float32 [32], replicated, may hold values from 1 to 100
- pressure_balance_matrix: float32 [32, 32], replicated, may hold values from -1 to 1
Outputs:
- next_grid_rows: bfloat16 [3, 1536, 32, 2816], P(None, 'lat', 'lev')
The draws below stay inside these ranges and needn't reach their ends.
Inputs may be any that keep to these rules, and one draw needn't show every extreme that they name: `band_counts`: latitudes in each band, in band order; the bands cover all 1280 latitudes and the fullest holds 192. `pair_m`: each of 0 to 383 once.
All inputs are finite; a program needn't handle non-finite values.
Results may differ from the reference program's by a relative error of at most 0.0072.
Values may be sent and summed in bfloat16 or wider, within the bound.
No kernel may reach another device: no remote copies, remote signals or barrier semaphores. Data moves between devices by JAX's collectives and lax.ppermute only.
A program may use at most 576 MiB of HBM per device.

```python
import math
import jax
import jax.numpy as jnp
import numpy as np
from jax import lax

M = 768
NLAT = 1280
NLON = 2816
LEVELS = 32
BAND_ROW_LIMIT = 192
SLOTS = 1536
PAIRS = 384
N_LAT = 8


def shard_levels(stream_key, shape, cuts, low, largest):
    def one(dim, blocks):
        steps = jax.random.uniform(jax.random.fold_in(jax.random.fold_in(stream_key, 6), dim), (blocks,), jnp.float32, low / len(cuts), largest / len(cuts))
        return jnp.repeat(jnp.exp(steps), shape[dim] // blocks).reshape((-1,) + (1,) * (len(shape) - dim - 1))

    gain = one(*cuts[0])
    for cut in cuts[1:]:
        gain = gain * one(*cut)
    return gain


def length_profile(number_of, total, most, skew):
    portions = [(1 << 20) // math.isqrt(grade ** skew) + 1 for grade in range(2, number_of + 1)]
    rest, given = total - most - (number_of - 1), [1] * (number_of - 1)
    while rest > 0:
        movable = [i for i in range(number_of - 1) if given[i] < most]
        mass, budget = sum([portions[i] for i in movable]), rest
        for i in movable:
            more = min(most - given[i], max(1, budget * portions[i] // mass), rest)
            given[i] = given[i] + more
            rest = rest - more
    return np.array([most] + given)


def uneven(stream_key, amount, total, reach, skew):
    if amount == 2:
        one = jax.random.randint(stream_key, (), max(1, total - reach), min(reach, total - 1) + 1)
        return jnp.stack([one, total - one])
    sizes = jnp.asarray(length_profile(amount, total, reach, skew), jnp.int32)
    twos = (amount - 1) // 2
    giver, taker = sizes[1:1 + 2 * twos:2], sizes[2:2 + 2 * twos:2]
    room = jnp.minimum(giver - 1, reach - taker)
    passed = jax.random.randint(jax.random.fold_in(stream_key, 1), (twos,), 0, 1 << 20) % (room + 1)
    sizes = sizes.at[1:1 + 2 * twos:2].set(giver - passed).at[2:2 + 2 * twos:2].set(taker + passed)
    return sizes[jax.random.permutation(jax.random.fold_in(stream_key, 2), amount)]


def noise(stream_key, extent, spread, reach, cuts=(), held_as=jnp.bfloat16):
    values = spread * jax.random.normal(stream_key, extent, jnp.float32)
    if cuts:
        values = values * shard_levels(stream_key, extent, cuts, -0.22, 0.18)
    return jnp.clip(values, -reach, reach).astype(held_as)


def setup_inputs(seed: int = 0) -> dict:
    streams_of = jax.random.split(jax.random.key(seed), 10)
    grid = noise(streams_of[0], (3, SLOTS, LEVELS, NLON), 1.0, 6.0, ((1, 8), (2, 4)))
    legendre = noise(streams_of[1], (PAIRS, M + 1, NLAT), 1.0, 6.0, ((0, 32),))
    gauss_weights = jnp.clip(jnp.exp(jax.random.uniform(streams_of[2], (NLAT,), jnp.float32, math.log(0.00078125), math.log(0.003125))), 0.00078125, 0.003125)
    band_counts = uneven(streams_of[3], N_LAT, NLAT, BAND_ROW_LIMIT, 1).astype(jnp.int32)
    pair_m = jax.random.permutation(streams_of[4], PAIRS).astype(jnp.int32)
    vert_modes = noise(streams_of[5], (LEVELS, LEVELS), LEVELS ** -0.5, 1.0, (), jnp.float32)
    mode_depth = jnp.clip(jnp.exp(jax.random.uniform(streams_of[6], (LEVELS,), jnp.float32, math.log(0.5), math.log(50.0))), 0.5, 50.0)
    diffusion = jnp.clip(jnp.exp(jax.random.uniform(streams_of[7], (LEVELS,), jnp.float32, math.log(1.0), math.log(100.0))), 1.0, 100.0)
    pressure_balance_matrix = noise(streams_of[8], (LEVELS, LEVELS), LEVELS ** -0.5, 1.0, (), jnp.float32)
    return {"grid": grid, "legendre": legendre, "gauss_weights": gauss_weights, "band_counts": band_counts, "pair_m": pair_m, "vert_modes": vert_modes, "mode_depth": mode_depth, "diffusion": diffusion, "pressure_balance_matrix": pressure_balance_matrix}


def dft_tables(pair_m, width, points):
    lower_wave = pair_m.astype(jnp.int32)
    upper_wave = (width - 1 - lower_wave).astype(jnp.int32)
    harmonic_order_index = jnp.stack([lower_wave, lower_wave, upper_wave, upper_wave], axis=1).reshape(-1)
    component = jnp.arange(2 * width, dtype=jnp.int32) % 2
    phase_index = (harmonic_order_index[:, None] * jnp.arange(points, dtype=jnp.int32)[None, :]) % points
    angles = phase_index.astype(jnp.float32) * (2.0 * math.pi / points)
    trig_values = jnp.where((component == 0)[:, None], jnp.cos(angles), -jnp.sin(angles))
    factor = jnp.where(harmonic_order_index == 0, 1.0, 2.0).astype(jnp.float32)
    forward_table = (trig_values / points).astype(jnp.bfloat16)
    inverse_table = (trig_values * factor[:, None]).astype(jnp.bfloat16)
    return forward_table, inverse_table


def latitude_maps(band_counts, lat_cap, lat_total):
    counts = band_counts.astype(jnp.int32)
    group_count = counts.shape[0]
    band_starts = (jnp.cumsum(counts) - counts).astype(jnp.int32)
    groups = jnp.arange(group_count, dtype=jnp.int32)
    latitude_list = jnp.arange(lat_total, dtype=jnp.int32)
    lat_band = jnp.sum((band_starts[None, :] <= latitude_list[:, None]).astype(jnp.int32), axis=1).astype(jnp.int32) - 1
    lat_begin = jnp.sum(jnp.where(groups[None, :] == lat_band[:, None], band_starts[None, :], 0), axis=1).astype(jnp.int32)
    slot_for_latitude = (lat_band * lat_cap + latitude_list - lat_begin).astype(jnp.int32)
    slot_ids = jnp.arange(group_count * lat_cap, dtype=jnp.int32)
    slot_band = slot_ids // lat_cap
    offsets = slot_ids % lat_cap
    member = groups[None, :] == slot_band[:, None]
    slot_begin = jnp.sum(jnp.where(member, band_starts[None, :], 0), axis=1).astype(jnp.int32)
    slot_size = jnp.sum(jnp.where(member, counts[None, :], 0), axis=1).astype(jnp.int32)
    valid_slot = offsets < slot_size
    lat_of_slot = jnp.where(valid_slot, slot_begin + offsets, 0).astype(jnp.int32)
    return slot_for_latitude, lat_of_slot, valid_slot


def helmholtz(harmonic_model_snapshot, ratio, vert_modes, mode_depth, diffusion, pressure_balance_matrix):
    rotation_harmonic_coeffs = harmonic_model_snapshot[..., 0, :, :]
    velocity_spread_coeffs_map = harmonic_model_snapshot[..., 1, :, :]
    thermal_harmonic_coeffs = harmonic_model_snapshot[..., 2, :, :]
    rotation_harmonic_coeffs = rotation_harmonic_coeffs / (1.0 + diffusion[:, None] * ratio * ratio)
    modes = jnp.einsum('ql,...lk->...qk', vert_modes, velocity_spread_coeffs_map, precision=lax.Precision.HIGHEST)
    modes = modes / (1.0 + mode_depth[:, None] * ratio)
    velocity_spread_coeffs_map = jnp.einsum('ql,...qk->...lk', vert_modes, modes, precision=lax.Precision.HIGHEST)
    thermal_harmonic_coeffs = thermal_harmonic_coeffs - jnp.einsum('ja,...ax->...jx', pressure_balance_matrix, velocity_spread_coeffs_map, precision=lax.Precision.HIGHEST)
    return jnp.stack([rotation_harmonic_coeffs, velocity_spread_coeffs_map, thermal_harmonic_coeffs], axis=-3)


def reference(grid, legendre, gauss_weights, band_counts, pair_m, vert_modes, mode_depth, diffusion, pressure_balance_matrix):
    slot_for_latitude, lat_of_slot, valid_slot = latitude_maps(band_counts, BAND_ROW_LIMIT, NLAT)
    forward_table, inverse_table = dft_tables(pair_m, M, NLON)
    slot_weights = jnp.where(valid_slot, gauss_weights[lat_of_slot], 0.0).astype(jnp.float32)

    def analyse(field_grid):
        flat_grid = field_grid.reshape(SLOTS * LEVELS, NLON)
        coeffs = jnp.dot(forward_table, flat_grid.T, preferred_element_type=jnp.float32)
        return (coeffs.reshape(2 * M, SLOTS, LEVELS) * slot_weights[None, :, None]).astype(jnp.bfloat16)

    fourier = lax.map(analyse, grid)
    ordered = jnp.take(fourier, slot_for_latitude, axis=2)
    ordered = ordered.reshape(3, PAIRS, 2, 2, NLAT, LEVELS).transpose(1, 2, 3, 0, 5, 4)
    ordered = ordered.reshape(PAIRS, 2, 2, 3 * LEVELS, NLAT)
    half_rows = M // 2 + 1

    def each_mode_couple(inputs):
        table, coeffs, wave = inputs
        table_full = table.astype(jnp.float32)
        table_head = table_full[:half_rows]
        table_tail = table_full[half_rows:]
        coeffs_full = coeffs.astype(jnp.float32)
        row_ids = jnp.arange(M + 1, dtype=jnp.int32)
        own_rows = row_ids < M - wave
        degree = jnp.where(own_rows, wave + row_ids, row_ids - 1)
        ratio = (degree * (degree + 1)).astype(jnp.float32) / float(M * (M - 1))
        head_spec = jnp.einsum('kj,rcj->rck', table_head, coeffs_full[0])
        tail_both = jnp.einsum('kj,wrcj->wrck', table_tail, coeffs_full)
        tail_own = own_rows[half_rows:]
        tail_spec = jnp.where(tail_own, tail_both[0], tail_both[1])
        harmonic_model_snapshot = jnp.concatenate([head_spec, tail_spec], axis=-1).reshape(2, 3, LEVELS, M + 1)
        updated = helmholtz(harmonic_model_snapshot, ratio, vert_modes, mode_depth, diffusion, pressure_balance_matrix).astype(jnp.bfloat16)
        updated = updated.reshape(2, 3 * LEVELS, M + 1).astype(jnp.float32)
        head_part = jnp.einsum('kj,rck->rcj', table_head, updated[..., :half_rows])
        masks = jnp.stack([tail_own, jnp.logical_not(tail_own)]).astype(jnp.float32)
        masked = updated[None, :, :, half_rows:] * masks[:, None, None, :]
        tail_parts = jnp.einsum('kj,wrck->wrcj', table_tail, masked)
        synthesis = jnp.stack([tail_parts[0] + head_part, tail_parts[1]])
        return synthesis.astype(jnp.bfloat16)

    gridpoint = lax.map(each_mode_couple, (legendre, ordered, pair_m.astype(jnp.int32)))
    banded = jnp.take(gridpoint, lat_of_slot, axis=4) * valid_slot.astype(jnp.bfloat16)
    banded = jnp.moveaxis(banded.reshape(2 * M, 3, LEVELS * SLOTS), 1, 0)

    def synthesise(field_coeffs):
        values = jnp.dot(field_coeffs.T, inverse_table, preferred_element_type=jnp.float32)
        return values.reshape(LEVELS, SLOTS, NLON).transpose(1, 0, 2).astype(jnp.bfloat16)

    return lax.map(synthesise, banded)
```

```python
import functools
import math

import jax
import jax.numpy as jnp
from jax import lax
from jax.experimental import pallas as pl
from jax.experimental.pallas import tpu as pltpu
from jax.sharding import PartitionSpec as P

LANES = 128
VMEM_LIMIT = 56 * 1024 * 1024


def swap_units(parts, unit):
    lane = lax.broadcasted_iota(jnp.int32, parts[0].shape, 1)
    step = 1
    parts = list(parts)
    while step < len(parts):
        shift = unit * step
        high = (lane & shift) != 0
        for i in range(len(parts)):
            if not i & step:
                a, b = parts[i], parts[i | step]
                parts[i] = jnp.where(high, pltpu.roll(b, shift, 1), a)
                parts[i | step] = jnp.where(high, b, pltpu.roll(a, LANES - shift, 1))
        step *= 2
    return parts


def row_tile(rows, most):
    tile = most
    while rows % tile:
        tile -= 16
    return tile


def table_kernel(coarse_cos, coarse_sin, fine_cos, fine_sin, table):
    cos_b, sin_b = fine_cos[...], fine_sin[...]
    for a in range(table.shape[1] // LANES):
        values = coarse_cos[:, a : a + 1] * cos_b - coarse_sin[:, a : a + 1] * sin_b
        table[:, a * LANES : (a + 1) * LANES] = values.astype(table.dtype)


def trig_table(pair_m, width, points, devices, groups, group):
    pair_dev = pair_m.shape[0] // devices
    padded = jnp.pad(
        pair_m.reshape(devices, pair_dev),
        ((0, 0), (0, groups * group - pair_dev)),
        constant_values=-1,
    ).reshape(-1)
    waves = jnp.stack([padded, padded, width - 1 - padded, width - 1 - padded], axis=1).reshape(-1)
    real = jnp.repeat(padded >= 0, 4)
    rows = waves.shape[0]
    sine = (jnp.arange(rows, dtype=jnp.int32) % 2 == 1)[:, None]
    blocks = points // LANES
    unit = 2.0 * math.pi / points
    fine = (waves[:, None] * jnp.arange(LANES, dtype=jnp.int32)[None, :]) % points
    fine = fine.astype(jnp.float32) * unit
    coarse = (waves[:, None] * (LANES * jnp.arange(LANES, dtype=jnp.int32)[None, :])) % points
    coarse = coarse.astype(jnp.float32) * unit
    keep = real[:, None].astype(jnp.float32)
    cos_a, sin_a = jnp.cos(coarse) * keep, jnp.sin(coarse) * keep
    tile = row_tile(rows, 256) if rows % 256 == 0 else LANES
    narrow = pl.BlockSpec((tile, LANES), lambda t: (t, 0))
    return pl.pallas_call(
        table_kernel,
        grid=(rows // tile,),
        in_specs=[narrow] * 4,
        out_specs=pl.BlockSpec((tile, points), lambda t: (t, 0)),
        out_shape=jax.ShapeDtypeStruct((rows, points), jnp.bfloat16),
        cost_estimate=pl.CostEstimate(
            flops=4 * rows * points, bytes_accessed=2 * rows * points, transcendentals=0
        ),
        name="trig_table",
    )(
        jnp.where(sine, -sin_a, cos_a),
        jnp.where(sine, cos_a, sin_a),
        jnp.cos(fine),
        jnp.sin(fine),
    )


def forward_kernel(levels, unit, grid_ref, table_ref, weight_ref, out_ref, scratch):
    cols = table_ref.shape[0]
    rows = grid_ref.shape[1]
    cap = rows // levels
    tile = row_tile(cap, 32)
    for r in range(cap // tile):
        lo = r * tile * levels
        values = lax.dot_general(
            grid_ref[0, lo : lo + tile * levels, :],
            table_ref[...],
            (((1,), (1,)), ((), ())),
            preferred_element_type=jnp.float32,
        )
        for n in range(cols // LANES):
            scratch[n, lo : lo + tile * levels, :] = values[:, n * LANES : (n + 1) * LANES]
        weight = weight_ref[r * tile : (r + 1) * tile, :]
        for n in range(cols // LANES):
            parts = [
                scratch[n, pl.ds(lo + l, tile, stride=levels), :] * weight for l in range(levels)
            ]
            for a, part in enumerate(swap_units(parts, unit)):
                out_ref[n * levels + a, r * tile : (r + 1) * tile, :] = part.astype(jnp.bfloat16)


def forward(field, grid, table, weights, levels, unit):
    _, rows, points = grid.shape
    columns = table.shape[0]
    cap = rows // levels
    step = 2 * LANES if columns % (2 * LANES) == 0 else LANES
    pieces = step // unit
    return pl.pallas_call(
        functools.partial(forward_kernel, levels, unit),
        grid=(columns // step,),
        in_specs=[
            pl.BlockSpec((1, rows, points), lambda t: (field, 0, 0)),
            pl.BlockSpec((step, points), lambda t: (t, 0)),
            pl.BlockSpec((cap, LANES), lambda t: (0, 0)),
        ],
        out_specs=pl.BlockSpec((pieces, cap, LANES), lambda t: (t, 0, 0)),
        out_shape=jax.ShapeDtypeStruct((columns // unit, cap, LANES), jnp.bfloat16),
        scratch_shapes=[pltpu.VMEM((step // LANES, rows, LANES), jnp.float32)],
        compiler_params=pltpu.CompilerParams(vmem_limit_bytes=VMEM_LIMIT),
        cost_estimate=pl.CostEstimate(
            flops=2 * rows * points * columns,
            bytes_accessed=2 * (rows * points + columns * points + rows * columns),
            transcendentals=0,
        ),
        name="forward_dft",
    )(grid, table, weights)


def inverse_kernel(levels, unit, count_ref, spec_ref, table_ref, *rest):
    out_ref, scratch = rest[-2:]
    pieces, tile, _ = spec_ref.shape
    for n in range(pieces // levels):
        parts = [spec_ref[n * levels + a].astype(jnp.float32) for a in range(levels)]
        for l, part in enumerate(swap_units(parts, unit)):
            scratch[n, pl.ds(l, tile, stride=levels), :] = part
    rows = tile * levels
    row = pl.program_id(0) * rows + lax.broadcasted_iota(jnp.int32, (rows, LANES), 0)
    valid = row < count_ref[0] * levels
    columns = jnp.concatenate(
        [
            jnp.where(valid, scratch[n], 0.0).astype(jnp.bfloat16)
            for n in range(pieces // levels)
        ],
        axis=1,
    )
    out_ref[0] = jnp.dot(columns, table_ref[...], preferred_element_type=jnp.float32).astype(
        out_ref.dtype
    )


def inverse(field, fields, spec, table, count, partial, levels, unit):
    pieces, cap, _ = spec.shape
    columns, points = table.shape
    rows = cap * levels
    tile = row_tile(cap, 32)
    in_specs = [
        pl.BlockSpec((pieces, tile, LANES), lambda t, c: (0, t, 0)),
        pl.BlockSpec((columns, points), lambda t, c: (0, 0)),
    ]
    operands = [spec, table]
    if partial is not None:
        in_specs.append(pl.BlockSpec(memory_space=pl.ANY))
        operands.append(partial)
    return pl.pallas_call(
        functools.partial(inverse_kernel, levels, unit),
        grid_spec=pltpu.PrefetchScalarGridSpec(
            num_scalar_prefetch=1,
            grid=(cap // tile,),
            in_specs=in_specs,
            out_specs=pl.BlockSpec((1, tile * levels, points), lambda t, c: (field, t, 0)),
            scratch_shapes=[pltpu.VMEM((pieces // levels, tile * levels, LANES), jnp.float32)],
        ),
        out_shape=jax.ShapeDtypeStruct((fields, rows, points), jnp.bfloat16),
        input_output_aliases={} if partial is None else {3: 0},
        compiler_params=pltpu.CompilerParams(vmem_limit_bytes=VMEM_LIMIT),
        cost_estimate=pl.CostEstimate(
            flops=2 * rows * points * columns,
            bytes_accessed=2 * (rows * points + columns * points + rows * columns),
            transcendentals=0,
        ),
        name="inverse_dft",
    )(count, *operands)


def legendre_kernel(
    kind, pair_dev, lat_groups, group, counts_ref, waves_ref, recv_ref, leg_ref, *rest
):
    lane_ref = rest[0]
    if kind == "vorticity":
        out_ref, gathered, made = rest[1:]
    elif kind == "divergence":
        to_modes, from_modes, out_ref, div_out, gathered, made = rest[1:]
    else:
        balance, div_in, out_ref, gathered, made = rest[1:]
    row_count, lat_total = leg_ref.shape[1:]
    width = row_count - 1
    cap = recv_ref.shape[2]
    member = pl.program_id(1)
    pair = pl.program_id(0) * group + member

    @pl.when(member == 0)
    def _():
        start = 0
        for g in range(lat_groups):
            parts = [recv_ref[g * group + h, 0].astype(jnp.float32) for h in range(group)]
            for b, part in enumerate(swap_units(parts, 4)):
                gathered[b, pl.ds(start, cap), :] = part
            start = start + counts_ref[g]

    @pl.when(pair < pair_dev)
    def _():
        wave = waves_ref[pair]
        coeffs = gathered[member, :lat_total, :].astype(jnp.bfloat16)
        main = leg_ref[0, :width, :]
        last = jnp.broadcast_to(leg_ref[0, width:, :], (16, lat_total))
        spectral = jnp.concatenate(
            [
                jnp.dot(main, coeffs, preferred_element_type=jnp.float32),
                jnp.dot(last, coeffs, preferred_element_type=jnp.float32),
            ],
            axis=0,
        )
        shape = spectral.shape
        row = lax.broadcasted_iota(jnp.int32, shape, 0)
        lane = lax.broadcasted_iota(jnp.int32, shape, 1)
        own = row < width - wave
        upper = (lane & 2) != 0
        keep = jnp.logical_and(jnp.logical_xor(own, upper), row < row_count)
        degree = jnp.where(own, row + wave, row - 1)
        ratio = (degree * (degree + 1)).astype(jnp.float32) / float(width * (width - 1))
        spectral = jnp.where(keep, spectral, 0.0)
        exact = functools.partial(
            jnp.dot, precision=lax.Precision.HIGHEST, preferred_element_type=jnp.float32
        )
        if kind == "vorticity":
            new = spectral / (1.0 + lane_ref[...] * ratio * ratio)
        elif kind == "divergence":
            modes = exact(spectral, to_modes[...])
            modes = modes / (1.0 + lane_ref[...] * ratio)
            new = exact(modes, from_modes[...])
            div_out[0] = new
        else:
            new = spectral - exact(div_in[0], balance[...])
        zonal = jnp.logical_and(wave == 0, jnp.logical_not(upper))
        new = new * jnp.where(zonal, 1.0, 2.0)
        tail = jnp.concatenate(
            [new[width:], jnp.zeros((LANES - 16, LANES), jnp.float32)], axis=0
        )
        turned = jnp.dot(
            new[:width].T.astype(jnp.bfloat16), main, preferred_element_type=jnp.float32
        )
        turned += jnp.dot(
            tail.T.astype(jnp.bfloat16),
            jnp.broadcast_to(leg_ref[0, width:, :], (LANES, lat_total)),
            preferred_element_type=jnp.float32,
        )
        made[member, :lat_total, :] = turned.T
        made[member, lat_total:, :] = jnp.zeros((cap, LANES), jnp.float32)

    @pl.when(pair >= pair_dev)
    def _():
        made[member] = jnp.zeros(made.shape[1:], jnp.float32)

    @pl.when(member == group - 1)
    def _():
        start = 0
        for g in range(lat_groups):
            parts = [made[b, pl.ds(start, cap), :] for b in range(group)]
            for h, part in enumerate(swap_units(parts, 4)):
                out_ref[g * group + h, 0] = part.astype(jnp.bfloat16)
            start = start + counts_ref[g]


def legendre_step(kind, received, legendre, counts, waves, lane_values, extra, group):
    devices, groups, cap, _ = received.shape
    pair_dev, row_count, lat_total = legendre.shape
    lat_groups = devices // group

    def at_pair(i, b, *_):
        return (jnp.minimum(i * group + b, pair_dev - 1), 0, 0)

    def whole(i, b, *_):
        return (0, 0)

    blocks = pl.BlockSpec((devices, 1, cap, LANES), lambda i, b, *_: (0, i, 0, 0))
    square = pl.BlockSpec((LANES, LANES), whole)
    div_block = pl.BlockSpec((1, row_count + 15, LANES), at_pair)
    in_specs = [
        blocks,
        pl.BlockSpec((1, row_count, lat_total), at_pair),
        pl.BlockSpec((1, LANES), whole),
    ]
    out_specs = [blocks]
    out_shape = [jax.ShapeDtypeStruct(received.shape, jnp.bfloat16)]
    if kind == "divergence":
        in_specs += [square, square]
        out_specs.append(div_block)
        out_shape.append(jax.ShapeDtypeStruct((pair_dev, row_count + 15, LANES), jnp.float32))
    elif kind == "temperature":
        in_specs += [square, div_block]
    held = pltpu.VMEM((group, lat_total + cap, LANES), jnp.float32)
    result = pl.pallas_call(
        functools.partial(legendre_kernel, kind, pair_dev, lat_groups, group),
        grid_spec=pltpu.PrefetchScalarGridSpec(
            num_scalar_prefetch=2,
            grid=(groups, group),
            in_specs=in_specs,
            out_specs=out_specs,
            scratch_shapes=[held, held],
        ),
        out_shape=out_shape,
        compiler_params=pltpu.CompilerParams(vmem_limit_bytes=VMEM_LIMIT),
        cost_estimate=pl.CostEstimate(
            flops=8 * pair_dev * row_count * lat_total * LANES,
            bytes_accessed=2 * (legendre.size + 2 * received.size),
            transcendentals=0,
        ),
        name="legendre_" + kind,
    )(counts, waves, received, legendre, lane_values, *extra)
    return result


def shards(
    grid,
    legendre,
    gauss_weights,
    band_counts,
    pair_m,
    vert_modes,
    mode_depth,
    diffusion,
    pressure_balance_matrix,
):
    lat_groups = lax.axis_size("lat")
    group = lax.axis_size("lev")
    devices = lat_groups * group
    fields, cap, levels, points = grid.shape
    pair_dev, row_count, _ = legendre.shape
    width = row_count - 1
    unit = 4 * group
    groups = -(-pair_dev // group)
    band = lax.axis_index("lat")
    owner = band * group + lax.axis_index("lev")

    table = trig_table(pair_m, width, points, devices, groups, group)

    bands = jnp.arange(lat_groups, dtype=jnp.int32)
    start = jnp.sum(jnp.where(bands < band, band_counts, 0))
    count = jnp.sum(jnp.where(bands == band, band_counts, 0))
    weights = lax.dynamic_slice(jnp.pad(gauss_weights, (0, cap)), (start,), (cap,))
    weights = jnp.where(jnp.arange(cap, dtype=jnp.int32) < count, weights / points, 0.0)
    weights = jnp.broadcast_to(weights[:, None], (cap, LANES))

    waves = lax.dynamic_slice(pair_m, (owner * pair_dev,), (pair_dev,))
    def by_lane(per_level):
        ordered = per_level.reshape((group, levels) + per_level.shape[1:])
        return jnp.swapaxes(ordered, 0, 1).reshape(per_level.shape)

    def lane_matrix(matrix):
        ordered = by_lane(by_lane(matrix).T).T
        spread = ordered[:, None, :, None] * jnp.eye(4, dtype=jnp.float32)[None, :, None, :]
        return spread.reshape(LANES, LANES)

    def lane_row(per_level):
        return jnp.repeat(by_lane(per_level), 4)[None, :]

    rows = grid.reshape(fields, cap * levels, points)
    sent = [forward(f, rows, table, weights, levels, unit) for f in range(fields)]

    def exchange(blocks):
        return lax.all_to_all(
            blocks.reshape(devices, groups, cap, LANES),
            ("lat", "lev"),
            split_axis=0,
            concat_axis=0,
            tiled=True,
        )

    received = [exchange(x) for x in sent]
    step = functools.partial(
        legendre_step, legendre=legendre, counts=band_counts, waves=waves, group=group
    )
    (vorticity,) = step(
        "vorticity", received[0], lane_values=lane_row(diffusion), extra=()
    )
    divergence, new_divergence = step(
        "divergence",
        received[1],
        lane_values=lane_row(mode_depth),
        extra=(lane_matrix(vert_modes.T), lane_matrix(vert_modes)),
    )
    (temperature,) = step(
        "temperature",
        received[2],
        lane_values=lane_row(diffusion),
        extra=(lane_matrix(pressure_balance_matrix.T), new_divergence),
    )
    out = None
    for f, made in enumerate((vorticity, divergence, temperature)):
        back = exchange(made).reshape(devices * groups, cap, LANES)
        out = inverse(f, fields, back, table, count[None], out, levels, unit)
    return out.reshape(fields, cap, levels, points)


def solution(mesh):
    placed = (
        P(None, "lat", "lev", None),
        P(("lat", "lev"), None, None),
        P(),
        P(),
        P(),
        P(),
        P(),
        P(),
        P(),
    )
    return jax.shard_map(
        shards, mesh=mesh, in_specs=placed, out_specs=P(None, "lat", "lev", None), check_vma=False
    )
```

```python
import functools
import math

import jax
import jax.numpy as jnp
from jax import lax
from jax.experimental import pallas as pl
from jax.experimental.pallas import tpu as pltpu
from jax.sharding import PartitionSpec as P

LANES = 128
VMEM_LIMIT = 56 * 1024 * 1024


def swap_units(parts, unit):
    lane = lax.broadcasted_iota(jnp.int32, parts[0].shape, 1)
    step = 1
    parts = list(parts)
    while step < len(parts):
        shift = unit * step
        high = (lane & shift) != 0
        for i in range(len(parts)):
            if not i & step:
                a, b = parts[i], parts[i | step]
                parts[i] = jnp.where(high, pltpu.roll(b, shift, 1), a)
                parts[i | step] = jnp.where(high, b, pltpu.roll(a, LANES - shift, 1))
        step *= 2
    return parts


def row_tile(rows, most):
    tile = most
    while rows % tile:
        tile -= 16
    return tile


def unit_circle(wave, points):
    lane = lax.broadcasted_iota(jnp.int32, (wave.shape[0], LANES), 1).astype(jnp.float32)
    product = wave.astype(jnp.float32) * lane
    rest = product - points * jnp.floor(product * (1.0 / points))
    quarter = jnp.floor(rest * (4.0 / points) + 0.5)
    x = (rest - quarter * (points / 4.0)) * (2.0 * math.pi / points)
    y = x * x
    sine = x * (1 + y * (-1 / 6 + y * (1 / 120 + y * (-1 / 5040 + y * (1 / 362880)))))
    cosine = 1 + y * (-1 / 2 + y * (1 / 24 + y * (-1 / 720 + y * (1 / 40320))))
    odd = jnp.logical_or(quarter == 1, quarter == 3)
    cos_low = jnp.logical_or(quarter == 1, quarter == 2)
    sin_low = jnp.logical_or(quarter == 2, quarter == 3)
    cos_all = jnp.where(odd, sine, cosine)
    sin_all = jnp.where(odd, cosine, sine)
    return jnp.where(cos_low, -cos_all, cos_all), jnp.where(sin_low, -sin_all, sin_all)


def table_kernel(waves, table):
    count, points = waves.shape[0], table.shape[1]
    part = min(64, count)
    for lo in range(0, count, part):
        wave = waves[lo : lo + part, :]
        cos, sin = unit_circle(wave, points)
        cos, sin = jnp.where(wave < 0, 0.0, cos), jnp.where(wave < 0, 0.0, sin)
        half = LANES // 2
        cos_half, sin_half = cos[:, half : half + 1], sin[:, half : half + 1]
        cos_turn = jnp.broadcast_to(cos_half * cos_half - sin_half * sin_half, cos.shape)
        sin_turn = jnp.broadcast_to(2.0 * sin_half * cos_half, cos.shape)
        for a in range(points // LANES):
            both = jnp.stack(
                [cos.reshape(part // 8, 8, LANES), -sin.reshape(part // 8, 8, LANES)], axis=1
            )
            table[2 * lo : 2 * (lo + part), a * LANES : (a + 1) * LANES] = both.reshape(
                2 * part, LANES
            ).astype(table.dtype)
            cos, sin = cos * cos_turn - sin * sin_turn, sin * cos_turn + cos * sin_turn


def trig_table(pair_m, width, points, devices, groups, group):
    pair_dev = pair_m.shape[0] // devices
    lower = pair_m.reshape(devices, pair_dev)
    waves = jnp.stack([lower, width - 1 - lower], axis=2)
    waves = jnp.pad(
        waves, ((0, 0), (0, groups * group - pair_dev), (0, 0)), constant_values=-1
    )
    waves = jnp.swapaxes(waves.reshape(devices, groups, 2 * group), 0, 1).reshape(-1, 1)
    count = waves.shape[0]
    tile = LANES if count % LANES == 0 else count
    return pl.pallas_call(
        table_kernel,
        grid=(count // tile,),
        in_specs=[pl.BlockSpec((tile, 1), lambda t: (t, 0))],
        out_specs=pl.BlockSpec((2 * tile, points), lambda t: (t, 0)),
        out_shape=jax.ShapeDtypeStruct((2 * count, points), jnp.bfloat16),
        cost_estimate=pl.CostEstimate(
            flops=8 * count * points, bytes_accessed=4 * count * points, transcendentals=0
        ),
        name="trig_table",
    )(waves)


def forward_kernel(levels, unit, grid_ref, table_ref, weight_ref, out_ref, scratch):
    cols = table_ref.shape[0]
    rows = grid_ref.shape[1]
    cap = rows // levels
    tall = cap // 2 if cap % 32 == 0 else cap
    tile = row_tile(tall, 32)
    for r in range(0, cap, tall):
        values = lax.dot_general(
            grid_ref[0, r * levels : (r + tall) * levels, :],
            table_ref[...],
            (((1,), (1,)), ((), ())),
            preferred_element_type=jnp.float32,
        )
        for n in range(cols // LANES):
            scratch[n, r * levels : (r + tall) * levels, :] = values[
                :, n * LANES : (n + 1) * LANES
            ]
        for s in range(r, r + tall, tile):
            weight = weight_ref[s : s + tile, :]
            for n in range(cols // LANES):
                parts = [
                    scratch[n, pl.ds(s * levels + l, tile, stride=levels), :] * weight
                    for l in range(levels)
                ]
                for a, part in enumerate(swap_units(parts, unit)):
                    out_ref[n * levels + a, 0, s : s + tile, :] = part.astype(jnp.bfloat16)


def forward(field, first, count, grid, table, weights, levels, unit, devices):
    _, rows, points = grid.shape
    cap = rows // levels
    wide = 2 * levels if devices % (2 * levels) == 0 else levels
    steps = devices // wide
    columns = count * devices * unit
    return pl.pallas_call(
        functools.partial(forward_kernel, levels, unit),
        grid=(count, steps),
        in_specs=[
            pl.BlockSpec((1, rows, points), lambda i, t: (field, 0, 0)),
            pl.BlockSpec((wide * unit, points), lambda i, t: ((first + i) * steps + t, 0)),
            pl.BlockSpec((cap, LANES), lambda i, t: (0, 0)),
        ],
        out_specs=pl.BlockSpec((wide, 1, cap, LANES), lambda i, t: (t, i, 0, 0)),
        out_shape=jax.ShapeDtypeStruct((devices, count, cap, LANES), jnp.bfloat16),
        scratch_shapes=[pltpu.VMEM((wide * unit // LANES, rows, LANES), jnp.float32)],
        compiler_params=pltpu.CompilerParams(vmem_limit_bytes=VMEM_LIMIT),
        cost_estimate=pl.CostEstimate(
            flops=2 * rows * points * columns,
            bytes_accessed=2 * (rows * points + columns * points + rows * columns),
            transcendentals=0,
        ),
        name="forward_dft",
    )(grid, table, weights)


def inverse_kernel(levels, unit, first_row, count_ref, spec_ref, table_ref, *rest):
    out_ref, turned, columns = rest[-3:]
    devices, groups, cap, _ = spec_ref.shape
    tile = row_tile(cap, 32)
    rows = tile * levels
    blocks = [(i, d) for i in range(groups) for d in range(0, devices, levels)]

    @pl.when(pl.program_id(0) == 0)
    def _():
        @pl.loop(0, cap // tile)
        def _(r):
            at = pl.ds(pl.multiple_of(r * tile, tile), tile)
            for n, (i, d) in enumerate(blocks):
                parts = [spec_ref[d + a, i, at, :].astype(jnp.float32) for a in range(levels)]
                for l, part in enumerate(swap_units(parts, unit)):
                    turned[n, pl.ds(l, tile, stride=levels), :] = part
            row = r * rows + lax.broadcasted_iota(jnp.int32, (rows, LANES), 0)
            valid = row < (count_ref[0] - first_row) * levels
            lines = pl.ds(pl.multiple_of(r * rows, rows), rows)
            for n in range(len(blocks)):
                columns[lines, n * LANES : (n + 1) * LANES] = jnp.where(
                    valid, turned[n], 0.0
                ).astype(jnp.bfloat16)

    out_ref[0] = jnp.dot(
        columns[...], table_ref[...], preferred_element_type=jnp.float32
    ).astype(out_ref.dtype)


def inverse(field, first_row, spec, table, count, partial, shape, levels, unit):
    devices, groups, cap, _ = spec.shape
    columns, points = table.shape
    rows = cap * levels
    tile = row_tile(cap, 32)
    wide = 2 * LANES if points % (2 * LANES) == 0 else LANES
    in_specs = [
        pl.BlockSpec((devices, groups, cap, LANES), lambda t, c: (0, 0, 0, 0)),
        pl.BlockSpec((columns, wide), lambda t, c: (0, t)),
    ]
    operands = [spec, table]
    if partial is not None:
        in_specs.append(pl.BlockSpec(memory_space=pl.ANY))
        operands.append(partial)
    return pl.pallas_call(
        functools.partial(inverse_kernel, levels, unit, first_row),
        grid_spec=pltpu.PrefetchScalarGridSpec(
            num_scalar_prefetch=1,
            grid=(points // wide,),
            in_specs=in_specs,
            out_specs=pl.BlockSpec((1, rows, wide), lambda t, c: (field, first_row // cap, t)),
            scratch_shapes=[
                pltpu.VMEM((columns // LANES, tile * levels, LANES), jnp.float32),
                pltpu.VMEM((rows, columns), jnp.bfloat16),
            ],
        ),
        out_shape=jax.ShapeDtypeStruct(shape, jnp.bfloat16),
        input_output_aliases={} if partial is None else {3: 0},
        compiler_params=pltpu.CompilerParams(vmem_limit_bytes=VMEM_LIMIT),
        cost_estimate=pl.CostEstimate(
            flops=2 * rows * points * columns,
            bytes_accessed=2 * (rows * points + columns * points + rows * columns),
            transcendentals=0,
        ),
        name="inverse_dft",
    )(count, *operands)


def legendre_kernel(
    kind, first, pair_dev, lat_groups, group, outs, counts_ref, waves_ref, recv_ref, leg_ref, *rest
):
    lane_ref = rest[0]
    gathered, made = rest[-2:]
    if kind == "divergence":
        to_modes, from_modes = rest[1:3]
        div_out = rest[-3]
        out_refs = rest[-3 - outs : -3]
    else:
        out_refs = rest[-2 - outs : -2]
    if kind == "temperature":
        balance, div_in = rest[1:3]
    row_count, lat_total = leg_ref.shape[1:]
    width = row_count - 1
    cap = recv_ref.shape[2]
    member = pl.program_id(1)
    pair = (first + pl.program_id(0)) * group + member

    @pl.when(member == 0)
    def _():
        start = 0
        for g in range(lat_groups):
            parts = [recv_ref[g * group + h, 0].astype(jnp.float32) for h in range(group)]
            for b, part in enumerate(swap_units(parts, 2)):
                gathered[b, pl.ds(start, cap), :] = part
            start = start + counts_ref[g]

    @pl.when(pair < pair_dev)
    def _():
        wave = waves_ref[pair]
        coeffs = gathered[member, :lat_total, :].astype(jnp.bfloat16)
        main = leg_ref[0, :width, :]
        last = jnp.broadcast_to(leg_ref[0, width:, :], (16, lat_total))
        spectral = jnp.concatenate(
            [
                jnp.dot(main, coeffs, preferred_element_type=jnp.float32),
                jnp.dot(last, coeffs, preferred_element_type=jnp.float32),
            ],
            axis=0,
        )
        shape = spectral.shape
        row = lax.broadcasted_iota(jnp.int32, shape, 0)
        lane = lax.broadcasted_iota(jnp.int32, shape, 1)
        own = row < width - wave
        upper = (lane & 1) != 0
        keep = jnp.logical_and(jnp.logical_xor(own, upper), row < row_count)
        degree = jnp.where(own, row + wave, row - 1)
        ratio = (degree * (degree + 1)).astype(jnp.float32) / float(width * (width - 1))
        spectral = jnp.where(keep, spectral, 0.0)
        exact = functools.partial(
            jnp.dot, precision=lax.Precision.HIGHEST, preferred_element_type=jnp.float32
        )
        if kind == "vorticity":
            new = spectral / (1.0 + lane_ref[...] * ratio * ratio)
        elif kind == "divergence":
            modes = exact(spectral, to_modes[...])
            modes = modes / (1.0 + lane_ref[...] * ratio)
            new = exact(modes, from_modes[...])
            div_out[0] = new
        else:
            new = spectral - exact(div_in[0], balance[...])
        zonal = jnp.logical_and(wave == 0, jnp.logical_not(upper))
        new = new * jnp.where(zonal, 1.0, 2.0)
        tail = jnp.concatenate(
            [new[width:], jnp.zeros((LANES - 16, LANES), jnp.float32)], axis=0
        )
        turned = jnp.dot(
            new[:width].T.astype(jnp.bfloat16), main, preferred_element_type=jnp.float32
        )
        turned += jnp.dot(
            tail.T.astype(jnp.bfloat16),
            jnp.broadcast_to(leg_ref[0, width:, :], (LANES, lat_total)),
            preferred_element_type=jnp.float32,
        )
        made[member, :lat_total, :] = turned.T
        made[member, lat_total:, :] = jnp.zeros((cap, LANES), jnp.float32)

    @pl.when(pair >= pair_dev)
    def _():
        made[member] = jnp.zeros(made.shape[1:], jnp.float32)

    @pl.when(member == group - 1)
    def _():
        start = 0
        for g in range(lat_groups):
            parts = [made[b, pl.ds(start, cap), :] for b in range(group)]
            for h, part in enumerate(swap_units(parts, 2)):
                row = 0
                for out_ref in out_refs:
                    size = out_ref.shape[2]
                    out_ref[g * group + h, 0] = part[row : row + size].astype(jnp.bfloat16)
                    row += size
            start = start + counts_ref[g]


def legendre_step(
    kind, first, groups, splits, received, legendre, counts, waves, lane_values, extra, group, partial
):
    devices, some, cap, _ = received.shape
    pair_dev, row_count, lat_total = legendre.shape
    lat_groups = devices // group

    def at_pair(i, b, *_):
        return (jnp.minimum((first + i) * group + b, pair_dev - 1), 0, 0)

    def whole(i, b, *_):
        return (0, 0)

    square = pl.BlockSpec((LANES, LANES), whole)
    div_block = pl.BlockSpec((1, row_count + 15, LANES), at_pair)
    in_specs = [
        pl.BlockSpec((devices, 1, cap, LANES), lambda i, b, *_: (0, i, 0, 0)),
        pl.BlockSpec((1, row_count, lat_total), at_pair),
        pl.BlockSpec((1, LANES), whole),
    ]
    out_specs = [
        pl.BlockSpec((devices, 1, size, LANES), lambda i, b, *_: (0, first + i, 0, 0))
        for size in splits
    ]
    out_shape = [
        jax.ShapeDtypeStruct((devices, groups, size, LANES), jnp.bfloat16) for size in splits
    ]
    if kind == "divergence":
        in_specs += [square, square]
        out_specs.append(div_block)
        out_shape.append(jax.ShapeDtypeStruct((pair_dev, row_count + 15, LANES), jnp.float32))
    elif kind == "temperature":
        in_specs += [square, div_block]
    operands = [counts, waves, received, legendre, lane_values, *extra]
    aliases = {}
    if partial is not None:
        aliases = {len(operands): 0}
        in_specs.append(pl.BlockSpec(memory_space=pl.ANY))
        operands.append(partial)
    held = pltpu.VMEM((group, lat_total + cap, LANES), jnp.float32)
    return pl.pallas_call(
        functools.partial(legendre_kernel, kind, first, pair_dev, lat_groups, group, len(splits)),
        grid_spec=pltpu.PrefetchScalarGridSpec(
            num_scalar_prefetch=2,
            grid=(some, group),
            in_specs=in_specs,
            out_specs=out_specs,
            scratch_shapes=[held, held],
        ),
        out_shape=out_shape,
        input_output_aliases=aliases,
        compiler_params=pltpu.CompilerParams(vmem_limit_bytes=VMEM_LIMIT),
        cost_estimate=pl.CostEstimate(
            flops=8 * some * group * row_count * lat_total * LANES,
            bytes_accessed=2 * (some * group * row_count * lat_total + 2 * received.size),
            transcendentals=0,
        ),
        name="legendre_" + kind,
    )(*operands)


def shards(
    grid,
    legendre,
    gauss_weights,
    band_counts,
    pair_m,
    vert_modes,
    mode_depth,
    diffusion,
    pressure_balance_matrix,
):
    lat_groups = lax.axis_size("lat")
    group = lax.axis_size("lev")
    devices = lat_groups * group
    fields, cap, levels, points = grid.shape
    pair_dev, row_count, _ = legendre.shape
    width = row_count - 1
    unit = 4 * group
    groups = -(-pair_dev // group)
    band = lax.axis_index("lat")
    owner = band * group + lax.axis_index("lev")

    table = trig_table(pair_m, width, points, devices, groups, group)

    bands = jnp.arange(lat_groups, dtype=jnp.int32)
    start = jnp.sum(jnp.where(bands < band, band_counts, 0))
    count = jnp.sum(jnp.where(bands == band, band_counts, 0))
    weights = lax.dynamic_slice(jnp.pad(gauss_weights, (0, cap)), (start,), (cap,))
    weights = jnp.where(jnp.arange(cap, dtype=jnp.int32) < count, weights / points, 0.0)
    weights = jnp.broadcast_to(weights[:, None], (cap, LANES))

    waves = lax.dynamic_slice(pair_m, (owner * pair_dev,), (pair_dev,))

    def lane_row(per_level):
        ordered = per_level.reshape(group, levels).T[:, None, :, None]
        return jnp.broadcast_to(ordered, (levels, 2, group, 2)).reshape(1, LANES)

    def lane_matrix(matrix):
        ordered = matrix.reshape(group, levels, group, levels).transpose(1, 0, 3, 2)
        two = jnp.eye(2, dtype=jnp.float32)
        spread = jnp.einsum("ahbk,pq,vw->aphvbqkw", ordered, two, two, precision="highest")
        return spread.reshape(LANES, LANES)

    rows = grid.reshape(fields, cap * levels, points)

    def exchange(blocks):
        return lax.all_to_all(
            blocks, ("lat", "lev"), split_axis=0, concat_axis=0, tiled=True
        )

    plan = [(0, 0, 1), (0, 1, groups - 1)] if groups > 1 else [(0, 0, groups)]
    plan += [(f, 0, groups) for f in range(1, fields)]
    received = []
    for field, first, some in plan:
        sent = forward(field, first, some, rows, table, weights, levels, unit, devices)
        weights, _ = lax.optimization_barrier((weights, sent))
        received.append((first, exchange(sent)))

    step = functools.partial(
        legendre_step, groups=groups, legendre=legendre, counts=band_counts, waves=waves, group=group
    )
    late = max(16, cap // 3 // 16 * 16) if cap > 16 else 0
    pieces = (cap - late, late) if late and (cap - late) % late == 0 else (cap,)
    vorticity = None
    for first, blocks in received[:-2]:
        (vorticity,) = step(
            "vorticity",
            first,
            splits=(cap,),
            received=blocks,
            lane_values=lane_row(diffusion),
            extra=(),
            partial=vorticity,
        )
    divergence, new_divergence = step(
        "divergence",
        0,
        splits=(cap,),
        received=received[-2][1],
        lane_values=lane_row(mode_depth),
        extra=(lane_matrix(vert_modes.T), lane_matrix(vert_modes)),
        partial=None,
    )
    temperature = step(
        "temperature",
        0,
        splits=pieces,
        received=received[-1][1],
        lane_values=lane_row(diffusion),
        extra=(lane_matrix(pressure_balance_matrix.T), new_divergence),
        partial=None,
    )
    out = None
    back = [(0, 0, vorticity), (1, 0, divergence)]
    for n, made in enumerate(temperature):
        back.append((2, sum(pieces[:n]), made))
    for field, first_row, made in back:
        out = inverse(
            field,
            first_row,
            exchange(made),
            table,
            count[None],
            out,
            (fields, cap * levels, points),
            levels,
            unit,
        )
    return out.reshape(fields, cap, levels, points)


def solution(mesh):
    placed = (
        P(None, "lat", "lev", None),
        P(("lat", "lev"), None, None),
        P(),
        P(),
        P(),
        P(),
        P(),
        P(),
        P(),
    )
    return jax.shard_map(
        shards, mesh=mesh, in_specs=placed, out_specs=P(None, "lat", "lev", None), check_vma=False
    )
```

```python
import functools
import math

import jax
import jax.numpy as jnp
from jax import lax
from jax.experimental import pallas as pl
from jax.experimental.pallas import tpu as pltpu
from jax.sharding import PartitionSpec as P

LANES = 128
VMEM_LIMIT = 56 * 1024 * 1024


def swap_units(parts, unit):
    lane = lax.broadcasted_iota(jnp.int32, parts[0].shape, 1)
    step = 1
    parts = list(parts)
    while step < len(parts):
        shift = unit * step
        high = (lane & shift) != 0
        for i in range(len(parts)):
            if not i & step:
                a, b = parts[i], parts[i | step]
                parts[i] = jnp.where(high, pltpu.roll(b, shift, 1), a)
                parts[i | step] = jnp.where(high, b, pltpu.roll(a, LANES - shift, 1))
        step *= 2
    return parts


def row_tile(rows, most):
    tile = most
    while rows % tile:
        tile -= 16
    return tile


def ordered_after(value, *others):
    anywhere = pl.BlockSpec(memory_space=pl.ANY)
    return pl.pallas_call(
        lambda *refs: None,
        in_specs=[anywhere] * (1 + len(others)),
        out_specs=anywhere,
        out_shape=jax.ShapeDtypeStruct(value.shape, value.dtype),
        input_output_aliases={0: 0},
        name="ordered_after",
    )(value, *others)


def unit_circle(wave, points):
    lane = lax.broadcasted_iota(jnp.int32, (wave.shape[0], LANES), 1).astype(jnp.float32)
    product = wave.astype(jnp.float32) * lane
    rest = product - points * jnp.floor(product * (1.0 / points))
    quarter = jnp.floor(rest * (4.0 / points) + 0.5)
    x = (rest - quarter * (points / 4.0)) * (2.0 * math.pi / points)
    y = x * x
    sine = x * (1 + y * (-1 / 6 + y * (1 / 120 + y * (-1 / 5040 + y * (1 / 362880)))))
    cosine = 1 + y * (-1 / 2 + y * (1 / 24 + y * (-1 / 720 + y * (1 / 40320))))
    odd = jnp.logical_or(quarter == 1, quarter == 3)
    cos_low = jnp.logical_or(quarter == 1, quarter == 2)
    sin_low = jnp.logical_or(quarter == 2, quarter == 3)
    cos_all = jnp.where(odd, sine, cosine)
    sin_all = jnp.where(odd, cosine, sine)
    return jnp.where(cos_low, -cos_all, cos_all), jnp.where(sin_low, -sin_all, sin_all)


def table_kernel(waves, table):
    count, points = waves.shape[0], table.shape[1]
    part = min(64, count)
    for lo in range(0, count, part):
        wave = waves[lo : lo + part, :]
        cos, sin = unit_circle(wave, points)
        cos, sin = jnp.where(wave < 0, 0.0, cos), jnp.where(wave < 0, 0.0, sin)
        half = LANES // 2
        cos_half, sin_half = cos[:, half : half + 1], sin[:, half : half + 1]
        cos_turn = jnp.broadcast_to(cos_half * cos_half - sin_half * sin_half, cos.shape)
        sin_turn = jnp.broadcast_to(2.0 * sin_half * cos_half, cos.shape)
        for a in range(points // LANES):
            both = jnp.stack(
                [cos.reshape(part // 8, 8, LANES), -sin.reshape(part // 8, 8, LANES)], axis=1
            )
            table[2 * lo : 2 * (lo + part), a * LANES : (a + 1) * LANES] = both.reshape(
                2 * part, LANES
            ).astype(table.dtype)
            cos, sin = cos * cos_turn - sin * sin_turn, sin * cos_turn + cos * sin_turn


def trig_table(pair_m, width, points, devices, groups, group, some):
    pair_dev = pair_m.shape[0] // devices
    lower = pair_m.reshape(devices, pair_dev)
    waves = jnp.stack([lower, width - 1 - lower], axis=2)
    waves = jnp.pad(
        waves, ((0, 0), (0, groups * group - pair_dev), (0, 0)), constant_values=-1
    )
    waves = waves.reshape(devices, groups, 2 * group)[:, :some]
    waves = jnp.swapaxes(waves, 0, 1).reshape(-1, 1)
    count = waves.shape[0]
    tile = LANES if count % LANES == 0 else count
    return pl.pallas_call(
        table_kernel,
        grid=(count // tile,),
        in_specs=[pl.BlockSpec((tile, 1), lambda t: (t, 0))],
        out_specs=pl.BlockSpec((2 * tile, points), lambda t: (t, 0)),
        out_shape=jax.ShapeDtypeStruct((2 * count, points), jnp.bfloat16),
        cost_estimate=pl.CostEstimate(
            flops=8 * count * points, bytes_accessed=4 * count * points, transcendentals=0
        ),
        name="trig_table",
    )(waves)


def forward_kernel(levels, unit, grid_ref, table_ref, weight_ref, out_ref, scratch):
    cols = table_ref.shape[0]
    rows = grid_ref.shape[1]
    cap = rows // levels
    tile = row_tile(cap, 32)
    for s in range(0, cap, tile):
        lo = s * levels
        values = lax.dot_general(
            grid_ref[0, lo : lo + tile * levels, :],
            table_ref[...],
            (((1,), (1,)), ((), ())),
            preferred_element_type=jnp.float32,
        )
        for n in range(cols // LANES):
            scratch[n, lo : lo + tile * levels, :] = values[:, n * LANES : (n + 1) * LANES]
        weight = weight_ref[s : s + tile, :]
        for n in range(cols // LANES):
            parts = [
                scratch[n, pl.ds(lo + l, tile, stride=levels), :] * weight for l in range(levels)
            ]
            for a, part in enumerate(swap_units(parts, unit)):
                out_ref[n * levels + a, 0, s : s + tile, :] = part.astype(jnp.bfloat16)


def forward(fields, groups, grid, table, weights, levels, unit, devices):
    _, rows, points = grid.shape
    cap = rows // levels
    wide = 2 * levels if devices % (2 * levels) == 0 else levels
    steps = devices // wide
    (first_field, some_fields), (first, some) = fields, groups
    count = some_fields * some
    columns = count * devices * unit
    return pl.pallas_call(
        functools.partial(forward_kernel, levels, unit),
        grid=(count, steps),
        in_specs=[
            pl.BlockSpec((1, rows, points), lambda i, t: (first_field + i // some, 0, 0)),
            pl.BlockSpec((wide * unit, points), lambda i, t: ((first + i % some) * steps + t, 0)),
            pl.BlockSpec((cap, LANES), lambda i, t: (0, 0)),
        ],
        out_specs=pl.BlockSpec((wide, 1, cap, LANES), lambda i, t: (t, i, 0, 0)),
        out_shape=jax.ShapeDtypeStruct((devices, count, cap, LANES), jnp.bfloat16),
        scratch_shapes=[pltpu.VMEM((wide * unit // LANES, rows, LANES), jnp.float32)],
        compiler_params=pltpu.CompilerParams(vmem_limit_bytes=VMEM_LIMIT),
        cost_estimate=pl.CostEstimate(
            flops=2 * rows * points * columns,
            bytes_accessed=2 * (rows * points + columns * points + rows * columns),
            transcendentals=0,
        ),
        name="forward_dft",
    )(grid, table, weights)


def inverse_kernel(levels, unit, groups, first_row, count_ref, *refs):
    spec_refs, table_ref = refs[:groups], refs[groups]
    out_ref, token_ref, turned = refs[-3:]
    devices, rows, _ = spec_refs[0].shape
    tile = row_tile(rows, 32)
    blocks = [(i, d) for i in range(groups) for d in range(0, devices, levels)]
    base = first_row + pl.program_id(0) * rows
    for s in range(0, rows, tile):
        lines = pl.ds(s * levels, tile * levels)
        for n, (i, d) in enumerate(blocks):
            parts = [
                spec_refs[i][d + a, s : s + tile, :].astype(jnp.float32) for a in range(levels)
            ]
            for l, part in enumerate(swap_units(parts, unit)):
                turned[n, pl.ds(s * levels + l, tile, stride=levels), :] = part
        row = lax.broadcasted_iota(jnp.int32, (tile * levels, LANES), 0)
        valid = row < (count_ref[0] - base - s) * levels
        columns = jnp.concatenate(
            [
                jnp.where(valid, turned[n, lines, :], 0.0).astype(jnp.bfloat16)
                for n in range(len(blocks))
            ],
            axis=1,
        )
        out_ref[0, lines, :] = jnp.dot(
            columns, table_ref[...], preferred_element_type=jnp.float32
        ).astype(out_ref.dtype)
    token_ref[...] = jnp.zeros_like(token_ref)


def inverse(field, first_row, size, spec, offset, groups, table, count, partial, shape, levels, unit):
    devices = spec.shape[0]
    columns, points = table.shape
    tile = row_tile(size, 64 if size % 64 == 0 and offset % 64 == 0 else 32)
    if size <= 64:
        tile = row_tile(size, 32)
    rows = tile * levels

    def part(i):
        return pl.BlockSpec(
            (devices, tile, LANES), lambda t, c: (0, (offset + i * size) // tile + t, 0)
        )

    in_specs = [part(i) for i in range(groups)]
    in_specs.append(pl.BlockSpec((columns, points), lambda t, c: (0, 0)))
    operands = [spec] * groups + [table]
    if partial is not None:
        in_specs.append(pl.BlockSpec(memory_space=pl.ANY))
        operands.append(partial)
    return pl.pallas_call(
        functools.partial(inverse_kernel, levels, unit, groups, first_row),
        grid_spec=pltpu.PrefetchScalarGridSpec(
            num_scalar_prefetch=1,
            grid=(size // tile,),
            in_specs=in_specs,
            out_specs=[
                pl.BlockSpec((1, rows, points), lambda t, c: (field, first_row // tile + t, 0)),
                pl.BlockSpec((8, LANES), lambda t, c: (0, 0)),
            ],
            scratch_shapes=[pltpu.VMEM((columns // LANES, rows, LANES), jnp.float32)],
        ),
        out_shape=[
            jax.ShapeDtypeStruct(shape, jnp.bfloat16),
            jax.ShapeDtypeStruct((8, LANES), jnp.float32),
        ],
        input_output_aliases={} if partial is None else {groups + 2: 0},
        compiler_params=pltpu.CompilerParams(vmem_limit_bytes=VMEM_LIMIT),
        cost_estimate=pl.CostEstimate(
            flops=2 * size * levels * points * columns,
            bytes_accessed=2 * (size * levels * (points + columns) + columns * points),
            transcendentals=0,
        ),
        name="inverse_dft",
    )(count, *operands)


def lane_levels(levels, group):
    lane = lax.broadcasted_iota(jnp.int32, (LANES, levels * group), 0)
    level = lax.broadcasted_iota(jnp.int32, (LANES, levels * group), 1)
    held = lane // 2 % group * levels + lane // (4 * group)
    return (held == level).astype(jnp.float32)


def exact_dot(a, b, dims=((1,), (0,))):
    return lax.dot_general(
        a, b, (dims, ((), ())), precision=lax.Precision.HIGHEST, preferred_element_type=jnp.float32
    )


def lane_matrix(matrix, levels, group):
    chosen = lane_levels(levels, group)
    spread = exact_dot(exact_dot(chosen, matrix), chosen, ((1,), (1,)))
    row = lax.broadcasted_iota(jnp.int32, spread.shape, 0)
    lane = lax.broadcasted_iota(jnp.int32, spread.shape, 1)
    same = jnp.logical_and(
        row % 2 == lane % 2, row // (2 * group) % 2 == lane // (2 * group) % 2
    )
    return jnp.where(same, spread, 0.0)


def legendre_kernel(
    kind, first, pair_dev, lat_groups, group, outs, counts_ref, waves_ref, recv_ref, leg_ref, *rest
):
    gathered, made = rest[-2:]
    rest, out_refs = rest[:-2], rest[-2 - outs : -2]
    level_ref = rest[0]
    if kind == "divergence":
        modes_ref, div_out = rest[1], out_refs[-1]
        out_refs = out_refs[:-1]
    if kind == "temperature":
        balance_ref, div_in = rest[1:3]
    levels = level_ref.shape[1] // group
    row_count, lat_total = leg_ref.shape[1:]
    width = row_count - 1
    cap = recv_ref.shape[2]
    member = pl.program_id(1)
    pair = (first + pl.program_id(0)) * group + member

    @pl.when(member == 0)
    def _():
        start = 0
        for g in range(lat_groups):
            parts = [recv_ref[g * group + h, 0].astype(jnp.float32) for h in range(group)]
            for b, part in enumerate(swap_units(parts, 2)):
                gathered[b, pl.ds(start, cap), :] = part
            start = start + counts_ref[g]

    @pl.when(pair < pair_dev)
    def _():
        wave = waves_ref[pair]
        coeffs = gathered[member, :lat_total, :].astype(jnp.bfloat16)
        main = leg_ref[0, :width, :]
        last = jnp.broadcast_to(leg_ref[0, width:, :], (16, lat_total))
        spectral = jnp.concatenate(
            [
                jnp.dot(main, coeffs, preferred_element_type=jnp.float32),
                jnp.dot(last, coeffs, preferred_element_type=jnp.float32),
            ],
            axis=0,
        )
        shape = spectral.shape
        row = lax.broadcasted_iota(jnp.int32, shape, 0)
        lane = lax.broadcasted_iota(jnp.int32, shape, 1)
        own = row < width - wave
        upper = (lane & 1) != 0
        keep = jnp.logical_and(jnp.logical_xor(own, upper), row < row_count)
        degree = jnp.where(own, row + wave, row - 1)
        ratio = (degree * (degree + 1)).astype(jnp.float32) / float(width * (width - 1))
        spectral = jnp.where(keep, spectral, 0.0)
        if kind != "temperature":
            per_level = jnp.broadcast_to(level_ref[...], (8, level_ref.shape[1]))
            per_lane = exact_dot(per_level, lane_levels(levels, group), ((1,), (1,)))[:1]
        if kind == "vorticity":
            new = spectral / (1.0 + per_lane * ratio * ratio)
        elif kind == "divergence":
            modes_matrix = lane_matrix(modes_ref[...], levels, group)
            modes = exact_dot(spectral, modes_matrix, ((1,), (1,)))
            modes = modes / (1.0 + per_lane * ratio)
            new = exact_dot(modes, modes_matrix)
            div_out[0] = new
        else:
            balance = lane_matrix(balance_ref[...], levels, group)
            new = spectral - exact_dot(div_in[0], balance, ((1,), (1,)))
        zonal = jnp.logical_and(wave == 0, jnp.logical_not(upper))
        new = new * jnp.where(zonal, 1.0, 2.0)
        tail = jnp.concatenate(
            [new[width:], jnp.zeros((LANES - 16, LANES), jnp.float32)], axis=0
        )
        turned = jnp.dot(
            new[:width].T.astype(jnp.bfloat16), main, preferred_element_type=jnp.float32
        )
        turned += jnp.dot(
            tail.T.astype(jnp.bfloat16),
            jnp.broadcast_to(leg_ref[0, width:, :], (LANES, lat_total)),
            preferred_element_type=jnp.float32,
        )
        made[member, :lat_total, :] = turned.T
        made[member, lat_total:, :] = jnp.zeros((cap, LANES), jnp.float32)

    @pl.when(pair >= pair_dev)
    def _():
        made[member] = jnp.zeros(made.shape[1:], jnp.float32)

    @pl.when(member == group - 1)
    def _():
        start = 0
        for g in range(lat_groups):
            parts = [made[b, pl.ds(start, cap), :] for b in range(group)]
            for h, part in enumerate(swap_units(parts, 2)):
                row = 0
                for out_ref in out_refs:
                    size = out_ref.shape[1]
                    out_ref[g * group + h] = part[row : row + size].astype(jnp.bfloat16)
                    row += size
            start = start + counts_ref[g]


def legendre_step(
    kind, first, some, source, received, targets, legendre, counts, waves, levels, extra, group, partial
):
    devices, _, cap, _ = received.shape
    pair_dev, row_count, lat_total = legendre.shape
    lat_groups = devices // group

    def at_pair(i, b, *_):
        return (jnp.minimum((first + i) * group + b, pair_dev - 1), 0, 0)

    def whole(i, b, *_):
        return (0, 0)

    def blocks(size, offset):
        return pl.BlockSpec(
            (devices, size, LANES), lambda i, b, *_: (0, offset // size + first + i, 0)
        )

    square = pl.BlockSpec(extra[0].shape, whole) if extra else None
    div_block = pl.BlockSpec((1, row_count + 15, LANES), at_pair)
    in_specs = [
        pl.BlockSpec((devices, 1, cap, LANES), lambda i, b, *_: (0, source + i, 0, 0)),
        pl.BlockSpec((1, row_count, lat_total), at_pair),
        pl.BlockSpec((1, levels.shape[0]), whole),
    ]
    out_specs = [blocks(size, offset) for size, offset, _ in targets]
    out_shape = [
        jax.ShapeDtypeStruct((devices, total, LANES), jnp.bfloat16) for _, _, total in targets
    ]
    if kind == "divergence":
        in_specs.append(square)
        out_specs.append(div_block)
        out_shape.append(jax.ShapeDtypeStruct((pair_dev, row_count + 15, LANES), jnp.float32))
    elif kind == "temperature":
        in_specs += [square, div_block]
    operands = [counts, waves, received, legendre, levels[None, :], *extra]
    aliases = {}
    if partial is not None:
        aliases = {len(operands): 0}
        in_specs.append(pl.BlockSpec(memory_space=pl.ANY))
        operands.append(partial)
    held = pltpu.VMEM((group, lat_total + cap, LANES), jnp.float32)
    return pl.pallas_call(
        functools.partial(
            legendre_kernel, kind, first, pair_dev, lat_groups, group, len(out_specs)
        ),
        grid_spec=pltpu.PrefetchScalarGridSpec(
            num_scalar_prefetch=2,
            grid=(some, group),
            in_specs=in_specs,
            out_specs=out_specs,
            scratch_shapes=[held, held],
        ),
        out_shape=out_shape,
        input_output_aliases=aliases,
        compiler_params=pltpu.CompilerParams(vmem_limit_bytes=VMEM_LIMIT),
        cost_estimate=pl.CostEstimate(
            flops=8 * some * group * row_count * lat_total * LANES,
            bytes_accessed=2 * some * (group * row_count * lat_total + 2 * devices * cap * LANES),
            transcendentals=0,
        ),
        name="legendre_" + kind,
    )(*operands)


def shards(
    grid,
    legendre,
    gauss_weights,
    band_counts,
    pair_m,
    vert_modes,
    mode_depth,
    diffusion,
    pressure_balance_matrix,
):
    lat_groups = lax.axis_size("lat")
    group = lax.axis_size("lev")
    devices = lat_groups * group
    fields, cap, levels, points = grid.shape
    pair_dev, row_count, _ = legendre.shape
    width = row_count - 1
    unit = 4 * group
    groups = -(-pair_dev // group)
    band = lax.axis_index("lat")
    owner = band * group + lax.axis_index("lev")


    bands = jnp.arange(lat_groups, dtype=jnp.int32)
    start = jnp.sum(jnp.where(bands < band, band_counts, 0))
    count = jnp.sum(jnp.where(bands == band, band_counts, 0))
    weights = lax.dynamic_slice(jnp.pad(gauss_weights, (0, cap)), (start,), (cap,))
    weights = jnp.where(jnp.arange(cap, dtype=jnp.int32) < count, weights / points, 0.0)
    weights = jnp.broadcast_to(weights[:, None], (cap, LANES))

    waves = lax.dynamic_slice(pair_m, (owner * pair_dev,), (pair_dev,))

    rows = grid.reshape(fields, cap * levels, points)

    def exchange(blocks):
        return lax.all_to_all(
            blocks, ("lat", "lev"), split_axis=0, concat_axis=0, tiled=True
        )

    ahead = 1 if groups > 1 else groups
    make_table = functools.partial(
        trig_table, width=width, points=points, devices=devices, groups=groups, group=group
    )
    dft = functools.partial(forward, grid=rows, levels=levels, unit=unit, devices=devices)
    table = make_table(pair_m, some=ahead)
    sent = dft((0, 1), (0, ahead), table=table, weights=weights)
    received = [(0, ahead, exchange(sent))]
    if ahead < groups:
        later_m, _ = lax.optimization_barrier((pair_m, sent))
        table = make_table(later_m, some=groups)
        sent = dft((0, 1), (ahead, groups - ahead), table=table, weights=weights)
        received.append((ahead, groups - ahead, exchange(sent)))
    weights, _ = lax.optimization_barrier((weights, sent))
    others = exchange(dft((1, fields - 1), (0, groups), table=table, weights=weights))

    step = functools.partial(
        legendre_step, legendre=legendre, counts=band_counts, waves=waves, group=group
    )
    vorticity = None
    for first, some, blocks in received:
        (vorticity,) = step(
            "vorticity",
            first,
            some,
            0,
            blocks,
            targets=[(cap, 0, groups * cap)],
            levels=diffusion,
            extra=(),
            partial=vorticity,
        )
    vorticity = exchange(ordered_after(vorticity, others))
    late = max(16, cap // 3 // 16 * 16)
    if late >= cap or groups * (cap - late) % cap or (cap - late) % late:
        late = 0
    main, offset = cap - late, groups * (cap - late)
    total = offset + groups * cap
    back, new_divergence = step(
        "divergence",
        0,
        groups,
        0,
        others,
        targets=[(cap, offset, total)],
        levels=mode_depth,
        extra=(vert_modes,),
        partial=None,
    )
    targets = [(main, 0, total)] + ([(late, 0, groups * late)] if late else [])
    back, *rest = step(
        "temperature",
        0,
        groups,
        groups,
        others,
        targets=targets,
        levels=diffusion,
        extra=(pressure_balance_matrix, new_divergence),
        partial=back,
    )
    to_grid = functools.partial(
        inverse,
        groups=groups,
        table=table,
        count=count[None],
        shape=(fields, cap * levels, points),
        levels=levels,
        unit=unit,
    )
    out, token = to_grid(0, 0, cap, vorticity, 0, partial=None)
    back = exchange(back)
    if late:
        last = exchange(ordered_after(rest[0], back, token))
    out, _ = to_grid(1, 0, cap, back, offset, partial=out)
    out, _ = to_grid(2, 0, main, back, 0, partial=out)
    if late:
        out, _ = to_grid(2, main, late, last, 0, partial=out)
    return out.reshape(fields, cap, levels, points)


def solution(mesh):
    placed = (
        P(None, "lat", "lev", None),
        P(("lat", "lev"), None, None),
        P(),
        P(),
        P(),
        P(),
        P(),
        P(),
        P(),
    )
    return jax.shard_map(
        shards, mesh=mesh, in_specs=placed, out_specs=P(None, "lat", "lev", None), check_vma=False
    )
```

```python
import functools
import math

import jax
import jax.numpy as jnp
from jax import lax
from jax.experimental import pallas as pl
from jax.experimental.pallas import tpu as pltpu
from jax.sharding import PartitionSpec as P

LANES = 128
VMEM_LIMIT = 56 * 1024 * 1024


def swap_units(parts, unit):
    lane = lax.broadcasted_iota(jnp.int32, parts[0].shape, 1)
    step = 1
    parts = list(parts)
    while step < len(parts):
        shift = unit * step
        high = (lane & shift) != 0
        for i in range(len(parts)):
            if not i & step:
                a, b = parts[i], parts[i | step]
                parts[i] = jnp.where(high, pltpu.roll(b, shift, 1), a)
                parts[i | step] = jnp.where(high, b, pltpu.roll(a, LANES - shift, 1))
        step *= 2
    return parts


def row_tile(rows, most):
    tile = most
    while rows % tile:
        tile -= 16
    return tile


def ordered_after(value, *others):
    anywhere = pl.BlockSpec(memory_space=pl.ANY)
    return pl.pallas_call(
        lambda *refs: None,
        in_specs=[anywhere] * (1 + len(others)),
        out_specs=anywhere,
        out_shape=jax.ShapeDtypeStruct(value.shape, value.dtype),
        input_output_aliases={0: 0},
        name="ordered_after",
    )(value, *others)


def unit_circle(wave, points):
    lane = lax.broadcasted_iota(jnp.int32, wave.shape, 1).astype(jnp.float32)
    product = wave.astype(jnp.float32) * lane
    rest = product - points * jnp.floor(product * (1.0 / points))
    quarter = jnp.floor(rest * (4.0 / points) + 0.5)
    x = (rest - quarter * (points / 4.0)) * (2.0 * math.pi / points)
    y = x * x
    sine = x * (1 + y * (-1 / 6 + y * (1 / 120 + y * (-1 / 5040 + y * (1 / 362880)))))
    cosine = 1 + y * (-1 / 2 + y * (1 / 24 + y * (-1 / 720 + y * (1 / 40320))))
    odd = jnp.logical_or(quarter == 1, quarter == 3)
    cos_low = jnp.logical_or(quarter == 1, quarter == 2)
    sin_low = jnp.logical_or(quarter == 2, quarter == 3)
    cos_all = jnp.where(odd, sine, cosine)
    sin_all = jnp.where(odd, cosine, sine)
    return jnp.where(cos_low, -cos_all, cos_all), jnp.where(sin_low, -sin_all, sin_all)


def wave_rows(pair_ref, pair_dev, group, width, pair_group, device):
    row = lax.broadcasted_iota(jnp.int32, (2 * group, LANES), 0)
    wave = jnp.full((2 * group, LANES), -1, jnp.int32)
    for b in range(group):
        pair = pair_group * group + b
        lower = pair_ref[device * pair_dev + jnp.minimum(pair, pair_dev - 1)]
        both = jnp.where(row % 2 == 0, lower, width - 1 - lower)
        wave = jnp.where(jnp.logical_and(row // 2 == b, pair < pair_dev), both, wave)
    return wave


def fill_table(table, pair_ref, pair_dev, group, width, pair_group, first_device):
    points = table.shape[-1]
    some = 64 // (2 * group)
    count = 2 * some * group

    @pl.loop(0, table.shape[0] // (2 * count))
    def _(n):
        wave = jnp.concatenate(
            [
                wave_rows(pair_ref, pair_dev, group, width, pair_group, first_device + n * some + d)
                for d in range(some)
            ],
            axis=0,
        )
        cos, sin = unit_circle(wave, points)
        cos, sin = jnp.where(wave < 0, 0.0, cos), jnp.where(wave < 0, 0.0, sin)
        half = LANES // 2
        cos_half, sin_half = cos[:, half : half + 1], sin[:, half : half + 1]
        cos_turn = jnp.broadcast_to(cos_half * cos_half - sin_half * sin_half, cos.shape)
        sin_turn = jnp.broadcast_to(2.0 * sin_half * cos_half, cos.shape)
        at = pl.ds(pl.multiple_of(n * 2 * count, 2 * count), 2 * count)
        for a in range(points // LANES):
            both = jnp.stack(
                [cos.reshape(some, 2 * group, LANES), -sin.reshape(some, 2 * group, LANES)], axis=1
            )
            table[at, a * LANES : (a + 1) * LANES] = both.reshape(2 * count, LANES).astype(
                table.dtype
            )
            cos, sin = cos * cos_turn - sin * sin_turn, sin * cos_turn + cos * sin_turn


def table_kernel(pair_dev, group, width, wide, pair_ref, table):
    fill_table(
        table, pair_ref, pair_dev, group, width, pl.program_id(0), pl.program_id(1) * wide
    )


def trig_table(pair_m, width, points, devices, groups, group):
    pair_dev = pair_m.shape[0] // devices
    wide = 16 if devices % 16 == 0 else 8
    rows = wide * 4 * group
    steps = devices // wide
    return pl.pallas_call(
        functools.partial(table_kernel, pair_dev, group, width, wide),
        grid_spec=pltpu.PrefetchScalarGridSpec(
            num_scalar_prefetch=1,
            grid=(groups, steps),
            in_specs=[],
            out_specs=pl.BlockSpec((rows, points), lambda i, t, m: (i * steps + t, 0)),
        ),
        out_shape=jax.ShapeDtypeStruct((groups * steps * rows, points), jnp.bfloat16),
        cost_estimate=pl.CostEstimate(
            flops=4 * groups * steps * rows * points,
            bytes_accessed=2 * groups * steps * rows * points,
            transcendentals=0,
        ),
        name="trig_table",
    )(pair_m)


def forward_kernel(levels, unit, grid_ref, table_ref, out_ref, scratch):
    cols = table_ref.shape[0]
    rows = grid_ref.shape[1]
    cap = rows // levels
    tile = row_tile(cap, 32)
    for s in range(0, cap, tile):
        lo = s * levels
        values = lax.dot_general(
            grid_ref[0, lo : lo + tile * levels, :],
            table_ref[...],
            (((1,), (1,)), ((), ())),
            preferred_element_type=jnp.float32,
        )
        for n in range(cols // LANES):
            scratch[n, lo : lo + tile * levels, :] = values[:, n * LANES : (n + 1) * LANES]
        for n in range(cols // LANES):
            parts = [scratch[n, pl.ds(lo + l, tile, stride=levels), :] for l in range(levels)]
            for a, part in enumerate(swap_units(parts, unit)):
                out_ref[n * levels + a, 0, s : s + tile, :] = part.astype(jnp.bfloat16)


def forward(fields, groups, grid, table, levels, unit, devices):
    _, rows, points = grid.shape
    cap = rows // levels
    wide = 2 * levels if devices % (2 * levels) == 0 else levels
    steps = devices // wide
    (first_field, some_fields), (first, some) = fields, groups
    count = some_fields * some
    columns = count * devices * unit
    return pl.pallas_call(
        functools.partial(forward_kernel, levels, unit),
        grid=(count, steps),
        in_specs=[
            pl.BlockSpec((1, rows, points), lambda i, t: (first_field + i // some, 0, 0)),
            pl.BlockSpec((wide * unit, points), lambda i, t: ((first + i % some) * steps + t, 0)),
        ],
        out_specs=pl.BlockSpec((wide, 1, cap, LANES), lambda i, t: (t, i, 0, 0)),
        out_shape=jax.ShapeDtypeStruct((devices, count, cap, LANES), jnp.bfloat16),
        scratch_shapes=[pltpu.VMEM((wide * unit // LANES, rows, LANES), jnp.float32)],
        compiler_params=pltpu.CompilerParams(vmem_limit_bytes=VMEM_LIMIT),
        cost_estimate=pl.CostEstimate(
            flops=2 * rows * points * columns,
            bytes_accessed=2 * (rows * points + columns * points + rows * columns),
            transcendentals=0,
        ),
        name="forward_dft",
    )(grid, table)


def first_kernel(levels, unit, pair_dev, group, width, pair_ref, grid_ref, out_ref, table, scratch):
    @pl.when(pl.program_id(0) == 0)
    def _():
        fill_table(table, pair_ref, pair_dev, group, width, 0, 0)

    tile = grid_ref.shape[1] // levels
    wide = min(2 * LANES, table.shape[0])
    for lo in range(0, table.shape[0], wide):
        values = lax.dot_general(
            grid_ref[0],
            table[lo : lo + wide, :],
            (((1,), (1,)), ((), ())),
            preferred_element_type=jnp.float32,
        )
        for n in range(lo // LANES, (lo + wide) // LANES):
            scratch[n] = values[:, n * LANES - lo : (n + 1) * LANES - lo]
            parts = [scratch[n, pl.ds(l, tile, stride=levels), :] for l in range(levels)]
            for a, part in enumerate(swap_units(parts, unit)):
                out_ref[n * levels + a, 0] = part.astype(jnp.bfloat16)


def forward_first(grid, pair_m, levels, unit, devices, group, width):
    _, rows, points = grid.shape
    cap = rows // levels
    tile = row_tile(cap, 32)
    columns = devices * unit
    return pl.pallas_call(
        functools.partial(
            first_kernel, levels, unit, pair_m.shape[0] // devices, group, width
        ),
        grid_spec=pltpu.PrefetchScalarGridSpec(
            num_scalar_prefetch=1,
            grid=(cap // tile,),
            in_specs=[pl.BlockSpec((1, tile * levels, points), lambda t, m: (0, t, 0))],
            out_specs=pl.BlockSpec((devices, 1, tile, LANES), lambda t, m: (0, 0, t, 0)),
            scratch_shapes=[
                pltpu.VMEM((columns, points), jnp.bfloat16),
                pltpu.VMEM((columns // LANES, tile * levels, LANES), jnp.float32),
            ],
        ),
        out_shape=jax.ShapeDtypeStruct((devices, 1, cap, LANES), jnp.bfloat16),
        compiler_params=pltpu.CompilerParams(vmem_limit_bytes=VMEM_LIMIT),
        cost_estimate=pl.CostEstimate(
            flops=2 * rows * points * columns,
            bytes_accessed=2 * rows * (points + columns),
            transcendentals=0,
        ),
        name="forward_first",
    )(pair_m, grid)


def inverse_kernel(levels, unit, groups, first_row, count_ref, *refs):
    spec_refs, table_ref = refs[:groups], refs[groups]
    out_ref, token_ref, turned = refs[-3:]
    devices, rows, _ = spec_refs[0].shape
    tile = row_tile(rows, 32)
    blocks = [(i, d) for i in range(groups) for d in range(0, devices, levels)]
    base = first_row + pl.program_id(0) * rows
    for s in range(0, rows, tile):
        lines = pl.ds(s * levels, tile * levels)
        for n, (i, d) in enumerate(blocks):
            parts = [
                spec_refs[i][d + a, s : s + tile, :].astype(jnp.float32) for a in range(levels)
            ]
            for l, part in enumerate(swap_units(parts, unit)):
                turned[n, pl.ds(s * levels + l, tile, stride=levels), :] = part
        row = lax.broadcasted_iota(jnp.int32, (tile * levels, LANES), 0)
        valid = row < (count_ref[0] - base - s) * levels
        columns = jnp.concatenate(
            [
                jnp.where(valid, turned[n, lines, :], 0.0).astype(jnp.bfloat16)
                for n in range(len(blocks))
            ],
            axis=1,
        )
        out_ref[0, lines, :] = jnp.dot(
            columns, table_ref[...], preferred_element_type=jnp.float32
        ).astype(out_ref.dtype)
    token_ref[...] = jnp.zeros_like(token_ref)


def inverse(field, first_row, size, spec, offset, groups, table, count, partial, shape, levels, unit):
    devices = spec.shape[0]
    columns, points = table.shape
    tile = row_tile(size, 64 if size % 64 == 0 and offset % 64 == 0 else 32)
    if size <= 64:
        tile = row_tile(size, 32)
    rows = tile * levels

    def part(i):
        return pl.BlockSpec(
            (devices, tile, LANES), lambda t, c: (0, (offset + i * size) // tile + t, 0)
        )

    in_specs = [part(i) for i in range(groups)]
    in_specs.append(pl.BlockSpec((columns, points), lambda t, c: (0, 0)))
    operands = [spec] * groups + [table]
    if partial is not None:
        in_specs.append(pl.BlockSpec(memory_space=pl.ANY))
        operands.append(partial)
    return pl.pallas_call(
        functools.partial(inverse_kernel, levels, unit, groups, first_row),
        grid_spec=pltpu.PrefetchScalarGridSpec(
            num_scalar_prefetch=1,
            grid=(size // tile,),
            in_specs=in_specs,
            out_specs=[
                pl.BlockSpec((1, rows, points), lambda t, c: (field, first_row // tile + t, 0)),
                pl.BlockSpec((8, LANES), lambda t, c: (0, 0)),
            ],
            scratch_shapes=[pltpu.VMEM((columns // LANES, rows, LANES), jnp.float32)],
        ),
        out_shape=[
            jax.ShapeDtypeStruct(shape, jnp.bfloat16),
            jax.ShapeDtypeStruct((8, LANES), jnp.float32),
        ],
        input_output_aliases={} if partial is None else {groups + 2: 0},
        compiler_params=pltpu.CompilerParams(vmem_limit_bytes=VMEM_LIMIT),
        cost_estimate=pl.CostEstimate(
            flops=2 * size * levels * points * columns,
            bytes_accessed=2 * (size * levels * (points + columns) + columns * points),
            transcendentals=0,
        ),
        name="inverse_dft",
    )(count, *operands)


def lane_levels(levels, group):
    lane = lax.broadcasted_iota(jnp.int32, (LANES, levels * group), 0)
    level = lax.broadcasted_iota(jnp.int32, (LANES, levels * group), 1)
    held = lane // 2 % group * levels + lane // (4 * group)
    return (held == level).astype(jnp.float32)


def exact_dot(a, b, dims=((1,), (0,))):
    return lax.dot_general(
        a, b, (dims, ((), ())), precision=lax.Precision.HIGHEST, preferred_element_type=jnp.float32
    )


def lane_matrix(matrix, levels, group):
    chosen = lane_levels(levels, group)
    spread = exact_dot(exact_dot(chosen, matrix), chosen, ((1,), (1,)))
    row = lax.broadcasted_iota(jnp.int32, spread.shape, 0)
    lane = lax.broadcasted_iota(jnp.int32, spread.shape, 1)
    same = jnp.logical_and(
        row % 2 == lane % 2, row // (2 * group) % 2 == lane // (2 * group) % 2
    )
    return jnp.where(same, spread, 0.0)


def legendre_kernel(
    kind, first, pair_dev, lat_groups, group, outs, counts_ref, waves_ref, recv_ref, leg_ref, *rest
):
    weight_ref, rest = rest[0], rest[1:]
    gathered, made = rest[-2:]
    rest, out_refs = rest[:-2], rest[-2 - outs : -2]
    level_ref = rest[0]
    if kind == "divergence":
        modes_ref, div_out = rest[1], out_refs[-1]
        out_refs = out_refs[:-1]
    if kind == "temperature":
        balance_ref, div_in = rest[1:3]
    levels = level_ref.shape[1] // group
    row_count, lat_total = leg_ref.shape[1:]
    width = row_count - 1
    cap = recv_ref.shape[2]
    member = pl.program_id(1)
    pair = (first + pl.program_id(0)) * group + member

    @pl.when(member == 0)
    def _():
        start = 0
        for g in range(lat_groups):
            parts = [recv_ref[g * group + h, 0].astype(jnp.float32) for h in range(group)]
            for b, part in enumerate(swap_units(parts, 2)):
                gathered[b, pl.ds(start, cap), :] = part
            start = start + counts_ref[g]

    @pl.when(pair < pair_dev)
    def _():
        wave = waves_ref[pair]
        coeffs = (gathered[member, :lat_total, :] * weight_ref[...]).astype(jnp.bfloat16)
        main = leg_ref[0, :width, :]
        last = jnp.broadcast_to(leg_ref[0, width:, :], (16, lat_total))
        spectral = jnp.concatenate(
            [
                jnp.dot(main, coeffs, preferred_element_type=jnp.float32),
                jnp.dot(last, coeffs, preferred_element_type=jnp.float32),
            ],
            axis=0,
        )
        shape = spectral.shape
        row = lax.broadcasted_iota(jnp.int32, shape, 0)
        lane = lax.broadcasted_iota(jnp.int32, shape, 1)
        own = row < width - wave
        upper = (lane & 1) != 0
        keep = jnp.logical_and(jnp.logical_xor(own, upper), row < row_count)
        degree = jnp.where(own, row + wave, row - 1)
        ratio = (degree * (degree + 1)).astype(jnp.float32) / float(width * (width - 1))
        spectral = jnp.where(keep, spectral, 0.0)
        if kind != "temperature":
            per_level = jnp.broadcast_to(level_ref[...], (8, level_ref.shape[1]))
            per_lane = exact_dot(per_level, lane_levels(levels, group), ((1,), (1,)))[:1]
        if kind == "vorticity":
            new = spectral / (1.0 + per_lane * ratio * ratio)
        elif kind == "divergence":
            modes_matrix = lane_matrix(modes_ref[...], levels, group)
            modes = exact_dot(spectral, modes_matrix, ((1,), (1,)))
            modes = modes / (1.0 + per_lane * ratio)
            new = exact_dot(modes, modes_matrix)
            div_out[0] = new
        else:
            balance = lane_matrix(balance_ref[...], levels, group)
            new = spectral - exact_dot(div_in[0], balance, ((1,), (1,)))
        zonal = jnp.logical_and(wave == 0, jnp.logical_not(upper))
        new = new * jnp.where(zonal, 1.0, 2.0)
        tail = jnp.concatenate(
            [new[width:], jnp.zeros((LANES - 16, LANES), jnp.float32)], axis=0
        )
        turned = jnp.dot(
            new[:width].T.astype(jnp.bfloat16), main, preferred_element_type=jnp.float32
        )
        turned += jnp.dot(
            tail.T.astype(jnp.bfloat16),
            jnp.broadcast_to(leg_ref[0, width:, :], (LANES, lat_total)),
            preferred_element_type=jnp.float32,
        )
        made[member, :lat_total, :] = turned.T
        made[member, lat_total:, :] = jnp.zeros((cap, LANES), jnp.float32)

    @pl.when(pair >= pair_dev)
    def _():
        made[member] = jnp.zeros(made.shape[1:], jnp.float32)

    @pl.when(member == group - 1)
    def _():
        start = 0
        for g in range(lat_groups):
            parts = [made[b, pl.ds(start, cap), :] for b in range(group)]
            for h, part in enumerate(swap_units(parts, 2)):
                row = 0
                for out_ref in out_refs:
                    size = out_ref.shape[1]
                    out_ref[g * group + h] = part[row : row + size].astype(jnp.bfloat16)
                    row += size
            start = start + counts_ref[g]


def legendre_step(
    kind, first, some, source, received, targets, legendre, weights, counts, waves, levels, extra, group, partial
):
    devices, _, cap, _ = received.shape
    pair_dev, row_count, lat_total = legendre.shape
    lat_groups = devices // group

    def at_pair(i, b, *_):
        return (jnp.minimum((first + i) * group + b, pair_dev - 1), 0, 0)

    def whole(i, b, *_):
        return (0, 0)

    def blocks(size, offset):
        return pl.BlockSpec(
            (devices, size, LANES), lambda i, b, *_: (0, offset // size + first + i, 0)
        )

    square = pl.BlockSpec(extra[0].shape, whole) if extra else None
    div_block = pl.BlockSpec((1, row_count + 15, LANES), at_pair)
    in_specs = [
        pl.BlockSpec((devices, 1, cap, LANES), lambda i, b, *_: (0, source + i, 0, 0)),
        pl.BlockSpec((1, row_count, lat_total), at_pair),
        pl.BlockSpec((lat_total, LANES), whole),
        pl.BlockSpec((1, levels.shape[0]), whole),
    ]
    out_specs = [blocks(size, offset) for size, offset, _ in targets]
    out_shape = [
        jax.ShapeDtypeStruct((devices, total, LANES), jnp.bfloat16) for _, _, total in targets
    ]
    if kind == "divergence":
        in_specs.append(square)
        out_specs.append(div_block)
        out_shape.append(jax.ShapeDtypeStruct((pair_dev, row_count + 15, LANES), jnp.float32))
    elif kind == "temperature":
        in_specs += [square, div_block]
    operands = [counts, waves, received, legendre, weights, levels[None, :], *extra]
    aliases = {}
    if partial is not None:
        aliases = {len(operands): 0}
        in_specs.append(pl.BlockSpec(memory_space=pl.ANY))
        operands.append(partial)
    held = pltpu.VMEM((group, lat_total + cap, LANES), jnp.float32)
    return pl.pallas_call(
        functools.partial(
            legendre_kernel, kind, first, pair_dev, lat_groups, group, len(out_specs)
        ),
        grid_spec=pltpu.PrefetchScalarGridSpec(
            num_scalar_prefetch=2,
            grid=(some, group),
            in_specs=in_specs,
            out_specs=out_specs,
            scratch_shapes=[held, held],
        ),
        out_shape=out_shape,
        input_output_aliases=aliases,
        compiler_params=pltpu.CompilerParams(vmem_limit_bytes=VMEM_LIMIT),
        cost_estimate=pl.CostEstimate(
            flops=8 * some * group * row_count * lat_total * LANES,
            bytes_accessed=2 * some * (group * row_count * lat_total + 2 * devices * cap * LANES),
            transcendentals=0,
        ),
        name="legendre_" + kind,
    )(*operands)


def shards(
    grid,
    legendre,
    gauss_weights,
    band_counts,
    pair_m,
    vert_modes,
    mode_depth,
    diffusion,
    pressure_balance_matrix,
):
    lat_groups = lax.axis_size("lat")
    group = lax.axis_size("lev")
    devices = lat_groups * group
    fields, cap, levels, points = grid.shape
    pair_dev, row_count, _ = legendre.shape
    width = row_count - 1
    unit = 4 * group
    groups = -(-pair_dev // group)
    band = lax.axis_index("lat")
    owner = band * group + lax.axis_index("lev")


    bands = jnp.arange(lat_groups, dtype=jnp.int32)
    count = jnp.sum(jnp.where(bands == band, band_counts, 0))
    weights = jnp.broadcast_to((gauss_weights / points)[:, None], (gauss_weights.shape[0], LANES))
    waves = lax.dynamic_slice(pair_m, (owner * pair_dev,), (pair_dev,))

    rows = grid.reshape(fields, cap * levels, points)

    def exchange(blocks):
        return lax.all_to_all(
            blocks, ("lat", "lev"), split_axis=0, concat_axis=0, tiled=True
        )

    sent = forward_first(rows, pair_m, levels, unit, devices, group, width)
    received = [(0, 1, exchange(sent))]
    later_m, _ = lax.optimization_barrier((pair_m, sent))
    table = trig_table(later_m, width, points, devices, groups, group)
    dft = functools.partial(
        forward, grid=rows, table=table, levels=levels, unit=unit, devices=devices
    )
    if groups > 1:
        sent = dft((0, 1), (1, groups - 1))
        received.append((1, groups - 1, exchange(sent)))
    others = exchange(dft((1, fields - 1), (0, groups)))

    step = functools.partial(
        legendre_step,
        legendre=legendre,
        weights=weights,
        counts=band_counts,
        waves=waves,
        group=group,
    )
    vorticity = None
    for first, some, blocks in received:
        (vorticity,) = step(
            "vorticity",
            first,
            some,
            0,
            blocks,
            targets=[(cap, 0, groups * cap)],
            levels=diffusion,
            extra=(),
            partial=vorticity,
        )
    vorticity = exchange(ordered_after(vorticity, others))
    late = max(16, cap // 3 // 16 * 16)
    if late >= cap or groups * (cap - late) % cap or (cap - late) % late:
        late = 0
    main, offset = cap - late, groups * (cap - late)
    total = offset + groups * cap
    back, new_divergence = step(
        "divergence",
        0,
        groups,
        0,
        others,
        targets=[(cap, offset, total)],
        levels=mode_depth,
        extra=(vert_modes,),
        partial=None,
    )
    targets = [(main, 0, total)] + ([(late, 0, groups * late)] if late else [])
    back, *rest = step(
        "temperature",
        0,
        groups,
        groups,
        others,
        targets=targets,
        levels=diffusion,
        extra=(pressure_balance_matrix, new_divergence),
        partial=back,
    )
    to_grid = functools.partial(
        inverse,
        groups=groups,
        table=table,
        count=count[None],
        shape=(fields, cap * levels, points),
        levels=levels,
        unit=unit,
    )
    out, token = to_grid(0, 0, cap, vorticity, 0, partial=None)
    back = exchange(back)
    if late:
        last = exchange(ordered_after(rest[0], back, token))
    out, _ = to_grid(1, 0, cap, back, offset, partial=out)
    out, _ = to_grid(2, 0, main, back, 0, partial=out)
    if late:
        out, _ = to_grid(2, main, late, last, 0, partial=out)
    return out.reshape(fields, cap, levels, points)


def solution(mesh):
    placed = (
        P(None, "lat", "lev", None),
        P(("lat", "lev"), None, None),
        P(),
        P(),
        P(),
        P(),
        P(),
        P(),
        P(),
    )
    return jax.shard_map(
        shards, mesh=mesh, in_specs=placed, out_specs=P(None, "lat", "lev", None), check_vma=False
    )
```

```python
import functools
import math

import jax
import jax.numpy as jnp
from jax import lax
from jax.experimental import pallas as pl
from jax.experimental.pallas import tpu as pltpu
from jax.sharding import PartitionSpec as P

LANES = 128
VMEM_LIMIT = 56 * 1024 * 1024


def swap_units(parts, unit):
    lane = lax.broadcasted_iota(jnp.int32, parts[0].shape, 1)
    step = 1
    parts = list(parts)
    while step < len(parts):
        shift = unit * step
        high = (lane & shift) != 0
        for i in range(len(parts)):
            if not i & step:
                a, b = parts[i], parts[i | step]
                parts[i] = jnp.where(high, pltpu.roll(b, shift, 1), a)
                parts[i | step] = jnp.where(high, b, pltpu.roll(a, LANES - shift, 1))
        step *= 2
    return parts


def row_tile(rows, most):
    tile = most
    while rows % tile:
        tile -= 16
    return tile


def ordered_after(value, *others):
    anywhere = pl.BlockSpec(memory_space=pl.ANY)
    return pl.pallas_call(
        lambda *refs: None,
        in_specs=[anywhere] * (1 + len(others)),
        out_specs=anywhere,
        out_shape=jax.ShapeDtypeStruct(value.shape, value.dtype),
        input_output_aliases={0: 0},
        name="ordered_after",
    )(value, *others)


def unit_circle(wave, points):
    lane = lax.broadcasted_iota(jnp.int32, wave.shape, 1).astype(jnp.float32)
    product = wave.astype(jnp.float32) * lane
    rest = product - points * jnp.floor(product * (1.0 / points))
    quarter = jnp.floor(rest * (4.0 / points) + 0.5)
    x = (rest - quarter * (points / 4.0)) * (2.0 * math.pi / points)
    y = x * x
    sine = x * (1 + y * (-1 / 6 + y * (1 / 120 + y * (-1 / 5040 + y * (1 / 362880)))))
    cosine = 1 + y * (-1 / 2 + y * (1 / 24 + y * (-1 / 720 + y * (1 / 40320))))
    odd = jnp.logical_or(quarter == 1, quarter == 3)
    cos_low = jnp.logical_or(quarter == 1, quarter == 2)
    sin_low = jnp.logical_or(quarter == 2, quarter == 3)
    cos_all = jnp.where(odd, sine, cosine)
    sin_all = jnp.where(odd, cosine, sine)
    return jnp.where(cos_low, -cos_all, cos_all), jnp.where(sin_low, -sin_all, sin_all)


def wave_rows(pair_ref, shift_ref, devices, pair_dev, group, width, pair_group, device):
    row = lax.broadcasted_iota(jnp.int32, (2 * group, LANES), 0)
    wave = jnp.full((2 * group, LANES), -1, jnp.int32)
    device = device + shift_ref[0]
    device = jnp.where(device >= devices, device - devices, device)
    for b in range(group):
        pair = pair_group * group + b
        lower = pair_ref[device * pair_dev + jnp.minimum(pair, pair_dev - 1)]
        both = jnp.where(row % 2 == 0, lower, width - 1 - lower)
        wave = jnp.where(jnp.logical_and(row // 2 == b, pair < pair_dev), both, wave)
    return wave


def fill_table(table, waves_of, group, pair_group, first_device):
    points = table.shape[-1]
    some = 64 // (2 * group)
    count = 2 * some * group

    @pl.loop(0, table.shape[0] // (2 * count))
    def _(n):
        wave = jnp.concatenate(
            [
                waves_of(pair_group=pair_group, device=first_device + n * some + d)
                for d in range(some)
            ],
            axis=0,
        )
        cos, sin = unit_circle(wave, points)
        cos, sin = jnp.where(wave < 0, 0.0, cos), jnp.where(wave < 0, 0.0, sin)
        half = LANES // 2
        cos_half, sin_half = cos[:, half : half + 1], sin[:, half : half + 1]
        cos_turn = jnp.broadcast_to(cos_half * cos_half - sin_half * sin_half, cos.shape)
        sin_turn = jnp.broadcast_to(2.0 * sin_half * cos_half, cos.shape)
        at = pl.ds(pl.multiple_of(n * 2 * count, 2 * count), 2 * count)
        for a in range(points // LANES):
            both = jnp.stack(
                [cos.reshape(some, 2 * group, LANES), -sin.reshape(some, 2 * group, LANES)], axis=1
            )
            table[at, a * LANES : (a + 1) * LANES] = both.reshape(2 * count, LANES).astype(
                table.dtype
            )
            cos, sin = cos * cos_turn - sin * sin_turn, sin * cos_turn + cos * sin_turn


def table_kernel(devices, pair_dev, group, width, wide, pair_ref, shift_ref, table):
    waves_of = functools.partial(
        wave_rows, pair_ref, shift_ref, devices, pair_dev, group, width
    )
    fill_table(table, waves_of, group, pl.program_id(0), pl.program_id(1) * wide)


def trig_table(pair_m, shift, width, points, devices, groups, group):
    pair_dev = pair_m.shape[0] // devices
    wide = 16 if devices % 16 == 0 else 8
    rows = wide * 4 * group
    steps = devices // wide
    return pl.pallas_call(
        functools.partial(table_kernel, devices, pair_dev, group, width, wide),
        grid_spec=pltpu.PrefetchScalarGridSpec(
            num_scalar_prefetch=2,
            grid=(groups, steps),
            in_specs=[],
            out_specs=pl.BlockSpec((rows, points), lambda i, t, *_: (i * steps + t, 0)),
        ),
        out_shape=jax.ShapeDtypeStruct((groups * steps * rows, points), jnp.bfloat16),
        cost_estimate=pl.CostEstimate(
            flops=4 * groups * steps * rows * points,
            bytes_accessed=2 * groups * steps * rows * points,
            transcendentals=0,
        ),
        name="trig_table",
    )(pair_m, shift)


def forward_kernel(levels, unit, grid_ref, table_ref, out_ref, scratch):
    cols = table_ref.shape[0]
    rows = grid_ref.shape[1]
    cap = rows // levels
    tile = row_tile(cap, 32)
    for s in range(0, cap, tile):
        lo = s * levels
        values = lax.dot_general(
            grid_ref[0, lo : lo + tile * levels, :],
            table_ref[...],
            (((1,), (1,)), ((), ())),
            preferred_element_type=jnp.float32,
        )
        for n in range(cols // LANES):
            scratch[n, lo : lo + tile * levels, :] = values[:, n * LANES : (n + 1) * LANES]
        for n in range(cols // LANES):
            parts = [scratch[n, pl.ds(lo + l, tile, stride=levels), :] for l in range(levels)]
            for a, part in enumerate(swap_units(parts, unit)):
                out_ref[n * levels + a, 0, s : s + tile, :] = part.astype(jnp.bfloat16)


def forward(fields, groups, grid, table, levels, unit, devices):
    _, rows, points = grid.shape
    cap = rows // levels
    wide = 2 * levels if devices % (2 * levels) == 0 else levels
    steps = devices // wide
    (first_field, some_fields), (first, some) = fields, groups
    count = some_fields * some
    columns = count * devices * unit
    return pl.pallas_call(
        functools.partial(forward_kernel, levels, unit),
        grid=(count, steps),
        in_specs=[
            pl.BlockSpec((1, rows, points), lambda i, t: (first_field + i // some, 0, 0)),
            pl.BlockSpec((wide * unit, points), lambda i, t: ((first + i % some) * steps + t, 0)),
        ],
        out_specs=pl.BlockSpec((wide, 1, cap, LANES), lambda i, t: (t, i, 0, 0)),
        out_shape=jax.ShapeDtypeStruct((devices, count, cap, LANES), jnp.bfloat16),
        scratch_shapes=[pltpu.VMEM((wide * unit // LANES, rows, LANES), jnp.float32)],
        compiler_params=pltpu.CompilerParams(vmem_limit_bytes=VMEM_LIMIT),
        cost_estimate=pl.CostEstimate(
            flops=2 * rows * points * columns,
            bytes_accessed=2 * (rows * points + columns * points + rows * columns),
            transcendentals=0,
        ),
        name="forward_dft",
    )(grid, table)


def first_kernel(
    levels, unit, pair_dev, group, width, pair_ref, shift_ref, grid_ref, out_ref, table, scratch
):
    @pl.when(pl.program_id(0) == 0)
    def _():
        waves_of = functools.partial(
            wave_rows, pair_ref, shift_ref, out_ref.shape[0], pair_dev, group, width
        )
        fill_table(table, waves_of, group, 0, 0)

    tile = grid_ref.shape[1] // levels
    wide = min(2 * LANES, table.shape[0])
    for lo in range(0, table.shape[0], wide):
        values = lax.dot_general(
            grid_ref[0],
            table[lo : lo + wide, :],
            (((1,), (1,)), ((), ())),
            preferred_element_type=jnp.float32,
        )
        for n in range(lo // LANES, (lo + wide) // LANES):
            scratch[n] = values[:, n * LANES - lo : (n + 1) * LANES - lo]
            parts = [scratch[n, pl.ds(l, tile, stride=levels), :] for l in range(levels)]
            for a, part in enumerate(swap_units(parts, unit)):
                out_ref[n * levels + a, 0] = part.astype(jnp.bfloat16)


def forward_first(grid, pair_m, shift, levels, unit, devices, group, width):
    _, rows, points = grid.shape
    cap = rows // levels
    tile = row_tile(cap, 32)
    columns = devices * unit
    return pl.pallas_call(
        functools.partial(
            first_kernel, levels, unit, pair_m.shape[0] // devices, group, width
        ),
        grid_spec=pltpu.PrefetchScalarGridSpec(
            num_scalar_prefetch=2,
            grid=(cap // tile,),
            in_specs=[pl.BlockSpec((1, tile * levels, points), lambda t, *_: (0, t, 0))],
            out_specs=pl.BlockSpec((devices, 1, tile, LANES), lambda t, *_: (0, 0, t, 0)),
            scratch_shapes=[
                pltpu.VMEM((columns, points), jnp.bfloat16),
                pltpu.VMEM((columns // LANES, tile * levels, LANES), jnp.float32),
            ],
        ),
        out_shape=jax.ShapeDtypeStruct((devices, 1, cap, LANES), jnp.bfloat16),
        compiler_params=pltpu.CompilerParams(vmem_limit_bytes=VMEM_LIMIT),
        cost_estimate=pl.CostEstimate(
            flops=2 * rows * points * columns,
            bytes_accessed=2 * rows * (points + columns),
            transcendentals=0,
        ),
        name="forward_first",
    )(pair_m, shift, grid)


def inverse_kernel(levels, unit, has_partial, first_row, count_ref, *refs):
    planes = len(refs) - 4 - (1 if has_partial else 0)
    spec_refs, table_ref = refs[:planes], refs[planes]
    out_ref, token_ref, turned = refs[-3:]
    plane, groups, rows, _ = spec_refs[0].shape
    tile = row_tile(rows, 32)
    blocks = [
        (i, k, d) for i in range(groups) for k in range(planes) for d in range(0, plane, levels)
    ]
    base = first_row + pl.program_id(0) * rows
    for s in range(0, rows, tile):
        lines = pl.ds(s * levels, tile * levels)
        for n, (i, k, d) in enumerate(blocks):
            parts = [
                spec_refs[k][d + a, i, s : s + tile, :].astype(jnp.float32) for a in range(levels)
            ]
            for l, part in enumerate(swap_units(parts, unit)):
                turned[n, pl.ds(s * levels + l, tile, stride=levels), :] = part
        row = lax.broadcasted_iota(jnp.int32, (tile * levels, LANES), 0)
        valid = row < (count_ref[0] - base - s) * levels
        columns = jnp.concatenate(
            [
                jnp.where(valid, turned[n, lines, :], 0.0).astype(jnp.bfloat16)
                for n in range(len(blocks))
            ],
            axis=1,
        )
        out_ref[0, lines, :] = jnp.dot(
            columns, table_ref[...], preferred_element_type=jnp.float32
        ).astype(out_ref.dtype)
    token_ref[...] = jnp.zeros_like(token_ref)


def inverse(field, first_row, specs, table, count, partial, shape, levels, unit):
    plane, groups, size, _ = specs[0].shape
    columns, points = table.shape
    tile = row_tile(size, 64 if size % 64 == 0 and size > 64 else 32)
    rows = tile * levels
    in_specs = [
        pl.BlockSpec((plane, groups, tile, LANES), lambda t, c: (0, 0, t, 0)) for _ in specs
    ]
    in_specs.append(pl.BlockSpec((columns, points), lambda t, c: (0, 0)))
    operands = [*specs, table]
    if partial is not None:
        in_specs.append(pl.BlockSpec(memory_space=pl.ANY))
        operands.append(partial)
    return pl.pallas_call(
        functools.partial(inverse_kernel, levels, unit, partial is not None, first_row),
        grid_spec=pltpu.PrefetchScalarGridSpec(
            num_scalar_prefetch=1,
            grid=(size // tile,),
            in_specs=in_specs,
            out_specs=[
                pl.BlockSpec((1, rows, points), lambda t, c: (field, first_row // tile + t, 0)),
                pl.BlockSpec((8, LANES), lambda t, c: (0, 0)),
            ],
            scratch_shapes=[pltpu.VMEM((columns // LANES, rows, LANES), jnp.float32)],
        ),
        out_shape=[
            jax.ShapeDtypeStruct(shape, jnp.bfloat16),
            jax.ShapeDtypeStruct((8, LANES), jnp.float32),
        ],
        input_output_aliases={} if partial is None else {len(specs) + 2: 0},
        compiler_params=pltpu.CompilerParams(vmem_limit_bytes=VMEM_LIMIT),
        cost_estimate=pl.CostEstimate(
            flops=2 * size * levels * points * columns,
            bytes_accessed=2 * (size * levels * (points + columns) + columns * points),
            transcendentals=0,
        ),
        name="inverse_dft",
    )(count, *operands)


def lane_levels(levels, group):
    lane = lax.broadcasted_iota(jnp.int32, (LANES, levels * group), 0)
    level = lax.broadcasted_iota(jnp.int32, (LANES, levels * group), 1)
    held = lane // 2 % group * levels + lane // (4 * group)
    return (held == level).astype(jnp.float32)


def exact_dot(a, b, dims=((1,), (0,))):
    return lax.dot_general(
        a, b, (dims, ((), ())), precision=lax.Precision.HIGHEST, preferred_element_type=jnp.float32
    )


def lane_matrix(matrix, levels, group):
    chosen = lane_levels(levels, group)
    spread = exact_dot(exact_dot(chosen, matrix), chosen, ((1,), (1,)))
    row = lax.broadcasted_iota(jnp.int32, spread.shape, 0)
    lane = lax.broadcasted_iota(jnp.int32, spread.shape, 1)
    same = jnp.logical_and(
        row % 2 == lane % 2, row // (2 * group) % 2 == lane // (2 * group) % 2
    )
    return jnp.where(same, spread, 0.0)


def legendre_kernel(
    kind, first, pair_dev, lat_groups, group, outs, counts_ref, waves_ref, z_ref, recv_ref, leg_ref, *rest
):
    weight_ref, rest = rest[0], rest[1:]
    gathered, made = rest[-2:]
    rest, out_refs = rest[:-2], rest[-2 - outs : -2]
    level_ref, out_ref = rest[0], out_refs[0]
    if kind == "divergence":
        modes_ref, div_out = rest[1], out_refs[1]
    if kind == "temperature":
        balance_ref, div_in = rest[1:3]
    levels = level_ref.shape[1] // group
    row_count, lat_total = leg_ref.shape[1:]
    width = row_count - 1
    planes, cap = recv_ref.shape[1], recv_ref.shape[3]
    rows_of = lat_groups // planes
    member = pl.program_id(1)
    pair = (first + pl.program_id(0)) * group + member

    @pl.when(member == 0)
    def _():
        start = 0
        for g in range(lat_groups):
            far = (z_ref[0] + planes - g // rows_of) % planes
            near = g % rows_of * group
            parts = [recv_ref[near + h, far, 0].astype(jnp.float32) for h in range(group)]
            for b, part in enumerate(swap_units(parts, 2)):
                gathered[b, pl.ds(start, cap), :] = part
            start = start + counts_ref[g]

    @pl.when(pair < pair_dev)
    def _():
        wave = waves_ref[pair]
        coeffs = (gathered[member, :lat_total, :] * weight_ref[...]).astype(jnp.bfloat16)
        main = leg_ref[0, :width, :]
        last = jnp.broadcast_to(leg_ref[0, width:, :], (16, lat_total))
        spectral = jnp.concatenate(
            [
                jnp.dot(main, coeffs, preferred_element_type=jnp.float32),
                jnp.dot(last, coeffs, preferred_element_type=jnp.float32),
            ],
            axis=0,
        )
        shape = spectral.shape
        row = lax.broadcasted_iota(jnp.int32, shape, 0)
        lane = lax.broadcasted_iota(jnp.int32, shape, 1)
        own = row < width - wave
        upper = (lane & 1) != 0
        keep = jnp.logical_and(jnp.logical_xor(own, upper), row < row_count)
        degree = jnp.where(own, row + wave, row - 1)
        ratio = (degree * (degree + 1)).astype(jnp.float32) / float(width * (width - 1))
        spectral = jnp.where(keep, spectral, 0.0)
        if kind != "temperature":
            per_level = jnp.broadcast_to(level_ref[...], (8, level_ref.shape[1]))
            per_lane = exact_dot(per_level, lane_levels(levels, group), ((1,), (1,)))[:1]
        if kind == "vorticity":
            new = spectral / (1.0 + per_lane * ratio * ratio)
        elif kind == "divergence":
            modes_matrix = lane_matrix(modes_ref[...], levels, group)
            modes = exact_dot(spectral, modes_matrix, ((1,), (1,)))
            modes = modes / (1.0 + per_lane * ratio)
            new = exact_dot(modes, modes_matrix)
            div_out[0] = new
        else:
            balance = lane_matrix(balance_ref[...], levels, group)
            new = spectral - exact_dot(div_in[0], balance, ((1,), (1,)))
        zonal = jnp.logical_and(wave == 0, jnp.logical_not(upper))
        new = new * jnp.where(zonal, 1.0, 2.0)
        tail = jnp.concatenate(
            [new[width:], jnp.zeros((LANES - 16, LANES), jnp.float32)], axis=0
        )
        turned = jnp.dot(
            new[:width].T.astype(jnp.bfloat16), main, preferred_element_type=jnp.float32
        )
        turned += jnp.dot(
            tail.T.astype(jnp.bfloat16),
            jnp.broadcast_to(leg_ref[0, width:, :], (LANES, lat_total)),
            preferred_element_type=jnp.float32,
        )
        made[member, :lat_total, :] = turned.T
        made[member, lat_total:, :] = jnp.zeros((cap, LANES), jnp.float32)

    @pl.when(pair >= pair_dev)
    def _():
        made[member] = jnp.zeros(made.shape[1:], jnp.float32)

    @pl.when(member == group - 1)
    def _():
        start = 0
        for g in range(lat_groups):
            parts = [made[b, pl.ds(start, cap), :] for b in range(group)]
            far = (g // rows_of + planes - z_ref[0]) % planes
            near = g % rows_of * group
            for h, part in enumerate(swap_units(parts, 2)):
                out_ref[near + h, far, 0] = part.astype(jnp.bfloat16)
            start = start + counts_ref[g]


def legendre_step(
    kind, first, received, groups, legendre, weights, counts, waves, z, levels, extra, group, partial
):
    plane, planes, some, cap, _ = received.shape
    pair_dev, row_count, lat_total = legendre.shape
    lat_groups = plane * planes // group

    def at_pair(i, b, *_):
        return (jnp.minimum((first + i) * group + b, pair_dev - 1), 0, 0)

    def whole(i, b, *_):
        return (0, 0)

    square = pl.BlockSpec(extra[0].shape, whole) if extra else None
    div_block = pl.BlockSpec((1, row_count + 15, LANES), at_pair)
    in_specs = [
        pl.BlockSpec((plane, planes, 1, cap, LANES), lambda i, b, *_: (0, 0, i, 0, 0)),
        pl.BlockSpec((1, row_count, lat_total), at_pair),
        pl.BlockSpec((lat_total, LANES), whole),
        pl.BlockSpec((1, levels.shape[0]), whole),
    ]
    out_specs = [
        pl.BlockSpec((plane, planes, 1, cap, LANES), lambda i, b, *_: (0, 0, first + i, 0, 0))
    ]
    out_shape = [jax.ShapeDtypeStruct((plane, planes, groups, cap, LANES), jnp.bfloat16)]
    if kind == "divergence":
        in_specs.append(square)
        out_specs.append(div_block)
        out_shape.append(jax.ShapeDtypeStruct((pair_dev, row_count + 15, LANES), jnp.float32))
    elif kind == "temperature":
        in_specs += [square, div_block]
    operands = [counts, waves, z, received, legendre, weights, levels[None, :], *extra]
    aliases = {}
    if partial is not None:
        aliases = {len(operands): 0}
        in_specs.append(pl.BlockSpec(memory_space=pl.ANY))
        operands.append(partial)
    held = pltpu.VMEM((group, lat_total + cap, LANES), jnp.float32)
    return pl.pallas_call(
        functools.partial(
            legendre_kernel, kind, first, pair_dev, lat_groups, group, len(out_specs)
        ),
        grid_spec=pltpu.PrefetchScalarGridSpec(
            num_scalar_prefetch=3,
            grid=(some, group),
            in_specs=in_specs,
            out_specs=out_specs,
            scratch_shapes=[held, held],
        ),
        out_shape=out_shape,
        input_output_aliases=aliases,
        compiler_params=pltpu.CompilerParams(vmem_limit_bytes=VMEM_LIMIT),
        cost_estimate=pl.CostEstimate(
            flops=8 * some * group * row_count * lat_total * LANES,
            bytes_accessed=2 * (some * group * row_count * lat_total + 2 * received.size),
            transcendentals=0,
        ),
        name="legendre_" + kind,
    )(*operands)


def shards(
    grid,
    legendre,
    gauss_weights,
    band_counts,
    pair_m,
    vert_modes,
    mode_depth,
    diffusion,
    pressure_balance_matrix,
):
    lat_groups = lax.axis_size("lat")
    group = lax.axis_size("lev")
    devices = lat_groups * group
    fields, cap, levels, points = grid.shape
    pair_dev, row_count, _ = legendre.shape
    width = row_count - 1
    unit = 4 * group
    groups = -(-pair_dev // group)
    band = lax.axis_index("lat")
    owner = band * group + lax.axis_index("lev")
    planes = 4 if lat_groups % 8 == 0 else 2
    rows_of = lat_groups // planes
    plane = rows_of * group
    z = jnp.asarray(band // rows_of, jnp.int32)[None]
    shift = z * plane


    bands = jnp.arange(lat_groups, dtype=jnp.int32)
    count = jnp.sum(jnp.where(bands == band, band_counts, 0))
    weights = jnp.broadcast_to((gauss_weights / points)[:, None], (gauss_weights.shape[0], LANES))
    waves = lax.dynamic_slice(pair_m, (owner * pair_dev,), (pair_dev,))

    rows = grid.reshape(fields, cap * levels, points)

    def shifted(blocks, distance):
        if distance == 0:
            return blocks
        pairs = [
            (a * rows_of + y, (a + distance) % planes * rows_of + y)
            for a in range(planes)
            for y in range(rows_of)
        ]
        return lax.ppermute(blocks, "lat", pairs)

    def within_plane(blocks):
        return lax.all_to_all(
            blocks,
            ("lat", "lev"),
            split_axis=0,
            concat_axis=0,
            tiled=True,
            axis_index_groups=[[p * plane + d for d in range(plane)] for p in range(planes)],
        )

    def to_owners(blocks):
        blocks = blocks.reshape((planes, plane) + blocks.shape[1:])
        return within_plane(jnp.stack([shifted(blocks[k], k) for k in range(planes)], axis=1))

    def to_bands(blocks, cuts):
        blocks = within_plane(blocks)
        made = []
        for low, high in cuts:
            came = [shifted(blocks[:, k, :, low:high], k) for k in range(planes)]
            made.append([came[-k % planes] for k in range(planes)])
        return made

    sent = forward_first(rows, pair_m, shift, levels, unit, devices, group, width)
    received = [(0, to_owners(sent))]
    later_m, _ = lax.optimization_barrier((pair_m, sent))
    table = trig_table(later_m, shift, width, points, devices, groups, group)
    dft = functools.partial(
        forward, grid=rows, table=table, levels=levels, unit=unit, devices=devices
    )
    if groups > 1:
        received.append((1, to_owners(dft((0, 1), (1, groups - 1)))))
    others = [to_owners(dft((f, 1), (0, groups))) for f in range(1, fields)]

    step = functools.partial(
        legendre_step,
        legendre=legendre,
        weights=weights,
        counts=band_counts,
        waves=waves,
        z=z,
        group=group,
        groups=groups,
    )
    vorticity = None
    for first, blocks in received:
        (vorticity,) = step(
            "vorticity", first, blocks, levels=diffusion, extra=(), partial=vorticity
        )
    divergence, new_divergence = step(
        "divergence", 0, others[0], levels=mode_depth, extra=(vert_modes,), partial=None
    )
    (temperature,) = step(
        "temperature",
        0,
        others[1],
        levels=diffusion,
        extra=(pressure_balance_matrix, new_divergence),
        partial=None,
    )
    late = max(16, cap // 6 // 16 * 16)
    if late >= cap or (cap - late) % late:
        late = 0
    cuts = [(0, cap - late), (cap - late, cap)] if late else [(0, cap)]
    out = None
    for field, made, pieces in (
        (0, vorticity, [(0, cap)]),
        (1, divergence, [(0, cap)]),
        (2, temperature, cuts),
    ):
        for (low, _), specs in zip(pieces, to_bands(made, pieces)):
            out, _ = inverse(
                field,
                low,
                specs,
                table=table,
                count=count[None],
                partial=out,
                shape=(fields, cap * levels, points),
                levels=levels,
                unit=unit,
            )
    return out.reshape(fields, cap, levels, points)


def solution(mesh):
    placed = (
        P(None, "lat", "lev", None),
        P(("lat", "lev"), None, None),
        P(),
        P(),
        P(),
        P(),
        P(),
        P(),
        P(),
    )
    return jax.shard_map(
        shards, mesh=mesh, in_specs=placed, out_specs=P(None, "lat", "lev", None), check_vma=False
    )
```

```python
import functools
import math

import jax
import jax.numpy as jnp
from jax import lax
from jax.experimental import pallas as pl
from jax.experimental.pallas import tpu as pltpu
from jax.sharding import PartitionSpec as P

LANES = 128
VMEM_LIMIT = 63 * 1024 * 1024


def swap_units(parts, unit):
    lane = lax.broadcasted_iota(jnp.int32, parts[0].shape, 1)
    step = 1
    parts = list(parts)
    while step < len(parts):
        shift = unit * step
        high = (lane & shift) != 0
        for i in range(len(parts)):
            if not i & step:
                a, b = parts[i], parts[i | step]
                parts[i] = jnp.where(high, pltpu.roll(b, shift, 1), a)
                parts[i | step] = jnp.where(high, b, pltpu.roll(a, LANES - shift, 1))
        step *= 2
    return parts


def row_tile(rows, most):
    tile = most
    while rows % tile:
        tile -= 16
    return tile


def ordered_after(value, *others):
    anywhere = pl.BlockSpec(memory_space=pl.ANY)
    return pl.pallas_call(
        lambda *refs: None,
        in_specs=[anywhere] * (1 + len(others)),
        out_specs=anywhere,
        out_shape=jax.ShapeDtypeStruct(value.shape, value.dtype),
        input_output_aliases={0: 0},
        name="ordered_after",
    )(value, *others)


def unit_circle(wave, points):
    lane = lax.broadcasted_iota(jnp.int32, wave.shape, 1).astype(jnp.float32)
    product = wave.astype(jnp.float32) * lane
    rest = product - points * jnp.floor(product * (1.0 / points))
    quarter = jnp.floor(rest * (4.0 / points) + 0.5)
    x = (rest - quarter * (points / 4.0)) * (2.0 * math.pi / points)
    y = x * x
    sine = x * (1 + y * (-1 / 6 + y * (1 / 120 + y * (-1 / 5040 + y * (1 / 362880)))))
    cosine = 1 + y * (-1 / 2 + y * (1 / 24 + y * (-1 / 720 + y * (1 / 40320))))
    odd = jnp.logical_or(quarter == 1, quarter == 3)
    cos_low = jnp.logical_or(quarter == 1, quarter == 2)
    sin_low = jnp.logical_or(quarter == 2, quarter == 3)
    cos_all = jnp.where(odd, sine, cosine)
    sin_all = jnp.where(odd, cosine, sine)
    return jnp.where(cos_low, -cos_all, cos_all), jnp.where(sin_low, -sin_all, sin_all)


def wave_rows(pair_ref, pair_dev, group, width, pair_group, device, parity):
    row = lax.broadcasted_iota(jnp.int32, (2 * group, LANES), 0)
    wave = jnp.full((2 * group, LANES), -1, jnp.int32)
    for b in range(group):
        pair = pair_group * group + b
        lower = pair_ref[device * pair_dev + jnp.minimum(pair, pair_dev - 1)]
        chosen = jnp.where(lower % 2 == parity, lower, width - 1 - lower)
        wave = jnp.where(jnp.logical_and(row % group == b, pair < pair_dev), chosen, wave)
    return wave


def fill_table(table, pair_ref, pair_dev, group, width, points, pair_group, first_device):
    unit = 2 * group
    count = 8 * unit

    @pl.loop(0, table.shape[1] // count)
    def _(n):
        at = pl.ds(pl.multiple_of(n * count, count), count)
        for parity in range(2):
            wave = jnp.concatenate(
                [
                    wave_rows(
                        pair_ref,
                        pair_dev,
                        group,
                        width,
                        pair_group,
                        first_device + n // 2 * 16 + n % 2 * 4 + j % 2 * 8 + j // 2,
                        parity,
                    )
                    for j in range(8)
                ],
                axis=0,
            )
            cos, sin = unit_circle(wave, points)
            cos, sin = jnp.where(wave < 0, 0.0, cos), jnp.where(wave < 0, 0.0, sin)
            half = LANES // 2
            cos_half, sin_half = cos[:, half : half + 1], sin[:, half : half + 1]
            cos_turn = jnp.broadcast_to(cos_half * cos_half - sin_half * sin_half, cos.shape)
            sin_turn = jnp.broadcast_to(2.0 * sin_half * cos_half, cos.shape)
            sine = lax.broadcasted_iota(jnp.int32, cos.shape, 0) // group % 2 == 1
            value, other = jnp.where(sine, -sin, cos), jnp.where(sine, cos, sin)
            for a in range(table.shape[2] // LANES):
                table[parity, at, a * LANES : (a + 1) * LANES] = value.astype(table.dtype)
                value, other = (
                    value * cos_turn - other * sin_turn,
                    other * cos_turn + value * sin_turn,
                )


def table_kernel(pair_dev, group, width, points, wide, pair_ref, table):
    fill_table(
        table, pair_ref, pair_dev, group, width, points, pl.program_id(0), pl.program_id(1) * wide
    )


def devices_at_once(devices):
    return 32 if devices % 32 == 0 else 16


def trig_table(pair_m, width, points, devices, groups, group):
    wide = devices_at_once(devices)
    rows = wide * 2 * group
    steps = devices // wide
    return pl.pallas_call(
        functools.partial(table_kernel, pair_m.shape[0] // devices, group, width, points, wide),
        grid_spec=pltpu.PrefetchScalarGridSpec(
            num_scalar_prefetch=1,
            grid=(groups, steps),
            in_specs=[],
            out_specs=pl.BlockSpec((2, rows, points // 2), lambda i, t, m: (0, i * steps + t, 0)),
        ),
        out_shape=jax.ShapeDtypeStruct((2, groups * steps * rows, points // 2), jnp.bfloat16),
        cost_estimate=pl.CostEstimate(
            flops=8 * groups * steps * rows * points,
            bytes_accessed=2 * groups * steps * rows * points,
            transcendentals=0,
        ),
        name="trig_table",
    )(pair_m)


def fold(lines):
    half = lines.shape[1] // 2
    low, high = lines[:, :half].astype(jnp.float32), lines[:, half:].astype(jnp.float32)
    return (low + high).astype(jnp.bfloat16), (low - high).astype(jnp.bfloat16)


def emit_blocks(folded, table, scratch, store, tile, levels, unit):
    for parity in range(2):
        values = lax.dot_general(
            folded[parity], table[parity], (((1,), (1,)), ((), ())),
            preferred_element_type=jnp.float32,
        )
        for n in range(values.shape[1] // LANES):
            scratch[parity, n] = values[:, n * LANES : (n + 1) * LANES]
    for n in range(scratch.shape[1]):
        by_level = [
            swap_units(
                [scratch[parity, n, pl.ds(l, tile, stride=levels), :] for parity in range(2)],
                unit // 2,
            )
            for l in range(levels)
        ]
        for b in range(2):
            for a, part in enumerate(swap_units([x[b] for x in by_level], unit)):
                store(n * 2 * levels + b * levels + a, part.astype(jnp.bfloat16))


def forward_kernel(levels, unit, some, grid_ref, table_ref, out_ref, folded, scratch):
    cap = grid_ref.shape[1] // levels
    tile = row_tile(cap, 32)

    @pl.when(jnp.logical_and(pl.program_id(0) % some == 0, pl.program_id(1) == 0))
    def _():
        for s in range(0, cap, tile):
            lines = slice(s * levels, (s + tile) * levels)
            folded[0, lines, :], folded[1, lines, :] = fold(grid_ref[0, lines, :])

    tables = [table_ref[0], table_ref[1]]
    for s in range(0, cap, tile):
        lines = slice(s * levels, (s + tile) * levels)

        def store(d, block, s=s):
            out_ref[d, 0, s : s + tile, :] = block

        emit_blocks(
            [folded[0, lines, :], folded[1, lines, :]],
            tables,
            scratch.at[s // tile],
            store,
            tile,
            levels,
            unit,
        )


def forward(fields, groups, grid, table, levels, unit, devices):
    _, rows, points = grid.shape
    cap = rows // levels
    tile = row_tile(cap, 32)
    wide = devices_at_once(devices)
    steps = devices // wide
    (first_field, some_fields), (first, some) = fields, groups
    count = some_fields * some
    columns = count * devices * unit
    half = wide * unit // 2
    return pl.pallas_call(
        functools.partial(forward_kernel, levels, unit, some),
        grid=(count, steps),
        in_specs=[
            pl.BlockSpec((1, rows, points), lambda i, t: (first_field + i // some, 0, 0)),
            pl.BlockSpec(
                (2, half, points // 2), lambda i, t: (0, (first + i % some) * steps + t, 0)
            ),
        ],
        out_specs=pl.BlockSpec((wide, 1, cap, LANES), lambda i, t: (t, i, 0, 0)),
        out_shape=jax.ShapeDtypeStruct((devices, count, cap, LANES), jnp.bfloat16),
        scratch_shapes=[
            pltpu.VMEM((2, rows, points // 2), jnp.bfloat16),
            pltpu.VMEM((cap // tile, 2, half // LANES, tile * levels, LANES), jnp.float32),
        ],
        compiler_params=pltpu.CompilerParams(vmem_limit_bytes=VMEM_LIMIT),
        cost_estimate=pl.CostEstimate(
            flops=rows * points * columns,
            bytes_accessed=2 * (some_fields * rows * points + rows * columns),
            transcendentals=0,
        ),
        name="forward_dft",
    )(grid, table)


def first_kernel(levels, unit, pair_dev, group, width, pair_ref, grid_ref, out_ref, table, scratch):
    @pl.when(pl.program_id(0) == 0)
    def _():
        fill_table(table, pair_ref, pair_dev, group, width, grid_ref.shape[2], 0, 0)

    tile = grid_ref.shape[1] // levels
    half = scratch.shape[2] * LANES
    folded = fold(grid_ref[0])
    for n in range(table.shape[1] // half):

        def store(d, block, n=n):
            out_ref[n * 2 * half // unit + d, 0] = block

        rows = slice(n * half, (n + 1) * half)
        emit_blocks(
            folded,
            [table[0, rows, :], table[1, rows, :]],
            scratch.at[n],
            store,
            tile,
            levels,
            unit,
        )


def forward_first(grid, pair_m, levels, unit, devices, group, width):
    _, rows, points = grid.shape
    cap = rows // levels
    tile = row_tile(cap, 32)
    columns = devices * unit
    half = devices_at_once(devices) * unit // 2
    return pl.pallas_call(
        functools.partial(first_kernel, levels, unit, pair_m.shape[0] // devices, group, width),
        grid_spec=pltpu.PrefetchScalarGridSpec(
            num_scalar_prefetch=1,
            grid=(cap // tile,),
            in_specs=[pl.BlockSpec((1, tile * levels, points), lambda t, m: (0, t, 0))],
            out_specs=pl.BlockSpec((devices, 1, tile, LANES), lambda t, m: (0, 0, t, 0)),
            scratch_shapes=[
                pltpu.VMEM((2, columns // 2, points // 2), jnp.bfloat16),
                pltpu.VMEM(
                    (columns // 2 // half, 2, half // LANES, tile * levels, LANES), jnp.float32
                ),
            ],
        ),
        out_shape=jax.ShapeDtypeStruct((devices, 1, cap, LANES), jnp.bfloat16),
        compiler_params=pltpu.CompilerParams(vmem_limit_bytes=VMEM_LIMIT),
        cost_estimate=pl.CostEstimate(
            flops=rows * points * columns,
            bytes_accessed=2 * rows * (points + columns),
            transcendentals=0,
        ),
        name="forward_first",
    )(pair_m, grid)


def inverse_kernel(levels, unit, groups, first_row, count_ref, *refs):
    spec_refs, table_ref = refs[:groups], refs[groups]
    out_ref, token_ref, turned = refs[-3:]
    devices, rows, _ = spec_refs[0].shape
    tile = row_tile(rows, 32)
    blocks = [(i, d) for i in range(groups) for d in range(0, devices, 2 * levels)]
    base = first_row + pl.program_id(0) * rows
    half = out_ref.shape[2] // 2
    for s in range(0, rows, tile):
        lines = pl.ds(s * levels, tile * levels)
        for n, (i, d) in enumerate(blocks):
            by_level = [
                swap_units(
                    [
                        spec_refs[i][d + b * levels + a, s : s + tile, :].astype(jnp.float32)
                        for a in range(levels)
                    ],
                    unit,
                )
                for b in range(2)
            ]
            for l in range(levels):
                parts = swap_units([by_level[0][l], by_level[1][l]], unit // 2)
                for parity in range(2):
                    turned[parity, n, pl.ds(s * levels + l, tile, stride=levels), :] = parts[parity]
        row = lax.broadcasted_iota(jnp.int32, (tile * levels, LANES), 0)
        valid = row < (count_ref[0] - base - s) * levels
        even, odd = [
            jnp.dot(
                jnp.concatenate(
                    [
                        jnp.where(valid, turned[parity, n, lines, :], 0.0).astype(jnp.bfloat16)
                        for n in range(len(blocks))
                    ],
                    axis=1,
                ),
                table_ref[parity],
                preferred_element_type=jnp.float32,
            )
            for parity in range(2)
        ]
        out_ref[0, lines, :half] = (even + odd).astype(out_ref.dtype)
        out_ref[0, lines, half:] = (even - odd).astype(out_ref.dtype)
    token_ref[...] = jnp.zeros_like(token_ref)


def inverse(field, first_row, size, spec, offset, groups, table, count, partial, shape, levels, unit):
    devices = spec.shape[0]
    columns, points = 2 * table.shape[1], 2 * table.shape[2]
    tile = row_tile(size, 64 if size % 64 == 0 and offset % 64 == 0 else 32)
    if size <= 64:
        tile = row_tile(size, 32)
    rows = tile * levels

    def part(i):
        return pl.BlockSpec(
            (devices, tile, LANES), lambda t, c: (0, (offset + i * size) // tile + t, 0)
        )

    in_specs = [part(i) for i in range(groups)]
    in_specs.append(pl.BlockSpec(table.shape, lambda t, c: (0, 0, 0)))
    operands = [spec] * groups + [table]
    if partial is not None:
        in_specs.append(pl.BlockSpec(memory_space=pl.ANY))
        operands.append(partial)
    return pl.pallas_call(
        functools.partial(inverse_kernel, levels, unit, groups, first_row),
        grid_spec=pltpu.PrefetchScalarGridSpec(
            num_scalar_prefetch=1,
            grid=(size // tile,),
            in_specs=in_specs,
            out_specs=[
                pl.BlockSpec((1, rows, points), lambda t, c: (field, first_row // tile + t, 0)),
                pl.BlockSpec((8, LANES), lambda t, c: (0, 0)),
            ],
            scratch_shapes=[pltpu.VMEM((2, columns // 2 // LANES, rows, LANES), jnp.float32)],
        ),
        out_shape=[
            jax.ShapeDtypeStruct(shape, jnp.bfloat16),
            jax.ShapeDtypeStruct((8, LANES), jnp.float32),
        ],
        input_output_aliases={} if partial is None else {groups + 2: 0},
        compiler_params=pltpu.CompilerParams(vmem_limit_bytes=VMEM_LIMIT),
        cost_estimate=pl.CostEstimate(
            flops=size * levels * points * columns,
            bytes_accessed=2 * size * levels * (points + columns) + columns * points,
            transcendentals=0,
        ),
        name="inverse_dft",
    )(count, *operands)


def lane_levels(levels, group):
    lane = lax.broadcasted_iota(jnp.int32, (LANES, levels * group), 0)
    level = lax.broadcasted_iota(jnp.int32, (LANES, levels * group), 1)
    held = lane % group * levels + lane // (4 * group)
    return (held == level).astype(jnp.float32)


def exact_dot(a, b, dims=((1,), (0,))):
    return lax.dot_general(
        a, b, (dims, ((), ())), precision=lax.Precision.HIGHEST, preferred_element_type=jnp.float32
    )


def lane_matrix(matrix, levels, group):
    chosen = lane_levels(levels, group)
    spread = exact_dot(exact_dot(chosen, matrix), chosen, ((1,), (1,)))
    row = lax.broadcasted_iota(jnp.int32, spread.shape, 0)
    lane = lax.broadcasted_iota(jnp.int32, spread.shape, 1)
    return jnp.where(row // group % 4 == lane // group % 4, spread, 0.0)


def legendre_kernel(
    kind, first, pair_dev, lat_groups, group, outs, counts_ref, waves_ref, recv_ref, leg_ref, *rest
):
    weight_ref, rest = rest[0], rest[1:]
    gathered, made = rest[-2:]
    rest, out_refs = rest[:-2], rest[-2 - outs : -2]
    level_ref = rest[0]
    if kind == "divergence":
        modes_ref, div_out = rest[1], out_refs[-1]
        out_refs = out_refs[:-1]
    if kind == "temperature":
        balance_ref, div_in = rest[1:3]
    levels = level_ref.shape[1] // group
    row_count, lat_total = leg_ref.shape[1:]
    width = row_count - 1
    cap = recv_ref.shape[2]
    member = pl.program_id(1)
    pair = (first + pl.program_id(0)) * group + member

    @pl.when(member == 0)
    def _():
        start = 0
        for g in range(lat_groups):
            parts = [recv_ref[g * group + h, 0].astype(jnp.float32) for h in range(group)]
            for b, part in enumerate(swap_units(parts, 1)):
                gathered[b, pl.ds(start, cap), :] = part
            start = start + counts_ref[g]

    @pl.when(pair < pair_dev)
    def _():
        wave = waves_ref[pair]
        coeffs = (gathered[member, :lat_total, :] * weight_ref[...]).astype(jnp.bfloat16)
        main = leg_ref[0, :width, :]
        last = jnp.broadcast_to(leg_ref[0, width:, :], (16, lat_total))
        spectral = jnp.concatenate(
            [
                jnp.dot(main, coeffs, preferred_element_type=jnp.float32),
                jnp.dot(last, coeffs, preferred_element_type=jnp.float32),
            ],
            axis=0,
        )
        shape = spectral.shape
        row = lax.broadcasted_iota(jnp.int32, shape, 0)
        lane = lax.broadcasted_iota(jnp.int32, shape, 1)
        own = row < width - wave
        upper = lane // (2 * group) % 2 != wave % 2
        keep = jnp.logical_and(jnp.logical_xor(own, upper), row < row_count)
        degree = jnp.where(own, row + wave, row - 1)
        ratio = (degree * (degree + 1)).astype(jnp.float32) / float(width * (width - 1))
        spectral = jnp.where(keep, spectral, 0.0)
        if kind != "temperature":
            per_level = jnp.broadcast_to(level_ref[...], (8, level_ref.shape[1]))
            per_lane = exact_dot(per_level, lane_levels(levels, group), ((1,), (1,)))[:1]
        if kind == "vorticity":
            new = spectral / (1.0 + per_lane * ratio * ratio)
        elif kind == "divergence":
            modes_matrix = lane_matrix(modes_ref[...], levels, group)
            modes = exact_dot(spectral, modes_matrix, ((1,), (1,)))
            modes = modes / (1.0 + per_lane * ratio)
            new = exact_dot(modes, modes_matrix)
            div_out[0] = new
        else:
            balance = lane_matrix(balance_ref[...], levels, group)
            new = spectral - exact_dot(div_in[0], balance, ((1,), (1,)))
        zonal = jnp.logical_and(wave == 0, jnp.logical_not(upper))
        new = new * jnp.where(zonal, 1.0, 2.0)
        tail = jnp.concatenate(
            [new[width:], jnp.zeros((LANES - 16, LANES), jnp.float32)], axis=0
        )
        turned = jnp.dot(
            new[:width].T.astype(jnp.bfloat16), main, preferred_element_type=jnp.float32
        )
        turned += jnp.dot(
            tail.T.astype(jnp.bfloat16),
            jnp.broadcast_to(leg_ref[0, width:, :], (LANES, lat_total)),
            preferred_element_type=jnp.float32,
        )
        made[member, :lat_total, :] = turned.T
        made[member, lat_total:, :] = jnp.zeros((cap, LANES), jnp.float32)

    @pl.when(pair >= pair_dev)
    def _():
        made[member] = jnp.zeros(made.shape[1:], jnp.float32)

    @pl.when(member == group - 1)
    def _():
        start = 0
        for g in range(lat_groups):
            parts = [made[b, pl.ds(start, cap), :] for b in range(group)]
            for h, part in enumerate(swap_units(parts, 1)):
                row = 0
                for out_ref in out_refs:
                    size = out_ref.shape[1]
                    out_ref[g * group + h] = part[row : row + size].astype(jnp.bfloat16)
                    row += size
            start = start + counts_ref[g]


def legendre_step(
    kind, first, some, source, received, targets, legendre, weights, counts, waves, levels, extra, group, partial
):
    devices, _, cap, _ = received.shape
    pair_dev, row_count, lat_total = legendre.shape
    lat_groups = devices // group

    def at_pair(i, b, *_):
        return (jnp.minimum((first + i) * group + b, pair_dev - 1), 0, 0)

    def whole(i, b, *_):
        return (0, 0)

    def blocks(size, offset):
        return pl.BlockSpec(
            (devices, size, LANES), lambda i, b, *_: (0, offset // size + first + i, 0)
        )

    square = pl.BlockSpec(extra[0].shape, whole) if extra else None
    div_block = pl.BlockSpec((1, row_count + 15, LANES), at_pair)
    in_specs = [
        pl.BlockSpec((devices, 1, cap, LANES), lambda i, b, *_: (0, source + i, 0, 0)),
        pl.BlockSpec((1, row_count, lat_total), at_pair),
        pl.BlockSpec((lat_total, LANES), whole),
        pl.BlockSpec((1, levels.shape[0]), whole),
    ]
    out_specs = [blocks(size, offset) for size, offset, _ in targets]
    out_shape = [
        jax.ShapeDtypeStruct((devices, total, LANES), jnp.bfloat16) for _, _, total in targets
    ]
    if kind == "divergence":
        in_specs.append(square)
        out_specs.append(div_block)
        out_shape.append(jax.ShapeDtypeStruct((pair_dev, row_count + 15, LANES), jnp.float32))
    elif kind == "temperature":
        in_specs += [square, div_block]
    operands = [counts, waves, received, legendre, weights, levels[None, :], *extra]
    aliases = {}
    if partial is not None:
        aliases = {len(operands): 0}
        in_specs.append(pl.BlockSpec(memory_space=pl.ANY))
        operands.append(partial)
    held = pltpu.VMEM((group, lat_total + cap, LANES), jnp.float32)
    return pl.pallas_call(
        functools.partial(
            legendre_kernel, kind, first, pair_dev, lat_groups, group, len(out_specs)
        ),
        grid_spec=pltpu.PrefetchScalarGridSpec(
            num_scalar_prefetch=2,
            grid=(some, group),
            in_specs=in_specs,
            out_specs=out_specs,
            scratch_shapes=[held, held],
        ),
        out_shape=out_shape,
        input_output_aliases=aliases,
        compiler_params=pltpu.CompilerParams(vmem_limit_bytes=VMEM_LIMIT),
        cost_estimate=pl.CostEstimate(
            flops=8 * some * group * row_count * lat_total * LANES,
            bytes_accessed=2 * some * (group * row_count * lat_total + 2 * devices * cap * LANES),
            transcendentals=0,
        ),
        name="legendre_" + kind,
    )(*operands)


def shards(
    grid,
    legendre,
    gauss_weights,
    band_counts,
    pair_m,
    vert_modes,
    mode_depth,
    diffusion,
    pressure_balance_matrix,
):
    lat_groups = lax.axis_size("lat")
    group = lax.axis_size("lev")
    devices = lat_groups * group
    fields, cap, levels, points = grid.shape
    pair_dev, row_count, _ = legendre.shape
    width = row_count - 1
    unit = 4 * group
    groups = -(-pair_dev // group)
    band = lax.axis_index("lat")
    owner = band * group + lax.axis_index("lev")


    bands = jnp.arange(lat_groups, dtype=jnp.int32)
    count = jnp.sum(jnp.where(bands == band, band_counts, 0))
    weights = jnp.broadcast_to((gauss_weights / points)[:, None], (gauss_weights.shape[0], LANES))
    waves = lax.dynamic_slice(pair_m, (owner * pair_dev,), (pair_dev,))

    rows = grid.reshape(fields, cap * levels, points)

    def exchange(blocks):
        return lax.all_to_all(
            blocks, ("lat", "lev"), split_axis=0, concat_axis=0, tiled=True
        )

    sent = forward_first(rows, pair_m, levels, unit, devices, group, width)
    received = [(0, 1, exchange(sent))]
    later_m, _ = lax.optimization_barrier((pair_m, sent))
    table = trig_table(later_m, width, points, devices, groups, group)
    dft = functools.partial(
        forward, grid=rows, table=table, levels=levels, unit=unit, devices=devices
    )
    if groups > 1:
        sent = dft((0, 1), (1, groups - 1))
        received.append((1, groups - 1, exchange(sent)))
    others = exchange(dft((1, fields - 1), (0, groups)))

    step = functools.partial(
        legendre_step,
        legendre=legendre,
        weights=weights,
        counts=band_counts,
        waves=waves,
        group=group,
    )
    vorticity = None
    for first, some, blocks in received:
        (vorticity,) = step(
            "vorticity",
            first,
            some,
            0,
            blocks,
            targets=[(cap, 0, groups * cap)],
            levels=diffusion,
            extra=(),
            partial=vorticity,
        )
    vorticity = exchange(ordered_after(vorticity, others))
    late = max(16, cap // 3 // 16 * 16)
    if late >= cap or groups * (cap - late) % cap or (cap - late) % late:
        late = 0
    main, offset = cap - late, groups * (cap - late)
    total = offset + groups * cap
    back, new_divergence = step(
        "divergence",
        0,
        groups,
        0,
        others,
        targets=[(cap, offset, total)],
        levels=mode_depth,
        extra=(vert_modes,),
        partial=None,
    )
    targets = [(main, 0, total)] + ([(late, 0, groups * late)] if late else [])
    back, *rest = step(
        "temperature",
        0,
        groups,
        groups,
        others,
        targets=targets,
        levels=diffusion,
        extra=(pressure_balance_matrix, new_divergence),
        partial=back,
    )
    to_grid = functools.partial(
        inverse,
        groups=groups,
        table=table,
        count=count[None],
        shape=(fields, cap * levels, points),
        levels=levels,
        unit=unit,
    )
    out, token = to_grid(0, 0, cap, vorticity, 0, partial=None)
    back = exchange(back)
    if late:
        last = exchange(ordered_after(rest[0], back, token))
    out, _ = to_grid(1, 0, cap, back, offset, partial=out)
    out, _ = to_grid(2, 0, main, back, 0, partial=out)
    if late:
        out, _ = to_grid(2, main, late, last, 0, partial=out)
    return out.reshape(fields, cap, levels, points)


def solution(mesh):
    placed = (
        P(None, "lat", "lev", None),
        P(("lat", "lev"), None, None),
        P(),
        P(),
        P(),
        P(),
        P(),
        P(),
        P(),
    )
    return jax.shard_map(
        shards, mesh=mesh, in_specs=placed, out_specs=P(None, "lat", "lev", None), check_vma=False
    )
```

```python
import functools
import math

import jax
import jax.numpy as jnp
from jax import lax
from jax.experimental import pallas as pl
from jax.experimental.pallas import tpu as pltpu
from jax.sharding import PartitionSpec as P

LANES = 128
VMEM_LIMIT = 63 * 1024 * 1024


def swap_units(parts, unit):
    lane = lax.broadcasted_iota(jnp.int32, parts[0].shape, 1)
    step = 1
    parts = list(parts)
    while step < len(parts):
        shift = unit * step
        high = (lane & shift) != 0
        for i in range(len(parts)):
            if not i & step:
                a, b = parts[i], parts[i | step]
                parts[i] = jnp.where(high, pltpu.roll(b, shift, 1), a)
                parts[i | step] = jnp.where(high, b, pltpu.roll(a, LANES - shift, 1))
        step *= 2
    return parts


def row_tile(rows, most):
    tile = most
    while rows % tile:
        tile -= 16
    return tile


def ordered_after(value, *others):
    anywhere = pl.BlockSpec(memory_space=pl.ANY)
    return pl.pallas_call(
        lambda *refs: None,
        in_specs=[anywhere] * (1 + len(others)),
        out_specs=anywhere,
        out_shape=jax.ShapeDtypeStruct(value.shape, value.dtype),
        input_output_aliases={0: 0},
        name="ordered_after",
    )(value, *others)


def unit_circle(wave, points):
    lane = lax.broadcasted_iota(jnp.int32, wave.shape, 1).astype(jnp.float32)
    product = wave.astype(jnp.float32) * lane
    rest = product - points * jnp.floor(product * (1.0 / points))
    quarter = jnp.floor(rest * (4.0 / points) + 0.5)
    x = (rest - quarter * (points / 4.0)) * (2.0 * math.pi / points)
    y = x * x
    sine = x * (1 + y * (-1 / 6 + y * (1 / 120 + y * (-1 / 5040 + y * (1 / 362880)))))
    cosine = 1 + y * (-1 / 2 + y * (1 / 24 + y * (-1 / 720 + y * (1 / 40320))))
    odd = jnp.logical_or(quarter == 1, quarter == 3)
    cos_low = jnp.logical_or(quarter == 1, quarter == 2)
    sin_low = jnp.logical_or(quarter == 2, quarter == 3)
    cos_all = jnp.where(odd, sine, cosine)
    sin_all = jnp.where(odd, cosine, sine)
    return jnp.where(cos_low, -cos_all, cos_all), jnp.where(sin_low, -sin_all, sin_all)


def wave_rows(pair_ref, pair_dev, group, width, pair_group, device, parity):
    row = lax.broadcasted_iota(jnp.int32, (2 * group, LANES), 0)
    wave = jnp.full((2 * group, LANES), -1, jnp.int32)
    for b in range(group):
        pair = pair_group * group + b
        lower = pair_ref[device * pair_dev + jnp.minimum(pair, pair_dev - 1)]
        chosen = jnp.where(lower % 2 == parity, lower, width - 1 - lower)
        wave = jnp.where(jnp.logical_and(row % group == b, pair < pair_dev), chosen, wave)
    return wave


def fill_table(table, pair_ref, pair_dev, group, width, points, pair_group, first_device):
    unit = 2 * group
    count = 8 * unit

    @pl.loop(0, table.shape[1] // count)
    def _(n):
        at = pl.ds(pl.multiple_of(n * count, count), count)
        for parity in range(2):
            wave = jnp.concatenate(
                [
                    wave_rows(
                        pair_ref,
                        pair_dev,
                        group,
                        width,
                        pair_group,
                        first_device + n // 2 * 16 + n % 2 * 4 + j % 2 * 8 + j // 2,
                        parity,
                    )
                    for j in range(8)
                ],
                axis=0,
            )
            cos, sin = unit_circle(wave, points)
            cos, sin = jnp.where(wave < 0, 0.0, cos), jnp.where(wave < 0, 0.0, sin)
            half = LANES // 2
            cos_half, sin_half = cos[:, half : half + 1], sin[:, half : half + 1]
            cos_turn = jnp.broadcast_to(cos_half * cos_half - sin_half * sin_half, cos.shape)
            sin_turn = jnp.broadcast_to(2.0 * sin_half * cos_half, cos.shape)
            sine = lax.broadcasted_iota(jnp.int32, cos.shape, 0) // group % 2 == 1
            value, other = jnp.where(sine, -sin, cos), jnp.where(sine, cos, sin)
            for a in range(table.shape[2] // LANES):
                table[parity, at, a * LANES : (a + 1) * LANES] = value.astype(table.dtype)
                value, other = (
                    value * cos_turn - other * sin_turn,
                    other * cos_turn + value * sin_turn,
                )


def table_kernel(pair_dev, group, width, points, wide, pair_ref, table):
    fill_table(
        table, pair_ref, pair_dev, group, width, points, pl.program_id(0), pl.program_id(1) * wide
    )


def devices_at_once(devices):
    return 32 if devices % 32 == 0 else 16


def trig_table(pair_m, width, points, devices, groups, group):
    wide = devices_at_once(devices)
    rows = wide * 2 * group
    steps = devices // wide
    return pl.pallas_call(
        functools.partial(table_kernel, pair_m.shape[0] // devices, group, width, points, wide),
        grid_spec=pltpu.PrefetchScalarGridSpec(
            num_scalar_prefetch=1,
            grid=(groups, steps),
            in_specs=[],
            out_specs=pl.BlockSpec((2, rows, points // 2), lambda i, t, m: (0, i * steps + t, 0)),
        ),
        out_shape=jax.ShapeDtypeStruct((2, groups * steps * rows, points // 2), jnp.bfloat16),
        cost_estimate=pl.CostEstimate(
            flops=8 * groups * steps * rows * points,
            bytes_accessed=2 * groups * steps * rows * points,
            transcendentals=0,
        ),
        name="trig_table",
    )(pair_m)


def fold(lines):
    half = lines.shape[1] // 2
    low, high = lines[:, :half], lines[:, half:]
    return low + high, low - high


def emit_blocks(folded, table, scratch, store, tile, levels, unit):
    for parity in range(2):
        values = lax.dot_general(
            folded[parity], table[parity], (((1,), (1,)), ((), ())),
            preferred_element_type=jnp.float32,
        )
        for n in range(values.shape[1] // LANES):
            scratch[parity, n] = values[:, n * LANES : (n + 1) * LANES]
    for n in range(scratch.shape[1]):
        by_level = [
            swap_units(
                [
                    scratch[parity, n, pl.ds(l, tile, stride=levels), :].astype(jnp.bfloat16)
                    for parity in range(2)
                ],
                unit // 2,
            )
            for l in range(levels)
        ]
        for b in range(2):
            for a, part in enumerate(swap_units([x[b] for x in by_level], unit)):
                store(n * 2 * levels + b * levels + a, part)


def forward_kernel(levels, unit, some, grid_ref, table_ref, out_ref, folded, scratch):
    cap = grid_ref.shape[1] // levels
    tile = row_tile(cap, 32)

    @pl.when(jnp.logical_and(pl.program_id(0) % some == 0, pl.program_id(1) == 0))
    def _():
        for s in range(0, cap, tile):
            lines = slice(s * levels, (s + tile) * levels)
            folded[0, lines, :], folded[1, lines, :] = fold(grid_ref[0, lines, :])

    tables = [table_ref[0], table_ref[1]]
    for s in range(0, cap, tile):
        lines = slice(s * levels, (s + tile) * levels)

        def store(d, block, s=s):
            out_ref[d, 0, s : s + tile, :] = block

        emit_blocks(
            [folded[0, lines, :], folded[1, lines, :]],
            tables,
            scratch.at[s // tile],
            store,
            tile,
            levels,
            unit,
        )


def forward(fields, groups, grid, table, levels, unit, devices):
    _, rows, points = grid.shape
    cap = rows // levels
    tile = row_tile(cap, 32)
    wide = devices_at_once(devices)
    steps = devices // wide
    (first_field, some_fields), (first, some) = fields, groups
    count = some_fields * some
    columns = count * devices * unit
    half = wide * unit // 2
    return pl.pallas_call(
        functools.partial(forward_kernel, levels, unit, some),
        grid=(count, steps),
        in_specs=[
            pl.BlockSpec((1, rows, points), lambda i, t: (first_field + i // some, 0, 0)),
            pl.BlockSpec(
                (2, half, points // 2), lambda i, t: (0, (first + i % some) * steps + t, 0)
            ),
        ],
        out_specs=pl.BlockSpec((wide, 1, cap, LANES), lambda i, t: (t, i, 0, 0)),
        out_shape=jax.ShapeDtypeStruct((devices, count, cap, LANES), jnp.bfloat16),
        scratch_shapes=[
            pltpu.VMEM((2, rows, points // 2), jnp.bfloat16),
            pltpu.VMEM((cap // tile, 2, half // LANES, tile * levels, LANES), jnp.float32),
        ],
        compiler_params=pltpu.CompilerParams(vmem_limit_bytes=VMEM_LIMIT),
        cost_estimate=pl.CostEstimate(
            flops=rows * points * columns,
            bytes_accessed=2 * (some_fields * rows * points + rows * columns),
            transcendentals=0,
        ),
        name="forward_dft",
    )(grid, table)


def first_kernel(levels, unit, pair_dev, group, width, pair_ref, grid_ref, out_ref, table, scratch):
    @pl.when(pl.program_id(0) == 0)
    def _():
        fill_table(table, pair_ref, pair_dev, group, width, grid_ref.shape[2], 0, 0)

    tile = grid_ref.shape[1] // levels
    half = scratch.shape[2] * LANES
    folded = fold(grid_ref[0])
    for n in range(table.shape[1] // half):

        def store(d, block, n=n):
            out_ref[n * 2 * half // unit + d, 0] = block

        rows = slice(n * half, (n + 1) * half)
        emit_blocks(
            folded,
            [table[0, rows, :], table[1, rows, :]],
            scratch.at[n],
            store,
            tile,
            levels,
            unit,
        )


def forward_first(grid, pair_m, levels, unit, devices, group, width):
    _, rows, points = grid.shape
    cap = rows // levels
    tile = row_tile(cap, 32)
    columns = devices * unit
    half = devices_at_once(devices) * unit // 2
    return pl.pallas_call(
        functools.partial(first_kernel, levels, unit, pair_m.shape[0] // devices, group, width),
        grid_spec=pltpu.PrefetchScalarGridSpec(
            num_scalar_prefetch=1,
            grid=(cap // tile,),
            in_specs=[pl.BlockSpec((1, tile * levels, points), lambda t, m: (0, t, 0))],
            out_specs=pl.BlockSpec((devices, 1, tile, LANES), lambda t, m: (0, 0, t, 0)),
            scratch_shapes=[
                pltpu.VMEM((2, columns // 2, points // 2), jnp.bfloat16),
                pltpu.VMEM(
                    (columns // 2 // half, 2, half // LANES, tile * levels, LANES), jnp.float32
                ),
            ],
        ),
        out_shape=jax.ShapeDtypeStruct((devices, 1, cap, LANES), jnp.bfloat16),
        compiler_params=pltpu.CompilerParams(vmem_limit_bytes=VMEM_LIMIT),
        cost_estimate=pl.CostEstimate(
            flops=rows * points * columns,
            bytes_accessed=2 * rows * (points + columns),
            transcendentals=0,
        ),
        name="forward_first",
    )(pair_m, grid)


def inverse_kernel(levels, unit, groups, first_row, count_ref, *refs):
    spec_refs, table_ref = refs[:groups], refs[groups]
    out_ref, token_ref, turned = refs[-3:]
    devices, rows, _ = spec_refs[0].shape
    tile = row_tile(rows, 32)
    blocks = [(i, d) for i in range(groups) for d in range(0, devices, 2 * levels)]
    base = first_row + pl.program_id(0) * rows
    half = out_ref.shape[2] // 2
    for s in range(0, rows, tile):
        lines = pl.ds(s * levels, tile * levels)
        for n, (i, d) in enumerate(blocks):
            by_level = [
                swap_units(
                    [
                        spec_refs[i][d + b * levels + a, s : s + tile, :]
                        for a in range(levels)
                    ],
                    unit,
                )
                for b in range(2)
            ]
            for l in range(levels):
                parts = swap_units([by_level[0][l], by_level[1][l]], unit // 2)
                for parity in range(2):
                    turned[parity, n, pl.ds(s * levels + l, tile, stride=levels), :] = parts[
                        parity
                    ].astype(jnp.float32)
        row = lax.broadcasted_iota(jnp.int32, (tile * levels, LANES), 0)
        valid = row < (count_ref[0] - base - s) * levels
        even, odd = [
            jnp.dot(
                jnp.concatenate(
                    [
                        jnp.where(valid, turned[parity, n, lines, :], 0.0).astype(jnp.bfloat16)
                        for n in range(len(blocks))
                    ],
                    axis=1,
                ),
                table_ref[parity],
                preferred_element_type=jnp.float32,
            )
            for parity in range(2)
        ]
        out_ref[0, lines, :half] = (even + odd).astype(out_ref.dtype)
        out_ref[0, lines, half:] = (even - odd).astype(out_ref.dtype)
    token_ref[...] = jnp.zeros_like(token_ref)


def inverse(field, first_row, size, spec, offset, groups, table, count, partial, shape, levels, unit):
    devices = spec.shape[0]
    columns, points = 2 * table.shape[1], 2 * table.shape[2]
    tile = row_tile(size, 64 if size % 64 == 0 and offset % 64 == 0 else 32)
    if size <= 64:
        tile = row_tile(size, 32)
    rows = tile * levels

    def part(i):
        return pl.BlockSpec(
            (devices, tile, LANES), lambda t, c: (0, (offset + i * size) // tile + t, 0)
        )

    in_specs = [part(i) for i in range(groups)]
    in_specs.append(pl.BlockSpec(table.shape, lambda t, c: (0, 0, 0)))
    operands = [spec] * groups + [table]
    if partial is not None:
        in_specs.append(pl.BlockSpec(memory_space=pl.ANY))
        operands.append(partial)
    return pl.pallas_call(
        functools.partial(inverse_kernel, levels, unit, groups, first_row),
        grid_spec=pltpu.PrefetchScalarGridSpec(
            num_scalar_prefetch=1,
            grid=(size // tile,),
            in_specs=in_specs,
            out_specs=[
                pl.BlockSpec((1, rows, points), lambda t, c: (field, first_row // tile + t, 0)),
                pl.BlockSpec((8, LANES), lambda t, c: (0, 0)),
            ],
            scratch_shapes=[pltpu.VMEM((2, columns // 2 // LANES, rows, LANES), jnp.float32)],
        ),
        out_shape=[
            jax.ShapeDtypeStruct(shape, jnp.bfloat16),
            jax.ShapeDtypeStruct((8, LANES), jnp.float32),
        ],
        input_output_aliases={} if partial is None else {groups + 2: 0},
        compiler_params=pltpu.CompilerParams(vmem_limit_bytes=VMEM_LIMIT),
        cost_estimate=pl.CostEstimate(
            flops=size * levels * points * columns,
            bytes_accessed=2 * size * levels * (points + columns) + columns * points,
            transcendentals=0,
        ),
        name="inverse_dft",
    )(count, *operands)


def lane_levels(levels, group):
    lane = lax.broadcasted_iota(jnp.int32, (LANES, levels * group), 0)
    level = lax.broadcasted_iota(jnp.int32, (LANES, levels * group), 1)
    held = lane % group * levels + lane // (4 * group)
    return (held == level).astype(jnp.float32)


def exact_dot(a, b, dims=((1,), (0,))):
    return lax.dot_general(
        a, b, (dims, ((), ())), precision=lax.Precision.HIGHEST, preferred_element_type=jnp.float32
    )


def lane_matrix(matrix, levels, group):
    chosen = lane_levels(levels, group)
    spread = exact_dot(exact_dot(chosen, matrix), chosen, ((1,), (1,)))
    row = lax.broadcasted_iota(jnp.int32, spread.shape, 0)
    lane = lax.broadcasted_iota(jnp.int32, spread.shape, 1)
    return jnp.where(row // group % 4 == lane // group % 4, spread, 0.0)


def legendre_kernel(
    kind, first, pair_dev, lat_groups, group, outs, counts_ref, waves_ref, recv_ref, leg_ref, *rest
):
    weight_ref, rest = rest[0], rest[1:]
    gathered, made = rest[-2:]
    rest, out_refs = rest[:-2], rest[-2 - outs : -2]
    level_ref = rest[0]
    if kind == "divergence":
        modes_ref, div_out = rest[1], out_refs[-1]
        out_refs = out_refs[:-1]
    if kind == "temperature":
        balance_ref, div_in = rest[1:3]
    levels = level_ref.shape[1] // group
    row_count, lat_total = leg_ref.shape[1:]
    width = row_count - 1
    cap = recv_ref.shape[2]
    member = pl.program_id(1)
    pair = (first + pl.program_id(0)) * group + member

    @pl.when(member == 0)
    def _():
        start = 0
        for g in range(lat_groups):
            parts = [recv_ref[g * group + h, 0] for h in range(group)]
            for b, part in enumerate(swap_units(parts, 1)):
                gathered[b, pl.ds(start, cap), :] = part.astype(jnp.float32)
            start = start + counts_ref[g]

    @pl.when(pair < pair_dev)
    def _():
        wave = waves_ref[pair]
        coeffs = (gathered[member, :lat_total, :] * weight_ref[...]).astype(jnp.bfloat16)
        main = leg_ref[0, :width, :]
        last = jnp.broadcast_to(leg_ref[0, width:, :], (16, lat_total))
        spectral = jnp.concatenate(
            [
                jnp.dot(main, coeffs, preferred_element_type=jnp.float32),
                jnp.dot(last, coeffs, preferred_element_type=jnp.float32),
            ],
            axis=0,
        )
        shape = spectral.shape
        row = lax.broadcasted_iota(jnp.int32, shape, 0)
        lane = lax.broadcasted_iota(jnp.int32, shape, 1)
        own = row < width - wave
        upper = lane // (2 * group) % 2 != wave % 2
        keep = jnp.logical_and(jnp.logical_xor(own, upper), row < row_count)
        degree = jnp.where(own, row + wave, row - 1)
        ratio = (degree * (degree + 1)).astype(jnp.float32) / float(width * (width - 1))
        spectral = jnp.where(keep, spectral, 0.0)
        if kind != "temperature":
            per_level = jnp.broadcast_to(level_ref[...], (8, level_ref.shape[1]))
            per_lane = exact_dot(per_level, lane_levels(levels, group), ((1,), (1,)))[:1]
        if kind == "vorticity":
            new = spectral / (1.0 + per_lane * ratio * ratio)
        elif kind == "divergence":
            modes_matrix = lane_matrix(modes_ref[...], levels, group)
            modes = exact_dot(spectral, modes_matrix, ((1,), (1,)))
            modes = modes / (1.0 + per_lane * ratio)
            new = exact_dot(modes, modes_matrix)
            div_out[0] = new
        else:
            balance = lane_matrix(balance_ref[...], levels, group)
            new = spectral - exact_dot(div_in[0], balance, ((1,), (1,)))
        zonal = jnp.logical_and(wave == 0, jnp.logical_not(upper))
        new = new * jnp.where(zonal, 1.0, 2.0)
        tail = jnp.concatenate(
            [new[width:], jnp.zeros((LANES - 16, LANES), jnp.float32)], axis=0
        )
        turned = jnp.dot(
            new[:width].T.astype(jnp.bfloat16), main, preferred_element_type=jnp.float32
        )
        turned += jnp.dot(
            tail.T.astype(jnp.bfloat16),
            jnp.broadcast_to(leg_ref[0, width:, :], (LANES, lat_total)),
            preferred_element_type=jnp.float32,
        )
        made[member, :lat_total, :] = turned.T
        made[member, lat_total:, :] = jnp.zeros((cap, LANES), jnp.float32)

    @pl.when(pair >= pair_dev)
    def _():
        made[member] = jnp.zeros(made.shape[1:], jnp.float32)

    @pl.when(member == group - 1)
    def _():
        start = 0
        for g in range(lat_groups):
            parts = [made[b, pl.ds(start, cap), :].astype(jnp.bfloat16) for b in range(group)]
            for h, part in enumerate(swap_units(parts, 1)):
                row = 0
                for out_ref in out_refs:
                    size = out_ref.shape[1]
                    out_ref[g * group + h] = part[row : row + size]
                    row += size
            start = start + counts_ref[g]


def legendre_step(
    kind, first, some, source, received, targets, legendre, weights, counts, waves, levels, extra, group, partial
):
    devices, _, cap, _ = received.shape
    pair_dev, row_count, lat_total = legendre.shape
    lat_groups = devices // group

    def at_pair(i, b, *_):
        return (jnp.minimum((first + i) * group + b, pair_dev - 1), 0, 0)

    def whole(i, b, *_):
        return (0, 0)

    def blocks(size, offset):
        return pl.BlockSpec(
            (devices, size, LANES), lambda i, b, *_: (0, offset // size + first + i, 0)
        )

    square = pl.BlockSpec(extra[0].shape, whole) if extra else None
    div_block = pl.BlockSpec((1, row_count + 15, LANES), at_pair)
    in_specs = [
        pl.BlockSpec((devices, 1, cap, LANES), lambda i, b, *_: (0, source + i, 0, 0)),
        pl.BlockSpec((1, row_count, lat_total), at_pair),
        pl.BlockSpec((lat_total, LANES), whole),
        pl.BlockSpec((1, levels.shape[0]), whole),
    ]
    out_specs = [blocks(size, offset) for size, offset, _ in targets]
    out_shape = [
        jax.ShapeDtypeStruct((devices, total, LANES), jnp.bfloat16) for _, _, total in targets
    ]
    if kind == "divergence":
        in_specs.append(square)
        out_specs.append(div_block)
        out_shape.append(jax.ShapeDtypeStruct((pair_dev, row_count + 15, LANES), jnp.float32))
    elif kind == "temperature":
        in_specs += [square, div_block]
    operands = [counts, waves, received, legendre, weights, levels[None, :], *extra]
    aliases = {}
    if partial is not None:
        aliases = {len(operands): 0}
        in_specs.append(pl.BlockSpec(memory_space=pl.ANY))
        operands.append(partial)
    held = pltpu.VMEM((group, lat_total + cap, LANES), jnp.float32)
    return pl.pallas_call(
        functools.partial(
            legendre_kernel, kind, first, pair_dev, lat_groups, group, len(out_specs)
        ),
        grid_spec=pltpu.PrefetchScalarGridSpec(
            num_scalar_prefetch=2,
            grid=(some, group),
            in_specs=in_specs,
            out_specs=out_specs,
            scratch_shapes=[held, held],
        ),
        out_shape=out_shape,
        input_output_aliases=aliases,
        compiler_params=pltpu.CompilerParams(vmem_limit_bytes=VMEM_LIMIT),
        cost_estimate=pl.CostEstimate(
            flops=8 * some * group * row_count * lat_total * LANES,
            bytes_accessed=2 * some * (group * row_count * lat_total + 2 * devices * cap * LANES),
            transcendentals=0,
        ),
        name="legendre_" + kind,
    )(*operands)


def shards(
    grid,
    legendre,
    gauss_weights,
    band_counts,
    pair_m,
    vert_modes,
    mode_depth,
    diffusion,
    pressure_balance_matrix,
):
    lat_groups = lax.axis_size("lat")
    group = lax.axis_size("lev")
    devices = lat_groups * group
    fields, cap, levels, points = grid.shape
    pair_dev, row_count, _ = legendre.shape
    width = row_count - 1
    unit = 4 * group
    groups = -(-pair_dev // group)
    band = lax.axis_index("lat")
    owner = band * group + lax.axis_index("lev")


    bands = jnp.arange(lat_groups, dtype=jnp.int32)
    count = jnp.sum(jnp.where(bands == band, band_counts, 0))
    weights = jnp.broadcast_to((gauss_weights / points)[:, None], (gauss_weights.shape[0], LANES))
    waves = lax.dynamic_slice(pair_m, (owner * pair_dev,), (pair_dev,))

    rows = grid.reshape(fields, cap * levels, points)

    def exchange(blocks):
        return lax.all_to_all(
            blocks, ("lat", "lev"), split_axis=0, concat_axis=0, tiled=True
        )

    sent = forward_first(rows, pair_m, levels, unit, devices, group, width)
    received = [(0, 1, exchange(sent))]
    later_m, _ = lax.optimization_barrier((pair_m, sent))
    table = trig_table(later_m, width, points, devices, groups, group)
    dft = functools.partial(
        forward, grid=rows, table=table, levels=levels, unit=unit, devices=devices
    )
    if groups > 1:
        sent = dft((0, 1), (1, groups - 1))
        received.append((1, groups - 1, exchange(sent)))
    others = exchange(dft((1, fields - 1), (0, groups)))

    step = functools.partial(
        legendre_step,
        legendre=legendre,
        weights=weights,
        counts=band_counts,
        waves=waves,
        group=group,
    )
    vorticity = None
    for first, some, blocks in received:
        (vorticity,) = step(
            "vorticity",
            first,
            some,
            0,
            blocks,
            targets=[(cap, 0, groups * cap)],
            levels=diffusion,
            extra=(),
            partial=vorticity,
        )
    vorticity = exchange(ordered_after(vorticity, others))
    late = max(16, cap // 3 // 16 * 16)
    if late >= cap or groups * (cap - late) % cap or (cap - late) % late:
        late = 0
    main, offset = cap - late, groups * (cap - late)
    total = offset + groups * cap
    back, new_divergence = step(
        "divergence",
        0,
        groups,
        0,
        others,
        targets=[(cap, offset, total)],
        levels=mode_depth,
        extra=(vert_modes,),
        partial=None,
    )
    targets = [(main, 0, total)] + ([(late, 0, groups * late)] if late else [])
    back, *rest = step(
        "temperature",
        0,
        groups,
        groups,
        others,
        targets=targets,
        levels=diffusion,
        extra=(pressure_balance_matrix, new_divergence),
        partial=back,
    )
    to_grid = functools.partial(
        inverse,
        groups=groups,
        table=table,
        count=count[None],
        shape=(fields, cap * levels, points),
        levels=levels,
        unit=unit,
    )
    out, token = to_grid(0, 0, cap, vorticity, 0, partial=None)
    back = exchange(back)
    if late:
        last = exchange(ordered_after(rest[0], back, token))
    out, _ = to_grid(1, 0, cap, back, offset, partial=out)
    out, _ = to_grid(2, 0, main, back, 0, partial=out)
    if late:
        out, _ = to_grid(2, main, late, last, 0, partial=out)
    return out.reshape(fields, cap, levels, points)


def solution(mesh):
    placed = (
        P(None, "lat", "lev", None),
        P(("lat", "lev"), None, None),
        P(),
        P(),
        P(),
        P(),
        P(),
        P(),
        P(),
    )
    return jax.shard_map(
        shards, mesh=mesh, in_specs=placed, out_specs=P(None, "lat", "lev", None), check_vma=False
    )
```

```python
import functools
import math

import jax
import jax.numpy as jnp
from jax import lax
from jax.experimental import pallas as pl
from jax.experimental.pallas import tpu as pltpu
from jax.sharding import PartitionSpec as P

LANES = 128
VMEM_LIMIT = 63 * 1024 * 1024


def swap_units(parts, unit):
    lane = lax.broadcasted_iota(jnp.int32, parts[0].shape, 1)
    step = 1
    parts = list(parts)
    while step < len(parts):
        shift = unit * step
        high = (lane & shift) != 0
        for i in range(len(parts)):
            if not i & step:
                a, b = parts[i], parts[i | step]
                parts[i] = jnp.where(high, pltpu.roll(b, shift, 1), a)
                parts[i | step] = jnp.where(high, b, pltpu.roll(a, LANES - shift, 1))
        step *= 2
    return parts


def row_tile(rows, most):
    tile = most
    while rows % tile:
        tile -= 16
    return tile


def ordered_after(value, *others):
    anywhere = pl.BlockSpec(memory_space=pl.ANY)
    return pl.pallas_call(
        lambda *refs: None,
        in_specs=[anywhere] * (1 + len(others)),
        out_specs=anywhere,
        out_shape=jax.ShapeDtypeStruct(value.shape, value.dtype),
        input_output_aliases={0: 0},
        name="ordered_after",
    )(value, *others)


def unit_circle(wave, points):
    lane = lax.broadcasted_iota(jnp.int32, wave.shape, 1).astype(jnp.float32)
    product = wave.astype(jnp.float32) * lane
    rest = product - points * jnp.floor(product * (1.0 / points))
    quarter = jnp.floor(rest * (4.0 / points) + 0.5)
    x = (rest - quarter * (points / 4.0)) * (2.0 * math.pi / points)
    y = x * x
    sine = x * (1 + y * (-1 / 6 + y * (1 / 120 + y * (-1 / 5040 + y * (1 / 362880)))))
    cosine = 1 + y * (-1 / 2 + y * (1 / 24 + y * (-1 / 720 + y * (1 / 40320))))
    odd = jnp.logical_or(quarter == 1, quarter == 3)
    cos_low = jnp.logical_or(quarter == 1, quarter == 2)
    sin_low = jnp.logical_or(quarter == 2, quarter == 3)
    cos_all = jnp.where(odd, sine, cosine)
    sin_all = jnp.where(odd, cosine, sine)
    return jnp.where(cos_low, -cos_all, cos_all), jnp.where(sin_low, -sin_all, sin_all)


def wave_rows(pair_ref, pair_dev, group, width, pair_group, device, parity):
    row = lax.broadcasted_iota(jnp.int32, (2 * group, LANES), 0)
    wave = jnp.full((2 * group, LANES), -1, jnp.int32)
    for b in range(group):
        pair = pair_group * group + b
        lower = pair_ref[device * pair_dev + jnp.minimum(pair, pair_dev - 1)]
        chosen = jnp.where(lower % 2 == parity, lower, width - 1 - lower)
        wave = jnp.where(jnp.logical_and(row % group == b, pair < pair_dev), chosen, wave)
    return wave


def fill_table(table, pair_ref, pair_dev, group, width, points, pair_group, first_device):
    unit = 2 * group
    count = 8 * unit

    @pl.loop(0, table.shape[1] // count)
    def _(n):
        at = pl.ds(pl.multiple_of(n * count, count), count)
        for parity in range(2):
            wave = jnp.concatenate(
                [
                    wave_rows(
                        pair_ref,
                        pair_dev,
                        group,
                        width,
                        pair_group,
                        first_device + n // 2 * 16 + n % 2 * 4 + j % 2 * 8 + j // 2,
                        parity,
                    )
                    for j in range(8)
                ],
                axis=0,
            )
            cos, sin = unit_circle(wave, points)
            cos, sin = jnp.where(wave < 0, 0.0, cos), jnp.where(wave < 0, 0.0, sin)
            half = LANES // 2
            cos_half, sin_half = cos[:, half : half + 1], sin[:, half : half + 1]
            cos_turn = jnp.broadcast_to(cos_half * cos_half - sin_half * sin_half, cos.shape)
            sin_turn = jnp.broadcast_to(2.0 * sin_half * cos_half, cos.shape)
            sine = lax.broadcasted_iota(jnp.int32, cos.shape, 0) // group % 2 == 1
            value, other = jnp.where(sine, -sin, cos), jnp.where(sine, cos, sin)
            for a in range(table.shape[2] // LANES):
                table[parity, at, a * LANES : (a + 1) * LANES] = value.astype(table.dtype)
                value, other = (
                    value * cos_turn - other * sin_turn,
                    other * cos_turn + value * sin_turn,
                )


def table_kernel(pair_dev, group, width, points, wide, pair_ref, table):
    fill_table(
        table, pair_ref, pair_dev, group, width, points, pl.program_id(0), pl.program_id(1) * wide
    )


def devices_at_once(devices):
    return 32 if devices % 32 == 0 else 16


def trig_table(pair_m, width, points, devices, groups, group):
    wide = devices_at_once(devices)
    rows = wide * 2 * group
    steps = devices // wide
    return pl.pallas_call(
        functools.partial(table_kernel, pair_m.shape[0] // devices, group, width, points, wide),
        grid_spec=pltpu.PrefetchScalarGridSpec(
            num_scalar_prefetch=1,
            grid=(groups, steps),
            in_specs=[],
            out_specs=pl.BlockSpec((2, rows, points // 2), lambda i, t, m: (0, i * steps + t, 0)),
        ),
        out_shape=jax.ShapeDtypeStruct((2, groups * steps * rows, points // 2), jnp.bfloat16),
        cost_estimate=pl.CostEstimate(
            flops=8 * groups * steps * rows * points,
            bytes_accessed=2 * groups * steps * rows * points,
            transcendentals=0,
        ),
        name="trig_table",
    )(pair_m)


def fold(lines):
    half = lines.shape[1] // 2
    low, high = lines[:, :half], lines[:, half:]
    return low + high, low - high


def emit_blocks(folded, table, scratch, store, tile, levels, unit):
    for parity in range(2):
        values = lax.dot_general(
            folded[parity], table[parity], (((1,), (1,)), ((), ())),
            preferred_element_type=jnp.float32,
        )
        for n in range(values.shape[1] // LANES):
            scratch[parity, n] = values[:, n * LANES : (n + 1) * LANES]
    for n in range(scratch.shape[1]):
        by_level = [
            swap_units(
                [
                    scratch[parity, n, pl.ds(l, tile, stride=levels), :].astype(jnp.bfloat16)
                    for parity in range(2)
                ],
                unit // 2,
            )
            for l in range(levels)
        ]
        for b in range(2):
            for a, part in enumerate(swap_units([x[b] for x in by_level], unit)):
                store(n * 2 * levels + b * levels + a, part)


def forward_kernel(levels, unit, some, grid_ref, table_ref, out_ref, folded, scratch):
    cap = grid_ref.shape[1] // levels
    tile = row_tile(cap, 32)

    @pl.when(jnp.logical_and(pl.program_id(0) % some == 0, pl.program_id(1) == 0))
    def _():
        for s in range(0, cap, tile):
            lines = slice(s * levels, (s + tile) * levels)
            folded[0, lines, :], folded[1, lines, :] = fold(grid_ref[0, lines, :])

    tables = [table_ref[0], table_ref[1]]
    for s in range(0, cap, tile):
        lines = slice(s * levels, (s + tile) * levels)

        def store(d, block, s=s):
            out_ref[d, 0, s : s + tile, :] = block

        emit_blocks(
            [folded[0, lines, :], folded[1, lines, :]],
            tables,
            scratch.at[s // tile],
            store,
            tile,
            levels,
            unit,
        )


def forward(fields, groups, grid, table, levels, unit, devices):
    _, rows, points = grid.shape
    cap = rows // levels
    tile = row_tile(cap, 32)
    wide = devices_at_once(devices)
    steps = devices // wide
    (first_field, some_fields), (first, some) = fields, groups
    count = some_fields * some
    columns = count * devices * unit
    half = wide * unit // 2
    return pl.pallas_call(
        functools.partial(forward_kernel, levels, unit, some),
        grid=(count, steps),
        in_specs=[
            pl.BlockSpec((1, rows, points), lambda i, t: (first_field + i // some, 0, 0)),
            pl.BlockSpec(
                (2, half, points // 2), lambda i, t: (0, (first + i % some) * steps + t, 0)
            ),
        ],
        out_specs=pl.BlockSpec((wide, 1, cap, LANES), lambda i, t: (t, i, 0, 0)),
        out_shape=jax.ShapeDtypeStruct((devices, count, cap, LANES), jnp.bfloat16),
        scratch_shapes=[
            pltpu.VMEM((2, rows, points // 2), jnp.bfloat16),
            pltpu.VMEM((cap // tile, 2, half // LANES, tile * levels, LANES), jnp.float32),
        ],
        compiler_params=pltpu.CompilerParams(vmem_limit_bytes=VMEM_LIMIT),
        cost_estimate=pl.CostEstimate(
            flops=rows * points * columns,
            bytes_accessed=2 * (some_fields * rows * points + rows * columns),
            transcendentals=0,
        ),
        name="forward_dft",
    )(grid, table)


def first_kernel(levels, unit, pair_dev, group, width, pair_ref, grid_ref, out_ref, table, scratch):
    @pl.when(pl.program_id(0) == 0)
    def _():
        fill_table(table, pair_ref, pair_dev, group, width, grid_ref.shape[2], 0, 0)

    tile = grid_ref.shape[1] // levels
    half = scratch.shape[2] * LANES
    folded = fold(grid_ref[0])
    for n in range(table.shape[1] // half):

        def store(d, block, n=n):
            out_ref[n * 2 * half // unit + d, 0] = block

        rows = slice(n * half, (n + 1) * half)
        emit_blocks(
            folded,
            [table[0, rows, :], table[1, rows, :]],
            scratch.at[n],
            store,
            tile,
            levels,
            unit,
        )


def forward_first(grid, pair_m, levels, unit, devices, group, width):
    _, rows, points = grid.shape
    cap = rows // levels
    tile = row_tile(cap, 32)
    columns = devices * unit
    half = devices_at_once(devices) * unit // 2
    return pl.pallas_call(
        functools.partial(first_kernel, levels, unit, pair_m.shape[0] // devices, group, width),
        grid_spec=pltpu.PrefetchScalarGridSpec(
            num_scalar_prefetch=1,
            grid=(cap // tile,),
            in_specs=[pl.BlockSpec((1, tile * levels, points), lambda t, m: (0, t, 0))],
            out_specs=pl.BlockSpec((devices, 1, tile, LANES), lambda t, m: (0, 0, t, 0)),
            scratch_shapes=[
                pltpu.VMEM((2, columns // 2, points // 2), jnp.bfloat16),
                pltpu.VMEM(
                    (columns // 2 // half, 2, half // LANES, tile * levels, LANES), jnp.float32
                ),
            ],
        ),
        out_shape=jax.ShapeDtypeStruct((devices, 1, cap, LANES), jnp.bfloat16),
        compiler_params=pltpu.CompilerParams(vmem_limit_bytes=VMEM_LIMIT),
        cost_estimate=pl.CostEstimate(
            flops=rows * points * columns,
            bytes_accessed=2 * rows * (points + columns),
            transcendentals=0,
        ),
        name="forward_first",
    )(pair_m, grid)


def inverse_kernel(levels, unit, groups, first_row, count_ref, *refs):
    spec_refs, table_ref = refs[:groups], refs[groups]
    out_ref, token_ref, turned = refs[-3:]
    devices, rows, _ = spec_refs[0].shape
    tile = rows if rows <= 48 else row_tile(rows, 32)
    blocks = [(i, d) for i in range(groups) for d in range(0, devices, 2 * levels)]
    base = first_row + pl.program_id(0) * rows
    half = out_ref.shape[2] // 2
    for s in range(0, rows, tile):
        lines = pl.ds(s * levels, tile * levels)
        for n, (i, d) in enumerate(blocks):
            by_level = [
                swap_units(
                    [
                        spec_refs[i][d + b * levels + a, s : s + tile, :]
                        for a in range(levels)
                    ],
                    unit,
                )
                for b in range(2)
            ]
            for l in range(levels):
                parts = swap_units([by_level[0][l], by_level[1][l]], unit // 2)
                for parity in range(2):
                    turned[parity, n, pl.ds(s * levels + l, tile, stride=levels), :] = parts[
                        parity
                    ].astype(jnp.float32)
        row = lax.broadcasted_iota(jnp.int32, (tile * levels, LANES), 0)
        valid = row < (count_ref[0] - base - s) * levels
        even, odd = [
            jnp.dot(
                jnp.concatenate(
                    [
                        jnp.where(valid, turned[parity, n, lines, :], 0.0).astype(jnp.bfloat16)
                        for n in range(len(blocks))
                    ],
                    axis=1,
                ),
                table_ref[parity],
                preferred_element_type=jnp.float32,
            )
            for parity in range(2)
        ]
        out_ref[0, lines, :half] = (even + odd).astype(out_ref.dtype)
        out_ref[0, lines, half:] = (even - odd).astype(out_ref.dtype)
    token_ref[...] = jnp.zeros_like(token_ref)


def inverse(field, first_row, size, spec, offset, groups, table, count, partial, shape, levels, unit):
    devices = spec.shape[0]
    columns, points = 2 * table.shape[1], 2 * table.shape[2]
    tile = 64 if size % 64 == 0 and offset % 64 == 0 else row_tile(size, 48)
    rows = tile * levels

    def part(i):
        return pl.BlockSpec(
            (devices, tile, LANES), lambda t, c: (0, (offset + i * size) // tile + t, 0)
        )

    in_specs = [part(i) for i in range(groups)]
    in_specs.append(pl.BlockSpec(table.shape, lambda t, c: (0, 0, 0)))
    operands = [spec] * groups + [table]
    if partial is not None:
        in_specs.append(pl.BlockSpec(memory_space=pl.ANY))
        operands.append(partial)
    return pl.pallas_call(
        functools.partial(inverse_kernel, levels, unit, groups, first_row),
        grid_spec=pltpu.PrefetchScalarGridSpec(
            num_scalar_prefetch=1,
            grid=(size // tile,),
            in_specs=in_specs,
            out_specs=[
                pl.BlockSpec((1, rows, points), lambda t, c: (field, first_row // tile + t, 0)),
                pl.BlockSpec((8, LANES), lambda t, c: (0, 0)),
            ],
            scratch_shapes=[pltpu.VMEM((2, columns // 2 // LANES, rows, LANES), jnp.float32)],
        ),
        out_shape=[
            jax.ShapeDtypeStruct(shape, jnp.bfloat16),
            jax.ShapeDtypeStruct((8, LANES), jnp.float32),
        ],
        input_output_aliases={} if partial is None else {groups + 2: 0},
        compiler_params=pltpu.CompilerParams(vmem_limit_bytes=VMEM_LIMIT),
        cost_estimate=pl.CostEstimate(
            flops=size * levels * points * columns,
            bytes_accessed=2 * size * levels * (points + columns) + columns * points,
            transcendentals=0,
        ),
        name="inverse_dft",
    )(count, *operands)


def lane_levels(levels, group):
    lane = lax.broadcasted_iota(jnp.int32, (LANES, levels * group), 0)
    level = lax.broadcasted_iota(jnp.int32, (LANES, levels * group), 1)
    held = lane % group * levels + lane // (4 * group)
    return (held == level).astype(jnp.float32)


def exact_dot(a, b, dims=((1,), (0,))):
    return lax.dot_general(
        a, b, (dims, ((), ())), precision=lax.Precision.HIGHEST, preferred_element_type=jnp.float32
    )


def lane_matrix(matrix, levels, group):
    chosen = lane_levels(levels, group)
    spread = exact_dot(exact_dot(chosen, matrix), chosen, ((1,), (1,)))
    row = lax.broadcasted_iota(jnp.int32, spread.shape, 0)
    lane = lax.broadcasted_iota(jnp.int32, spread.shape, 1)
    return jnp.where(row // group % 4 == lane // group % 4, spread, 0.0)


def legendre_kernel(
    kind, first, pair_dev, lat_groups, group, outs, counts_ref, waves_ref, recv_ref, leg_ref, *rest
):
    weight_ref, rest = rest[0], rest[1:]
    gathered, made = rest[-2:]
    rest, out_refs = rest[:-2], rest[-2 - outs : -2]
    level_ref = rest[0]
    if kind == "divergence":
        modes_ref, div_out = rest[1], out_refs[-1]
        out_refs = out_refs[:-1]
    if kind == "temperature":
        balance_ref, div_in = rest[1:3]
    levels = level_ref.shape[1] // group
    row_count, lat_total = leg_ref.shape[1:]
    width = row_count - 1
    cap = recv_ref.shape[2]
    member = pl.program_id(1)
    pair = (first + pl.program_id(0)) * group + member

    @pl.when(member == 0)
    def _():
        start = 0
        for g in range(lat_groups):
            parts = [recv_ref[g * group + h, 0] for h in range(group)]
            for b, part in enumerate(swap_units(parts, 1)):
                gathered[b, pl.ds(start, cap), :] = part.astype(jnp.float32)
            start = start + counts_ref[g]

    @pl.when(pair < pair_dev)
    def _():
        wave = waves_ref[pair]
        coeffs = (gathered[member, :lat_total, :] * weight_ref[...]).astype(jnp.bfloat16)
        main = leg_ref[0, :width, :]
        last = jnp.broadcast_to(leg_ref[0, width:, :], (16, lat_total))
        spectral = jnp.concatenate(
            [
                jnp.dot(main, coeffs, preferred_element_type=jnp.float32),
                jnp.dot(last, coeffs, preferred_element_type=jnp.float32),
            ],
            axis=0,
        )
        shape = spectral.shape
        row = lax.broadcasted_iota(jnp.int32, shape, 0)
        lane = lax.broadcasted_iota(jnp.int32, shape, 1)
        own = row < width - wave
        upper = lane // (2 * group) % 2 != wave % 2
        keep = jnp.logical_and(jnp.logical_xor(own, upper), row < row_count)
        degree = jnp.where(own, row + wave, row - 1)
        ratio = (degree * (degree + 1)).astype(jnp.float32) / float(width * (width - 1))
        spectral = jnp.where(keep, spectral, 0.0)
        if kind != "temperature":
            per_level = jnp.broadcast_to(level_ref[...], (8, level_ref.shape[1]))
            per_lane = exact_dot(per_level, lane_levels(levels, group), ((1,), (1,)))[:1]
        if kind == "vorticity":
            new = spectral / (1.0 + per_lane * ratio * ratio)
        elif kind == "divergence":
            modes_matrix = lane_matrix(modes_ref[...], levels, group)
            modes = exact_dot(spectral, modes_matrix, ((1,), (1,)))
            modes = modes / (1.0 + per_lane * ratio)
            new = exact_dot(modes, modes_matrix)
            div_out[0] = new
        else:
            balance = lane_matrix(balance_ref[...], levels, group)
            new = spectral - exact_dot(div_in[0], balance, ((1,), (1,)))
        zonal = jnp.logical_and(wave == 0, jnp.logical_not(upper))
        new = new * jnp.where(zonal, 1.0, 2.0)
        tail = jnp.concatenate(
            [new[width:], jnp.zeros((LANES - 16, LANES), jnp.float32)], axis=0
        )
        turned = jnp.dot(
            new[:width].T.astype(jnp.bfloat16), main, preferred_element_type=jnp.float32
        )
        turned += jnp.dot(
            tail.T.astype(jnp.bfloat16),
            jnp.broadcast_to(leg_ref[0, width:, :], (LANES, lat_total)),
            preferred_element_type=jnp.float32,
        )
        made[member, :lat_total, :] = turned.T
        made[member, lat_total:, :] = jnp.zeros((cap, LANES), jnp.float32)

    @pl.when(pair >= pair_dev)
    def _():
        made[member] = jnp.zeros(made.shape[1:], jnp.float32)

    @pl.when(member == group - 1)
    def _():
        start = 0
        for g in range(lat_groups):
            parts = [made[b, pl.ds(start, cap), :].astype(jnp.bfloat16) for b in range(group)]
            for h, part in enumerate(swap_units(parts, 1)):
                row = 0
                for out_ref in out_refs:
                    size = out_ref.shape[1]
                    out_ref[g * group + h] = part[row : row + size]
                    row += size
            start = start + counts_ref[g]


def legendre_step(
    kind, first, some, source, received, targets, legendre, weights, counts, waves, levels, extra, group, partial
):
    devices, _, cap, _ = received.shape
    pair_dev, row_count, lat_total = legendre.shape
    lat_groups = devices // group

    def at_pair(i, b, *_):
        return (jnp.minimum((first + i) * group + b, pair_dev - 1), 0, 0)

    def whole(i, b, *_):
        return (0, 0)

    def blocks(size, offset):
        return pl.BlockSpec(
            (devices, size, LANES), lambda i, b, *_: (0, offset // size + first + i, 0)
        )

    square = pl.BlockSpec(extra[0].shape, whole) if extra else None
    div_block = pl.BlockSpec((1, row_count + 15, LANES), at_pair)
    in_specs = [
        pl.BlockSpec((devices, 1, cap, LANES), lambda i, b, *_: (0, source + i, 0, 0)),
        pl.BlockSpec((1, row_count, lat_total), at_pair),
        pl.BlockSpec((lat_total, LANES), whole),
        pl.BlockSpec((1, levels.shape[0]), whole),
    ]
    out_specs = [blocks(size, offset) for size, offset, _ in targets]
    out_shape = [
        jax.ShapeDtypeStruct((devices, total, LANES), jnp.bfloat16) for _, _, total in targets
    ]
    if kind == "divergence":
        in_specs.append(square)
        out_specs.append(div_block)
        out_shape.append(jax.ShapeDtypeStruct((pair_dev, row_count + 15, LANES), jnp.float32))
    elif kind == "temperature":
        in_specs += [square, div_block]
    operands = [counts, waves, received, legendre, weights, levels[None, :], *extra]
    aliases = {}
    if partial is not None:
        aliases = {len(operands): 0}
        in_specs.append(pl.BlockSpec(memory_space=pl.ANY))
        operands.append(partial)
    held = pltpu.VMEM((group, lat_total + cap, LANES), jnp.float32)
    return pl.pallas_call(
        functools.partial(
            legendre_kernel, kind, first, pair_dev, lat_groups, group, len(out_specs)
        ),
        grid_spec=pltpu.PrefetchScalarGridSpec(
            num_scalar_prefetch=2,
            grid=(some, group),
            in_specs=in_specs,
            out_specs=out_specs,
            scratch_shapes=[held, held],
        ),
        out_shape=out_shape,
        input_output_aliases=aliases,
        compiler_params=pltpu.CompilerParams(vmem_limit_bytes=VMEM_LIMIT),
        cost_estimate=pl.CostEstimate(
            flops=8 * some * group * row_count * lat_total * LANES,
            bytes_accessed=2 * some * (group * row_count * lat_total + 2 * devices * cap * LANES),
            transcendentals=0,
        ),
        name="legendre_" + kind,
    )(*operands)


def shards(
    grid,
    legendre,
    gauss_weights,
    band_counts,
    pair_m,
    vert_modes,
    mode_depth,
    diffusion,
    pressure_balance_matrix,
):
    lat_groups = lax.axis_size("lat")
    group = lax.axis_size("lev")
    devices = lat_groups * group
    fields, cap, levels, points = grid.shape
    pair_dev, row_count, _ = legendre.shape
    width = row_count - 1
    unit = 4 * group
    groups = -(-pair_dev // group)
    band = lax.axis_index("lat")
    owner = band * group + lax.axis_index("lev")


    bands = jnp.arange(lat_groups, dtype=jnp.int32)
    count = jnp.sum(jnp.where(bands == band, band_counts, 0))
    weights = jnp.broadcast_to((gauss_weights / points)[:, None], (gauss_weights.shape[0], LANES))
    waves = lax.dynamic_slice(pair_m, (owner * pair_dev,), (pair_dev,))

    rows = grid.reshape(fields, cap * levels, points)

    def exchange(blocks):
        return lax.all_to_all(
            blocks, ("lat", "lev"), split_axis=0, concat_axis=0, tiled=True
        )

    sent = forward_first(rows, pair_m, levels, unit, devices, group, width)
    received = [(0, 1, exchange(sent))]
    later_m, _ = lax.optimization_barrier((pair_m, sent))
    table = trig_table(later_m, width, points, devices, groups, group)
    dft = functools.partial(
        forward, grid=rows, table=table, levels=levels, unit=unit, devices=devices
    )
    if groups > 1:
        sent = dft((0, 1), (1, groups - 1))
        received.append((1, groups - 1, exchange(sent)))
    others = exchange(dft((1, fields - 1), (0, groups)))

    step = functools.partial(
        legendre_step,
        legendre=legendre,
        weights=weights,
        counts=band_counts,
        waves=waves,
        group=group,
    )
    vorticity = None
    for first, some, blocks in received:
        (vorticity,) = step(
            "vorticity",
            first,
            some,
            0,
            blocks,
            targets=[(cap, 0, groups * cap)],
            levels=diffusion,
            extra=(),
            partial=vorticity,
        )
    vorticity = exchange(ordered_after(vorticity, others))
    late = max(16, cap // 4 // 16 * 16)
    if late >= cap or groups * cap % (cap - late) or (cap - late) % late:
        late = 0
    main, offset = cap - late, groups * cap
    total = offset + groups * main
    back, new_divergence = step(
        "divergence",
        0,
        groups,
        0,
        others,
        targets=[(cap, 0, total)],
        levels=mode_depth,
        extra=(vert_modes,),
        partial=None,
    )
    targets = [(main, offset, total)] + ([(late, 0, groups * late)] if late else [])
    back, *rest = step(
        "temperature",
        0,
        groups,
        groups,
        others,
        targets=targets,
        levels=diffusion,
        extra=(pressure_balance_matrix, new_divergence),
        partial=back,
    )
    to_grid = functools.partial(
        inverse,
        groups=groups,
        table=table,
        count=count[None],
        shape=(fields, cap * levels, points),
        levels=levels,
        unit=unit,
    )
    out, token = to_grid(0, 0, cap, vorticity, 0, partial=None)
    back = exchange(back)
    if late:
        last = exchange(ordered_after(rest[0], back, token))
    out, _ = to_grid(1, 0, cap, back, 0, partial=out)
    out, _ = to_grid(2, 0, main, back, offset, partial=out)
    if late:
        out, _ = to_grid(2, main, late, last, 0, partial=out)
    return out.reshape(fields, cap, levels, points)


def solution(mesh):
    placed = (
        P(None, "lat", "lev", None),
        P(("lat", "lev"), None, None),
        P(),
        P(),
        P(),
        P(),
        P(),
        P(),
        P(),
    )
    return jax.shard_map(
        shards, mesh=mesh, in_specs=placed, out_specs=P(None, "lat", "lev", None), check_vma=False
    )
```

```python
import functools
import math

import jax
import jax.numpy as jnp
from jax import lax
from jax.experimental import pallas as pl
from jax.experimental.pallas import tpu as pltpu
from jax.sharding import PartitionSpec as P

LANES = 128
VMEM_LIMIT = 63 * 1024 * 1024


def swap_units(parts, unit):
    lane = lax.broadcasted_iota(jnp.int32, parts[0].shape, 1)
    step = 1
    parts = list(parts)
    while step < len(parts):
        shift = unit * step
        high = (lane & shift) != 0
        for i in range(len(parts)):
            if not i & step:
                a, b = parts[i], parts[i | step]
                parts[i] = jnp.where(high, pltpu.roll(b, shift, 1), a)
                parts[i | step] = jnp.where(high, b, pltpu.roll(a, LANES - shift, 1))
        step *= 2
    return parts


def row_tile(rows, most):
    tile = most
    while rows % tile:
        tile -= 16
    return tile


def ordered_after(value, *others):
    anywhere = pl.BlockSpec(memory_space=pl.ANY)
    return pl.pallas_call(
        lambda *refs: None,
        in_specs=[anywhere] * (1 + len(others)),
        out_specs=anywhere,
        out_shape=jax.ShapeDtypeStruct(value.shape, value.dtype),
        input_output_aliases={0: 0},
        name="ordered_after",
    )(value, *others)


def unit_circle(wave, points):
    lane = lax.broadcasted_iota(jnp.int32, wave.shape, 1).astype(jnp.float32)
    product = wave.astype(jnp.float32) * lane
    rest = product - points * jnp.floor(product * (1.0 / points))
    quarter = jnp.floor(rest * (4.0 / points) + 0.5)
    x = (rest - quarter * (points / 4.0)) * (2.0 * math.pi / points)
    y = x * x
    sine = x * (1 + y * (-1 / 6 + y * (1 / 120 + y * (-1 / 5040 + y * (1 / 362880)))))
    cosine = 1 + y * (-1 / 2 + y * (1 / 24 + y * (-1 / 720 + y * (1 / 40320))))
    odd = jnp.logical_or(quarter == 1, quarter == 3)
    cos_low = jnp.logical_or(quarter == 1, quarter == 2)
    sin_low = jnp.logical_or(quarter == 2, quarter == 3)
    cos_all = jnp.where(odd, sine, cosine)
    sin_all = jnp.where(odd, cosine, sine)
    return jnp.where(cos_low, -cos_all, cos_all), jnp.where(sin_low, -sin_all, sin_all)


def wave_rows(pair_ref, pair_dev, group, width, pair_group, device, parity):
    row = lax.broadcasted_iota(jnp.int32, (2 * group, LANES), 0)
    wave = jnp.full((2 * group, LANES), -1, jnp.int32)
    for b in range(group):
        pair = pair_group * group + b
        lower = pair_ref[device * pair_dev + jnp.minimum(pair, pair_dev - 1)]
        chosen = jnp.where(lower % 2 == parity, lower, width - 1 - lower)
        wave = jnp.where(jnp.logical_and(row % group == b, pair < pair_dev), chosen, wave)
    return wave


def fill_table(table, pair_ref, pair_dev, group, width, points, pair_group, first_device):
    unit = 2 * group
    count = 8 * unit

    @pl.loop(0, table.shape[1] // count)
    def _(n):
        at = pl.ds(pl.multiple_of(n * count, count), count)
        for parity in range(2):
            wave = jnp.concatenate(
                [
                    wave_rows(
                        pair_ref,
                        pair_dev,
                        group,
                        width,
                        pair_group,
                        first_device + n // 2 * 16 + n % 2 * 4 + j % 2 * 8 + j // 2,
                        parity,
                    )
                    for j in range(8)
                ],
                axis=0,
            )
            cos, sin = unit_circle(wave, points)
            cos, sin = jnp.where(wave < 0, 0.0, cos), jnp.where(wave < 0, 0.0, sin)
            half = LANES // 2
            cos_half, sin_half = cos[:, half : half + 1], sin[:, half : half + 1]
            cos_turn = jnp.broadcast_to(cos_half * cos_half - sin_half * sin_half, cos.shape)
            sin_turn = jnp.broadcast_to(2.0 * sin_half * cos_half, cos.shape)
            sine = lax.broadcasted_iota(jnp.int32, cos.shape, 0) // group % 2 == 1
            value, other = jnp.where(sine, -sin, cos), jnp.where(sine, cos, sin)
            for a in range(table.shape[2] // LANES):
                table[parity, at, a * LANES : (a + 1) * LANES] = value.astype(table.dtype)
                value, other = (
                    value * cos_turn - other * sin_turn,
                    other * cos_turn + value * sin_turn,
                )


def table_kernel(pair_dev, group, width, points, wide, pair_ref, table):
    fill_table(
        table, pair_ref, pair_dev, group, width, points, pl.program_id(0), pl.program_id(1) * wide
    )


def devices_at_once(devices):
    return 32 if devices % 32 == 0 else 16


def trig_table(pair_m, width, points, devices, groups, group):
    wide = devices_at_once(devices)
    rows = wide * 2 * group
    steps = devices // wide
    return pl.pallas_call(
        functools.partial(table_kernel, pair_m.shape[0] // devices, group, width, points, wide),
        grid_spec=pltpu.PrefetchScalarGridSpec(
            num_scalar_prefetch=1,
            grid=(groups, steps),
            in_specs=[],
            out_specs=pl.BlockSpec((2, rows, points // 2), lambda i, t, m: (0, i * steps + t, 0)),
        ),
        out_shape=jax.ShapeDtypeStruct((2, groups * steps * rows, points // 2), jnp.bfloat16),
        cost_estimate=pl.CostEstimate(
            flops=8 * groups * steps * rows * points,
            bytes_accessed=2 * groups * steps * rows * points,
            transcendentals=0,
        ),
        name="trig_table",
    )(pair_m)


def fold(lines):
    half = lines.shape[1] // 2
    low, high = lines[:, :half], lines[:, half:]
    return low + high, low - high


def emit_blocks(folded, table, scratch, store, tile, levels, unit):
    for parity in range(2):
        values = lax.dot_general(
            folded[parity], table[parity], (((1,), (1,)), ((), ())),
            preferred_element_type=jnp.float32,
        )
        for n in range(values.shape[1] // LANES):
            scratch[parity, n] = values[:, n * LANES : (n + 1) * LANES]
    for n in range(scratch.shape[1]):
        by_level = [
            swap_units(
                [
                    scratch[parity, n, pl.ds(l, tile, stride=levels), :].astype(jnp.bfloat16)
                    for parity in range(2)
                ],
                unit // 2,
            )
            for l in range(levels)
        ]
        for b in range(2):
            for a, part in enumerate(swap_units([x[b] for x in by_level], unit)):
                store(n * 2 * levels + b * levels + a, part)


def forward_kernel(levels, unit, some, grid_ref, table_ref, out_ref, folded, scratch):
    cap = grid_ref.shape[1] // levels
    tile = row_tile(cap, 32)

    @pl.when(jnp.logical_and(pl.program_id(0) % some == 0, pl.program_id(1) == 0))
    def _():
        for s in range(0, cap, tile):
            lines = slice(s * levels, (s + tile) * levels)
            folded[0, lines, :], folded[1, lines, :] = fold(grid_ref[0, lines, :])

    tables = [table_ref[0], table_ref[1]]
    for s in range(0, cap, tile):
        lines = slice(s * levels, (s + tile) * levels)

        def store(d, block, s=s):
            out_ref[d, 0, s : s + tile, :] = block

        emit_blocks(
            [folded[0, lines, :], folded[1, lines, :]],
            tables,
            scratch.at[s // tile],
            store,
            tile,
            levels,
            unit,
        )


def forward(fields, groups, grid, table, levels, unit, devices):
    _, rows, points = grid.shape
    cap = rows // levels
    tile = row_tile(cap, 32)
    wide = devices_at_once(devices)
    steps = devices // wide
    (first_field, some_fields), (first, some) = fields, groups
    count = some_fields * some
    columns = count * devices * unit
    half = wide * unit // 2
    return pl.pallas_call(
        functools.partial(forward_kernel, levels, unit, some),
        grid=(count, steps),
        in_specs=[
            pl.BlockSpec((1, rows, points), lambda i, t: (first_field + i // some, 0, 0)),
            pl.BlockSpec(
                (2, half, points // 2), lambda i, t: (0, (first + i % some) * steps + t, 0)
            ),
        ],
        out_specs=pl.BlockSpec((wide, 1, cap, LANES), lambda i, t: (t, i, 0, 0)),
        out_shape=jax.ShapeDtypeStruct((devices, count, cap, LANES), jnp.bfloat16),
        scratch_shapes=[
            pltpu.VMEM((2, rows, points // 2), jnp.bfloat16),
            pltpu.VMEM((cap // tile, 2, half // LANES, tile * levels, LANES), jnp.float32),
        ],
        compiler_params=pltpu.CompilerParams(vmem_limit_bytes=VMEM_LIMIT),
        cost_estimate=pl.CostEstimate(
            flops=rows * points * columns,
            bytes_accessed=2 * (some_fields * rows * points + rows * columns),
            transcendentals=0,
        ),
        name="forward_dft",
    )(grid, table)


def first_kernel(levels, unit, pair_dev, group, width, pair_ref, grid_ref, out_ref, table, scratch):
    @pl.when(pl.program_id(0) == 0)
    def _():
        fill_table(table, pair_ref, pair_dev, group, width, grid_ref.shape[2], 0, 0)

    parts, half = scratch.shape[1], scratch.shape[3] * LANES
    tile = grid_ref.shape[1] // levels // parts
    for s in range(parts):
        folded = fold(grid_ref[0, s * tile * levels : (s + 1) * tile * levels, :])
        for n in range(table.shape[1] // half):

            def store(d, block, s=s, n=n):
                out_ref[n * 2 * half // unit + d, 0, s * tile : (s + 1) * tile, :] = block

            rows = slice(n * half, (n + 1) * half)
            emit_blocks(
                folded,
                [table[0, rows, :], table[1, rows, :]],
                scratch.at[n, s],
                store,
                tile,
                levels,
                unit,
            )


def forward_first(grid, pair_m, levels, unit, devices, group, width):
    _, rows, points = grid.shape
    cap = rows // levels
    tile = row_tile(cap, 32)
    parts = 2 if cap % (2 * tile) == 0 else 1
    columns = devices * unit
    half = devices_at_once(devices) * unit // 2
    return pl.pallas_call(
        functools.partial(first_kernel, levels, unit, pair_m.shape[0] // devices, group, width),
        grid_spec=pltpu.PrefetchScalarGridSpec(
            num_scalar_prefetch=1,
            grid=(cap // (parts * tile),),
            in_specs=[pl.BlockSpec((1, parts * tile * levels, points), lambda t, m: (0, t, 0))],
            out_specs=pl.BlockSpec((devices, 1, parts * tile, LANES), lambda t, m: (0, 0, t, 0)),
            scratch_shapes=[
                pltpu.VMEM((2, columns // 2, points // 2), jnp.bfloat16),
                pltpu.VMEM(
                    (columns // 2 // half, parts, 2, half // LANES, tile * levels, LANES),
                    jnp.float32,
                ),
            ],
        ),
        out_shape=jax.ShapeDtypeStruct((devices, 1, cap, LANES), jnp.bfloat16),
        compiler_params=pltpu.CompilerParams(vmem_limit_bytes=VMEM_LIMIT),
        cost_estimate=pl.CostEstimate(
            flops=rows * points * columns,
            bytes_accessed=2 * rows * (points + columns),
            transcendentals=0,
        ),
        name="forward_first",
    )(pair_m, grid)


def inverse_kernel(levels, unit, groups, first_row, count_ref, *refs):
    spec_refs, table_ref = refs[:groups], refs[groups]
    out_ref, token_ref, turned = refs[-3:]
    devices, rows, _ = spec_refs[0].shape
    tile = row_tile(rows, 32)
    blocks = [(i, d) for i in range(groups) for d in range(0, devices, 2 * levels)]
    base = first_row + pl.program_id(0) * rows
    half = out_ref.shape[2] // 2
    for s in range(0, rows, tile):
        lines = pl.ds(s * levels, tile * levels)
        for n, (i, d) in enumerate(blocks):
            by_level = [
                swap_units(
                    [
                        spec_refs[i][d + b * levels + a, s : s + tile, :]
                        for a in range(levels)
                    ],
                    unit,
                )
                for b in range(2)
            ]
            for l in range(levels):
                parts = swap_units([by_level[0][l], by_level[1][l]], unit // 2)
                for parity in range(2):
                    turned[parity, n, pl.ds(s * levels + l, tile, stride=levels), :] = parts[
                        parity
                    ].astype(jnp.float32)
        row = lax.broadcasted_iota(jnp.int32, (tile * levels, LANES), 0)
        valid = row < (count_ref[0] - base - s) * levels
        even, odd = [
            jnp.dot(
                jnp.concatenate(
                    [
                        jnp.where(valid, turned[parity, n, lines, :], 0.0).astype(jnp.bfloat16)
                        for n in range(len(blocks))
                    ],
                    axis=1,
                ),
                table_ref[parity],
                preferred_element_type=jnp.float32,
            )
            for parity in range(2)
        ]
        out_ref[0, lines, :half] = (even + odd).astype(out_ref.dtype)
        out_ref[0, lines, half:] = (even - odd).astype(out_ref.dtype)
    token_ref[...] = jnp.zeros_like(token_ref)


def inverse(field, first_row, size, spec, offset, groups, table, count, partial, shape, levels, unit):
    devices = spec.shape[0]
    columns, points = 2 * table.shape[1], 2 * table.shape[2]
    tile = row_tile(size, 64 if size % 64 == 0 and offset % 64 == 0 else 32)
    if size <= 64:
        tile = row_tile(size, 32)
    rows = tile * levels

    def part(i):
        return pl.BlockSpec(
            (devices, tile, LANES), lambda t, c: (0, (offset + i * size) // tile + t, 0)
        )

    in_specs = [part(i) for i in range(groups)]
    in_specs.append(pl.BlockSpec(table.shape, lambda t, c: (0, 0, 0)))
    operands = [spec] * groups + [table]
    if partial is not None:
        in_specs.append(pl.BlockSpec(memory_space=pl.ANY))
        operands.append(partial)
    return pl.pallas_call(
        functools.partial(inverse_kernel, levels, unit, groups, first_row),
        grid_spec=pltpu.PrefetchScalarGridSpec(
            num_scalar_prefetch=1,
            grid=(size // tile,),
            in_specs=in_specs,
            out_specs=[
                pl.BlockSpec((1, rows, points), lambda t, c: (field, first_row // tile + t, 0)),
                pl.BlockSpec((8, LANES), lambda t, c: (0, 0)),
            ],
            scratch_shapes=[pltpu.VMEM((2, columns // 2 // LANES, rows, LANES), jnp.float32)],
        ),
        out_shape=[
            jax.ShapeDtypeStruct(shape, jnp.bfloat16),
            jax.ShapeDtypeStruct((8, LANES), jnp.float32),
        ],
        input_output_aliases={} if partial is None else {groups + 2: 0},
        compiler_params=pltpu.CompilerParams(vmem_limit_bytes=VMEM_LIMIT),
        cost_estimate=pl.CostEstimate(
            flops=size * levels * points * columns,
            bytes_accessed=2 * size * levels * (points + columns) + columns * points,
            transcendentals=0,
        ),
        name="inverse_dft",
    )(count, *operands)


def lane_levels(levels, group):
    lane = lax.broadcasted_iota(jnp.int32, (LANES, levels * group), 0)
    level = lax.broadcasted_iota(jnp.int32, (LANES, levels * group), 1)
    held = lane % group * levels + lane // (4 * group)
    return (held == level).astype(jnp.float32)


def exact_dot(a, b, dims=((1,), (0,))):
    return lax.dot_general(
        a, b, (dims, ((), ())), precision=lax.Precision.HIGHEST, preferred_element_type=jnp.float32
    )


def lane_matrix(matrix, levels, group):
    chosen = lane_levels(levels, group)
    spread = exact_dot(exact_dot(chosen, matrix), chosen, ((1,), (1,)))
    row = lax.broadcasted_iota(jnp.int32, spread.shape, 0)
    lane = lax.broadcasted_iota(jnp.int32, spread.shape, 1)
    return jnp.where(row // group % 4 == lane // group % 4, spread, 0.0)


def legendre_kernel(
    kind, first, pair_dev, lat_groups, group, outs, counts_ref, waves_ref, recv_ref, leg_ref, *rest
):
    weight_ref, rest = rest[0], rest[1:]
    gathered, made = rest[-2:]
    rest, out_refs = rest[:-2], rest[-2 - outs : -2]
    level_ref = rest[0]
    if kind == "divergence":
        modes_ref, div_out = rest[1], out_refs[-1]
        out_refs = out_refs[:-1]
    if kind == "temperature":
        balance_ref, div_in = rest[1:3]
    levels = level_ref.shape[1] // group
    row_count, lat_total = leg_ref.shape[1:]
    width = row_count - 1
    cap = recv_ref.shape[2]
    member = pl.program_id(1)
    pair = (first + pl.program_id(0)) * group + member

    @pl.when(member == 0)
    def _():
        start = 0
        for g in range(lat_groups):
            parts = [recv_ref[g * group + h, 0] for h in range(group)]
            for b, part in enumerate(swap_units(parts, 1)):
                gathered[b, pl.ds(start, cap), :] = part.astype(jnp.float32)
            start = start + counts_ref[g]

    @pl.when(pair < pair_dev)
    def _():
        wave = waves_ref[pair]
        coeffs = (gathered[member, :lat_total, :] * weight_ref[...]).astype(jnp.bfloat16)
        main = leg_ref[0, :width, :]
        last = jnp.broadcast_to(leg_ref[0, width:, :], (16, lat_total))
        spectral = jnp.concatenate(
            [
                jnp.dot(main, coeffs, preferred_element_type=jnp.float32),
                jnp.dot(last, coeffs, preferred_element_type=jnp.float32),
            ],
            axis=0,
        )
        shape = spectral.shape
        row = lax.broadcasted_iota(jnp.int32, shape, 0)
        lane = lax.broadcasted_iota(jnp.int32, shape, 1)
        own = row < width - wave
        upper = lane // (2 * group) % 2 != wave % 2
        keep = jnp.logical_and(jnp.logical_xor(own, upper), row < row_count)
        degree = jnp.where(own, row + wave, row - 1)
        ratio = (degree * (degree + 1)).astype(jnp.float32) / float(width * (width - 1))
        spectral = jnp.where(keep, spectral, 0.0)
        if kind != "temperature":
            per_level = jnp.broadcast_to(level_ref[...], (8, level_ref.shape[1]))
            per_lane = exact_dot(per_level, lane_levels(levels, group), ((1,), (1,)))[:1]
        if kind == "vorticity":
            new = spectral / (1.0 + per_lane * ratio * ratio)
        elif kind == "divergence":
            modes_matrix = lane_matrix(modes_ref[...], levels, group)
            modes = exact_dot(spectral, modes_matrix, ((1,), (1,)))
            modes = modes / (1.0 + per_lane * ratio)
            new = exact_dot(modes, modes_matrix)
            div_out[0] = new
        else:
            balance = lane_matrix(balance_ref[...], levels, group)
            new = spectral - exact_dot(div_in[0], balance, ((1,), (1,)))
        zonal = jnp.logical_and(wave == 0, jnp.logical_not(upper))
        new = new * jnp.where(zonal, 1.0, 2.0)
        tail = jnp.concatenate(
            [new[width:], jnp.zeros((LANES - 16, LANES), jnp.float32)], axis=0
        )
        turned = jnp.dot(
            new[:width].T.astype(jnp.bfloat16), main, preferred_element_type=jnp.float32
        )
        turned += jnp.dot(
            tail.T.astype(jnp.bfloat16),
            jnp.broadcast_to(leg_ref[0, width:, :], (LANES, lat_total)),
            preferred_element_type=jnp.float32,
        )
        made[member, :lat_total, :] = turned.T
        made[member, lat_total:, :] = jnp.zeros((cap, LANES), jnp.float32)

    @pl.when(pair >= pair_dev)
    def _():
        made[member] = jnp.zeros(made.shape[1:], jnp.float32)

    @pl.when(member == group - 1)
    def _():
        start = 0
        for g in range(lat_groups):
            parts = [made[b, pl.ds(start, cap), :].astype(jnp.bfloat16) for b in range(group)]
            for h, part in enumerate(swap_units(parts, 1)):
                row = 0
                for out_ref in out_refs:
                    size = out_ref.shape[1]
                    out_ref[g * group + h] = part[row : row + size]
                    row += size
            start = start + counts_ref[g]


def legendre_step(
    kind, first, some, source, received, targets, legendre, weights, counts, waves, levels, extra, group, partial
):
    devices, _, cap, _ = received.shape
    pair_dev, row_count, lat_total = legendre.shape
    lat_groups = devices // group

    def at_pair(i, b, *_):
        return (jnp.minimum((first + i) * group + b, pair_dev - 1), 0, 0)

    def whole(i, b, *_):
        return (0, 0)

    def blocks(size, offset):
        return pl.BlockSpec(
            (devices, size, LANES), lambda i, b, *_: (0, offset // size + first + i, 0)
        )

    square = pl.BlockSpec(extra[0].shape, whole) if extra else None
    div_block = pl.BlockSpec((1, row_count + 15, LANES), at_pair)
    in_specs = [
        pl.BlockSpec((devices, 1, cap, LANES), lambda i, b, *_: (0, source + i, 0, 0)),
        pl.BlockSpec((1, row_count, lat_total), at_pair),
        pl.BlockSpec((lat_total, LANES), whole),
        pl.BlockSpec((1, levels.shape[0]), whole),
    ]
    out_specs = [blocks(size, offset) for size, offset, _ in targets]
    out_shape = [
        jax.ShapeDtypeStruct((devices, total, LANES), jnp.bfloat16) for _, _, total in targets
    ]
    if kind == "divergence":
        in_specs.append(square)
        out_specs.append(div_block)
        out_shape.append(jax.ShapeDtypeStruct((pair_dev, row_count + 15, LANES), jnp.float32))
    elif kind == "temperature":
        in_specs += [square, div_block]
    operands = [counts, waves, received, legendre, weights, levels[None, :], *extra]
    aliases = {}
    if partial is not None:
        aliases = {len(operands): 0}
        in_specs.append(pl.BlockSpec(memory_space=pl.ANY))
        operands.append(partial)
    held = pltpu.VMEM((group, lat_total + cap, LANES), jnp.float32)
    return pl.pallas_call(
        functools.partial(
            legendre_kernel, kind, first, pair_dev, lat_groups, group, len(out_specs)
        ),
        grid_spec=pltpu.PrefetchScalarGridSpec(
            num_scalar_prefetch=2,
            grid=(some, group),
            in_specs=in_specs,
            out_specs=out_specs,
            scratch_shapes=[held, held],
        ),
        out_shape=out_shape,
        input_output_aliases=aliases,
        compiler_params=pltpu.CompilerParams(vmem_limit_bytes=VMEM_LIMIT),
        cost_estimate=pl.CostEstimate(
            flops=8 * some * group * row_count * lat_total * LANES,
            bytes_accessed=2 * some * (group * row_count * lat_total + 2 * devices * cap * LANES),
            transcendentals=0,
        ),
        name="legendre_" + kind,
    )(*operands)


def shards(
    grid,
    legendre,
    gauss_weights,
    band_counts,
    pair_m,
    vert_modes,
    mode_depth,
    diffusion,
    pressure_balance_matrix,
):
    lat_groups = lax.axis_size("lat")
    group = lax.axis_size("lev")
    devices = lat_groups * group
    fields, cap, levels, points = grid.shape
    pair_dev, row_count, _ = legendre.shape
    width = row_count - 1
    unit = 4 * group
    groups = -(-pair_dev // group)
    band = lax.axis_index("lat")
    owner = band * group + lax.axis_index("lev")


    bands = jnp.arange(lat_groups, dtype=jnp.int32)
    count = jnp.sum(jnp.where(bands == band, band_counts, 0))
    weights = jnp.broadcast_to((gauss_weights / points)[:, None], (gauss_weights.shape[0], LANES))
    waves = lax.dynamic_slice(pair_m, (owner * pair_dev,), (pair_dev,))

    rows = grid.reshape(fields, cap * levels, points)

    def exchange(blocks):
        return lax.all_to_all(
            blocks, ("lat", "lev"), split_axis=0, concat_axis=0, tiled=True
        )

    sent = forward_first(rows, pair_m, levels, unit, devices, group, width)
    received = [(0, 1, exchange(sent))]
    later_m, _ = lax.optimization_barrier((pair_m, sent))
    table = trig_table(later_m, width, points, devices, groups, group)
    dft = functools.partial(
        forward, grid=rows, table=table, levels=levels, unit=unit, devices=devices
    )
    if groups > 1:
        sent = dft((0, 1), (1, groups - 1))
        received.append((1, groups - 1, exchange(sent)))
    others = exchange(dft((1, fields - 1), (0, groups)))

    step = functools.partial(
        legendre_step,
        legendre=legendre,
        weights=weights,
        counts=band_counts,
        waves=waves,
        group=group,
    )
    vorticity = None
    for first, some, blocks in received:
        (vorticity,) = step(
            "vorticity",
            first,
            some,
            0,
            blocks,
            targets=[(cap, 0, groups * cap)],
            levels=diffusion,
            extra=(),
            partial=vorticity,
        )
    vorticity = exchange(ordered_after(vorticity, others))
    late = max(16, cap // 3 // 16 * 16)
    if late >= cap or groups * (cap - late) % cap or (cap - late) % late:
        late = 0
    main, offset = cap - late, groups * (cap - late)
    total = offset + groups * cap
    back, new_divergence = step(
        "divergence",
        0,
        groups,
        0,
        others,
        targets=[(cap, offset, total)],
        levels=mode_depth,
        extra=(vert_modes,),
        partial=None,
    )
    targets = [(main, 0, total)] + ([(late, 0, groups * late)] if late else [])
    back, *rest = step(
        "temperature",
        0,
        groups,
        groups,
        others,
        targets=targets,
        levels=diffusion,
        extra=(pressure_balance_matrix, new_divergence),
        partial=back,
    )
    to_grid = functools.partial(
        inverse,
        groups=groups,
        table=table,
        count=count[None],
        shape=(fields, cap * levels, points),
        levels=levels,
        unit=unit,
    )
    out, token = to_grid(0, 0, cap, vorticity, 0, partial=None)
    back = exchange(back)
    if late:
        last = exchange(ordered_after(rest[0], back, token))
    out, _ = to_grid(1, 0, cap, back, offset, partial=out)
    out, _ = to_grid(2, 0, main, back, 0, partial=out)
    if late:
        out, _ = to_grid(2, main, late, last, 0, partial=out)
    return out.reshape(fields, cap, levels, points)


def solution(mesh):
    placed = (
        P(None, "lat", "lev", None),
        P(("lat", "lev"), None, None),
        P(),
        P(),
        P(),
        P(),
        P(),
        P(),
        P(),
    )
    return jax.shard_map(
        shards, mesh=mesh, in_specs=placed, out_specs=P(None, "lat", "lev", None), check_vma=False
    )
```
